32 devices in a mesh: dp: 8 (over y, x, core), tensor: 4 (over z).
Axes of the slice: x: 2, y: 2, z: 4, core: 2. Of those that a mesh axis runs over, the one named last changes fastest.
Arguments:
- pixels: bfloat16 [25600, 768], P(('dp', 'tensor')), may hold values from -6 to 6
- crop_sides: int32 [256], P(('dp', 'tensor')), may hold values from 7 to 10, as said below
- out_cotangent: bfloat16 [25600, 768], P(('dp', 'tensor')), may hold values from -6 to 6
- depth_kernel: bfloat16 [49, 768], replicated, may hold values from -0.875 to 0.875
- depth_bias: bfloat16 [768], replicated, may hold values from -1.5 to 1.5
- norm_gain: bfloat16 [768], replicated, may hold values from 0.099609375 to 1.8984375
- norm_shift: bfloat16 [768], replicated, may hold values from -1.5 to 1.5
- expand_weight: bfloat16 [768, 3072], P(None, 'tensor'), may hold values from -0.21875 to 0.21875
- expand_bias: bfloat16 [3072], P('tensor'), may hold values from -1.5 to 1.5
- reduce_weight: bfloat16 [3072, 768], P('tensor'), may hold values from -0.109375 to 0.109375
- reduce_bias: bfloat16 [768], replicated, may hold values from -1.5 to 1.5
- layer_scale: bfloat16 [768], replicated, may hold values from 0.5 to 2
Outputs:
- block_out: bfloat16 [25600, 768], P(('dp', 'tensor'))
- input_grad: float32 [25600, 768], P(('dp', 'tensor'))
- kernel_grad: float32 [49, 768], replicated
- depth_bias_grad: float32 [768], replicated
- gain_grad: float32 [768], replicated
- shift_grad: float32 [768], replicated
- expand_grad: float32 [768, 3072], P(None, 'tensor')
- expand_bias_grad: float32 [3072], P('tensor')
- reduce_grad: float32 [3072, 768], P('tensor')
- reduce_bias_grad: float32 [768], replicated
- scale_grad: float32 [768], replicated
The draws below stay inside these ranges and needn't reach their ends.
Inputs may be any that keep to these rules, and one draw needn't show every extreme that they name: `crop_sides`: each image's crop side is 7, 8 or 10; image 0 has 10 and image 1 has 7.
All inputs are finite; a program needn't handle non-finite values.
Results may differ from the reference program's by a relative error of at most 0.0066.
Values may be sent and summed in bfloat16 or wider, within the bound.
A program may use at most 320 MiB of HBM per device.

```python
import math
import jax
import jax.numpy as jnp
from jax import lax

D = 768
HID = 3072
KERNEL = 7
SIDE = 10
IMAGES = 256
PIX = 25600


def draw_crop_sides(key, part):
    picks = jax.random.randint(key, (IMAGES,), 0, 3)
    sides = jnp.where(picks == 0, 7, jnp.where(picks == 1, 8, 10)).astype(jnp.int32)
    return sides.at[0].set(10).at[1].set(7)


def shard_levels(own_key, dims, pieces, least, largest):
    def one(axis_at, parts):
        steps = jax.random.uniform(jax.random.fold_in(jax.random.fold_in(own_key, 6), axis_at), (parts,), jnp.float32, least / len(pieces), largest / len(pieces))
        return jnp.repeat(jnp.exp(steps), dims[axis_at] // parts).reshape((-1,) + (1,) * (len(dims) - axis_at - 1))

    loudness = one(*pieces[0])
    for cut in pieces[1:]:
        loudness = loudness * one(*cut)
    return loudness


def bell_draw(key, dims, scale, most, shards=(), kind=jnp.bfloat16):
    level = shard_levels(key, dims, shards, -0.22, 0.18) if shards else 1.0
    drawn = jax.random.normal(key, dims, jnp.float32) * scale * level
    return jnp.minimum(jnp.maximum(drawn, -most), most).astype(kind)


def setup_inputs(seed: int = 0) -> dict:
    key_of = jax.random.split(jax.random.key(seed), 13)
    pixels = bell_draw(key_of[0], (PIX, D), 1.0, 6.0, ((0, 32),))
    crop_sides = draw_crop_sides(jax.random.fold_in(key_of[12], 71), 0)
    out_cotangent = bell_draw(key_of[2], (PIX, D), 1.0, 6.0, ((0, 32),))
    depth_kernel = bell_draw(key_of[3], (KERNEL * KERNEL, D), (KERNEL * KERNEL) ** -0.5, 0.875)
    depth_bias = bell_draw(key_of[4], (D,), 0.3, 1.5)
    norm_gain = jnp.clip(1.0 + 0.18 * jax.random.normal(key_of[5], (D,), jnp.float32), 0.099609375, 1.8984375).astype(jnp.bfloat16)
    norm_shift = bell_draw(key_of[6], (D,), 0.3, 1.5)
    expand_weight = bell_draw(key_of[7], (D, HID), D ** -0.5, 0.21875, ((1, 4),))
    expand_bias = bell_draw(key_of[8], (HID,), 0.3, 1.5, ((0, 4),))
    reduce_weight = bell_draw(key_of[9], (HID, D), HID ** -0.5, 0.109375, ((0, 4),))
    reduce_bias = bell_draw(key_of[10], (D,), 0.3, 1.5)
    layer_scale = jnp.clip(jnp.exp(jax.random.uniform(key_of[11], (D,), jnp.float32, math.log(0.5), math.log(2.0))), 0.5, 2.0).astype(jnp.bfloat16)
    return dict(pixels=pixels, crop_sides=crop_sides, out_cotangent=out_cotangent, depth_kernel=depth_kernel, depth_bias=depth_bias, norm_gain=norm_gain, norm_shift=norm_shift, expand_weight=expand_weight, expand_bias=expand_bias, reduce_weight=reduce_weight, reduce_bias=reduce_bias, layer_scale=layer_scale)


@jax.custom_vjp
def low(v):
    return lax.optimization_barrier(v.astype(jnp.bfloat16)).astype(jnp.float32)

@jax.custom_vjp
def low_back(v):
    return v

def low_keep(v):
    return (low(v), None)

def low_pass(kept, grad):
    return (grad,)

def back_keep(v):
    return (v, None)

def back_low(kept, grad):
    return (low(grad),)
low.defvjp(low_keep, low_pass)
low_back.defvjp(back_keep, back_low)
norm_eps = 1e-06
block_images = 32

def pixel_mask(crop_sides):
    places = jnp.arange(SIDE * SIDE, dtype=jnp.int32)
    row_index = places // SIDE
    col_index = places % SIDE
    inside = (row_index[None, :] < crop_sides[:, None]) & (col_index[None, :] < crop_sides[:, None])
    return inside.astype(jnp.float32).reshape(-1, 1)

def front_part(values, keep_mask, kernel, bias, gain, shift):
    width = values.shape[1]
    images = (values * keep_mask).reshape(-1, SIDE, SIDE, width)
    margin = KERNEL // 2
    padded = jnp.pad(images, ((0, 0), (margin, margin), (margin, margin), (0, 0)))
    mixed = jnp.zeros_like(images)
    for offset_row in range(KERNEL):
        for offset_col in range(KERNEL):
            window = padded[:, offset_row:offset_row + SIDE, offset_col:offset_col + SIDE, :]
            mixed = mixed + window * kernel[offset_row * KERNEL + offset_col]
    mixed = (mixed + bias).reshape(values.shape)
    center = lax.optimization_barrier(jnp.mean(mixed, axis=1, keepdims=True))
    deviation = mixed - center
    spread = lax.optimization_barrier(jnp.mean(deviation * deviation, axis=1, keepdims=True))
    return deviation * lax.rsqrt(spread + norm_eps) * gain + shift

def block_forward(values, keep_mask, params):
    kernel, bias, gain, shift, expand_weight, expand_bias, reduce_weight, reduce_bias, layer_scale = params
    normed = low(front_part(values, keep_mask, kernel, bias, gain, shift))
    hidden = low_back(jnp.dot(normed, expand_weight, precision=lax.Precision.HIGHEST) + expand_bias)
    active = low(jax.nn.gelu(hidden, approximate=False))
    branch = low_back(jnp.dot(active, reduce_weight, precision=lax.Precision.HIGHEST) + reduce_bias)
    return keep_mask * (values + layer_scale * branch)

def reference(pixels, crop_sides, out_cotangent, depth_kernel, depth_bias, norm_gain, norm_shift, expand_weight, expand_bias, reduce_weight, reduce_bias, layer_scale):
    keep_mask = pixel_mask(crop_sides)
    width = pixels.shape[1]
    group_rows = block_images * SIDE * SIDE
    blocks = pixels.shape[0] // group_rows
    params = tuple((item.astype(jnp.float32) for item in (depth_kernel, depth_bias, norm_gain, norm_shift, expand_weight, expand_bias, reduce_weight, reduce_bias, layer_scale)))
    values = pixels.astype(jnp.float32).reshape(blocks, group_rows, width)
    masks = keep_mask.reshape(blocks, group_rows, 1)

    def whole(all_values, all_params):

        def one_block(item):
            return block_forward(item[0], item[1], all_params)
        return lax.map(jax.checkpoint(one_block), (all_values, masks))
    output, pullback = jax.vjp(whole, values, params)
    values_grad, params_grad = pullback(out_cotangent.astype(jnp.float32).reshape(blocks, group_rows, width))
    block_out = output.reshape(pixels.shape).astype(jnp.bfloat16)
    input_grad = values_grad.reshape(pixels.shape)
    return (block_out, input_grad, params_grad[0], params_grad[1], params_grad[2], params_grad[3], params_grad[4], params_grad[5], params_grad[6], params_grad[7], params_grad[8])
```

```python
import functools
import math
import jax
import jax.numpy as jnp
from jax import lax
from jax.experimental import pallas as pl
from jax.experimental.pallas import tpu as pltpu
from jax.sharding import PartitionSpec as P

KERNEL = 7
SIDE = 10
PLACES = SIDE * SIDE
TAPS = KERNEL * KERNEL
MARGIN = KERNEL // 2
LANES = 128
BLOCK = 256
norm_eps = 1e-06
f32 = jnp.float32
bf16 = jnp.bfloat16
MESH = pl.DeviceIdType.MESH
ROW_BIAS, ROW_GAIN, ROW_SHIFT, ROW_REDUCE, ROW_SCALE, ROW_EXPAND = 49, 50, 51, 52, 53, 54
SMALL = 64


def gelu_both(h):
    a = jnp.abs(h)
    t = 1.0 / (1.0 + a * (0.3275911 / math.sqrt(2.0)))
    e = jnp.exp(h * h * -0.5)
    poly = t * (
        0.254829592
        + t * (-0.284496736 + t * (1.421413741 + t * (-1.453152027 + t * 1.061405429)))
    )
    q = 0.5 * e * poly
    phi = jnp.where(h >= 0.0, 1.0 - q, q)
    return h * phi, phi + h * (e * (1.0 / math.sqrt(2.0 * math.pi)))


def dot(a, b):
    return jnp.dot(a, b, preferred_element_type=f32)


def dot_t(a, b):
    return lax.dot_general(a, b, (((1,), (1,)), ((), ())), preferred_element_type=f32)


def kernel(
    n_dp,
    n_tensor,
    pix_hbm,
    side_ref,
    cot_hbm,
    taps_ref,
    depth_bias_ref,
    gain_ref,
    shift_ref,
    we_hbm,
    eb_ref,
    wr_hbm,
    rb_ref,
    scale_ref,
    out_hbm,
    in_grad_hbm,
    gr_hbm,
    ge_hbm,
    small_hbm,
    stage,
    X,
    XH,
    RSTD,
    NM,
    CM,
    BC,
    KB,
    NT,
    BT,
    WE,
    WR,
    EB,
    ACT,
    HC,
    EBG,
    NC,
    KG,
    ACC,
    GS,
    R0,
    R1,
    R2,
    RZ,
    RX,
    OUTB,
    S,
    SR,
    SZ,
    SX,
    SALL,
    load_sem,
    out_sem,
    w_send,
    w_recv,
    e_send,
    e_recv,
    g_send,
    g_recv,
    x_send,
    x_recv,
    s_send,
    s_recv,
):
    D = NM.shape[1]
    G = D // LANES
    ROWS = NM.shape[0]
    IMG = ROWS // PLACES
    HALF, QUART, PIECE = D // 2, D // 4, D // 8
    SLOTS = n_tensor
    extra = n_dp.bit_length() - 4
    dp = lax.axis_index("dp")
    tz = lax.axis_index("tensor")
    core = lax.rem(dp, 2)
    xb = lax.rem(lax.div(dp, 2), 2)
    yb = lax.rem(lax.div(dp, 4), 2)
    low = lax.rem(dp, 8)
    bits = (core, xb, yb)

    def flip(b):
        bit = bits[b] if b < 3 else lax.rem(lax.div(dp, 1 << b), 2)
        return dp + (1 - 2 * bit) * (1 << b)

    def flip_low(j):
        d = dp
        for b in range(3):
            if j >> b & 1:
                d = d + (1 - 2 * bits[b]) * (1 << b)
        return d

    OFF = [0, 1, n_tensor - 1] + list(range(2, n_tensor - 1))

    peers = [(flip_low(j), tz) for j in range(1, 8)]
    peers += [(dp, lax.rem(tz + o, n_tensor)) for o in range(1, n_tensor)]
    peers += [(flip(b), tz) for b in range(3, 3 + extra)]
    barrier = pltpu.get_barrier_semaphore()
    for peer in peers:
        pl.semaphore_signal(barrier, inc=1, device_id=peer, device_id_type=MESH)

    loads = [
        pltpu.make_async_copy(pix_hbm, NM, load_sem.at[0]),
        pltpu.make_async_copy(cot_hbm, BC, load_sem.at[1]),
        pltpu.make_async_copy(we_hbm, WE.at[0], load_sem.at[2]),
        pltpu.make_async_copy(wr_hbm, WR.at[0], load_sem.at[3]),
    ]
    for copy in loads:
        copy.start()

    def remote(src, dst, send, recv, device):
        return pltpu.make_async_remote_copy(
            src_ref=src, dst_ref=dst, send_sem=send, recv_sem=recv,
            device_id=device, device_id_type=MESH,
        )

    W = (WE, WR)
    first = (xb, yb)
    second = (yb, xb)
    first_peer = (flip(1), flip(2))
    second_peer = (flip(2), flip(1))

    def w_rows(m, level):
        start = core * HALF
        if level <= 2:
            start = start + second[m] * QUART
        if level <= 1:
            start = start + first[m] * PIECE
        size = (PIECE, PIECE, QUART, HALF)[level]
        return pl.ds(pl.multiple_of(start, 16), size)

    def w_copy(s, m, level):
        rows = w_rows(m, level)
        here = W[m].at[s, rows, :]
        src = here
        if level == 0:
            src = (we_hbm, wr_hbm)[m].at[rows, :]
            device = (dp, lax.rem(tz + n_tensor - OFF[s], n_tensor))
        elif level == 1:
            device = (first_peer[m], tz)
        elif level == 2:
            device = (second_peer[m], tz)
        else:
            device = (flip(0), tz)
        return remote(src, here, w_send.at[s - 1, m, level], w_recv.at[s - 1, m, level], device)

    def e_copy(s):
        device = (dp, lax.rem(tz + n_tensor - OFF[s], n_tensor))
        return remote(EB.at[0], EB.at[s], e_send.at[s - 1], e_recv.at[s - 1], device)

    def w_step(s, level):
        for m in range(2):
            if level > 0:
                w_copy(s, m, level - 1).wait_recv()
            if level < 4:
                w_copy(s, m, level).start()
        if level == 4:
            e_copy(s).wait_recv()

    EB[0] = jnp.broadcast_to(eb_ref[...].astype(f32), (8, D))
    pl.semaphore_wait(barrier, len(peers))
    for s in range(1, SLOTS):
        w_step(s, 0)
        e_copy(s).start()

    g_first = (yb, xb)
    g_second = (xb, yb)
    g_first_peer = (flip(2), flip(1))
    g_second_peer = (flip(1), flip(2))

    def g_start(m, level):
        start = core * HALF
        if level >= 1:
            start = start + g_first[m] * QUART
        if level >= 2:
            start = start + g_second[m] * PIECE
        return start

    def g_copy(s, m, level):
        if level == 0:
            start, size, peer, dst = (1 - core) * HALF, HALF, flip(0), R0
        elif level == 1:
            start = g_start(m, 0) + (1 - g_first[m]) * QUART
            size, peer, dst = QUART, g_first_peer[m], R1
        else:
            start = g_start(m, 1) + (1 - g_second[m]) * PIECE
            size, peer, dst = PIECE, g_second_peer[m], R2
        src = GS.at[s, m, pl.ds(pl.multiple_of(start, 16), size), :]
        return remote(
            src, dst.at[s, m], g_send.at[s, m, level], g_recv.at[s, m, level], (peer, tz)
        )

    def z_copy(s, m):
        src = GS.at[s, m, pl.ds(pl.multiple_of(g_start(m, 2), 16), PIECE), :]
        device = (dp, lax.rem(tz + OFF[s], n_tensor))
        return remote(src, RZ.at[s - 1, m], g_send.at[s, m, 3], g_recv.at[s, m, 3], device)

    def g_step(s, level):
        for m in range(2):
            if level > 0:
                g_copy(s, m, level - 1).wait_recv()
                got = (R0, R1, R2)[level - 1]
                start = g_start(m, level - 1)
                size = (HALF, QUART, PIECE)[level - 1]

                def add(i, c):
                    rows = pl.ds(pl.multiple_of(start + i * 16, 16), 16)
                    GS[s, m, rows, :] = (
                        GS[s, m, rows, :] + got[s, m, pl.ds(pl.multiple_of(i * 16, 16), 16), :]
                    )
                    return c

                lax.fori_loop(0, size // 16, add, 0)
            if level < 3:
                g_copy(s, m, level).start()
            elif s > 0:
                z_copy(s, m).start()

    def a_copy(m, level):
        if level == 0:
            start, size, peer = g_start(m, 2), PIECE, g_second_peer[m]
        elif level == 1:
            start, size, peer = g_start(m, 1), QUART, g_first_peer[m]
        else:
            start, size, peer = g_start(m, 0), HALF, flip(0)
        here = OUTB.at[m, pl.ds(pl.multiple_of(start, 16), size), :]
        return remote(here, here, g_send.at[0, m, 3 + level], g_recv.at[0, m, 3 + level], (peer, tz))

    def x_copy(m, b):
        here = OUTB.at[m, pl.ds(pl.multiple_of(g_start(m, 2), 16), PIECE), :]
        return remote(here, RX.at[b - 3, m], x_send.at[b - 3, m], x_recv.at[b - 3, m], (flip(b), tz))

    def finish_sum():
        for m in range(2):
            for s in range(1, SLOTS):
                z_copy(s, m).wait_recv()
            start = g_start(m, 2)

            def add(i, c):
                rows = pl.ds(pl.multiple_of(start + i * 16, 16), 16)
                own = pl.ds(pl.multiple_of(i * 16, 16), 16)
                total = GS[0, m, rows, :].astype(f32)
                for s in range(1, SLOTS):
                    total = total + RZ[s - 1, m, own, :].astype(f32)
                OUTB[m, rows, :] = total.astype(bf16)
                return c

            lax.fori_loop(0, PIECE // 16, add, 0)
            for b in range(3, 3 + extra):
                x_copy(m, b).start()
                x_copy(m, b).wait()

                def add_x(i, c):
                    rows = pl.ds(pl.multiple_of(start + i * 16, 16), 16)
                    OUTB[m, rows, :] = (
                        OUTB[m, rows, :] + RX[b - 3, m, pl.ds(pl.multiple_of(i * 16, 16), 16), :]
                    )
                    return c

                lax.fori_loop(0, PIECE // 16, add_x, 0)
            a_copy(m, 0).start()

    def a_step(level):
        for m in range(2):
            a_copy(m, level - 1).wait_recv()
            if level < 3:
                a_copy(m, level).start()

    def sr_copy(j):
        dst_low = flip_low(j)
        rows = pl.ds(pl.multiple_of(lax.rem(dst_low, 8) * 8, 8), 8)
        return remote(S.at[rows, :], SR.at[j - 1], s_send.at[0, j], s_recv.at[0, j], (dst_low, tz))

    def sz_copy(o):
        return remote(
            SZ.at[tz], SZ.at[tz], s_send.at[1, o], s_recv.at[1, o],
            (dp, lax.rem(tz + o, n_tensor)),
        )

    own_small = pl.ds(pl.multiple_of(low * 8, 8), 8)

    def sa_copy(j):
        here = SALL.at[own_small, :]
        return remote(here, here, s_send.at[2, j], s_recv.at[2, j], (flip_low(j), tz))

    def sx_copy(b):
        return remote(
            SALL.at[own_small, :], SX.at[b - 3], s_send.at[3, b], s_recv.at[3, b], (flip(b), tz)
        )

    def small_step(level):
        if level == 0:
            for j in range(1, 8):
                sr_copy(j).start()
        elif level == 1:
            total = S[own_small, :]
            for j in range(1, 8):
                sr_copy(j).wait_recv()
                total = total + SR[j - 1]
            SZ[tz] = total
            for o in range(1, n_tensor):
                sz_copy(o).start()
        elif level == 2:
            for o in range(1, n_tensor):
                sz_copy(o).wait_recv()
            total = SZ[0]
            for o in range(1, n_tensor):
                total = total + SZ[o]
            SALL[own_small, :] = total
            for b in range(3, 3 + extra):
                sx_copy(b).start()
                sx_copy(b).wait()
                SALL[own_small, :] = SALL[own_small, :] + SX[b - 3]
            for j in range(1, 8):
                sa_copy(j).start()
        else:
            for j in range(1, 8):
                sa_copy(j).wait_recv()

    row = lax.broadcasted_iota(jnp.int32, (IMG, LANES), 0)
    sides = jnp.zeros((IMG, LANES), jnp.int32)
    for i in range(IMG):
        sides = jnp.where(row == i, side_ref[i], sides)

    def mask_at(p):
        if isinstance(p, int):
            return jnp.where(sides > max(p // SIDE, p % SIDE), 1.0, 0.0)
        return jnp.where(sides > jnp.maximum(lax.div(p, SIDE), lax.rem(p, SIDE)), 1.0, 0.0)

    def lanes(g):
        return slice(g * LANES, (g + 1) * LANES)

    def place(p):
        return pl.ds(p * IMG, IMG)

    def spread(src):
        def body(i, c):
            rows = pl.ds(pl.multiple_of(i * 80, 16), 80)
            for g in range(G):
                stage[g, rows, :] = src[rows, lanes(g)].astype(f32)
            return c

        lax.fori_loop(0, ROWS // 80, body, 0)

    def load_pixels():
        def body(p, c):
            m = mask_at(p)
            rows = pl.ds(pl.multiple_of(p * IMG, IMG), IMG)
            for g in range(G):
                X[g, rows, :] = stage[g, pl.ds(p, IMG, stride=PLACES), :] * m
            return c

        lax.fori_loop(0, PLACES, body, 0, unroll=2)

    def load_cot():
        scale = scale_ref[...].astype(f32)

        def body(q, sums):
            sums = list(sums)
            masks = [mask_at(2 * q + u) for u in range(2)]
            rows = pl.ds(pl.multiple_of(q * 2 * IMG, 2 * IMG), 2 * IMG)
            for g in range(G):
                c = [stage[g, pl.ds(2 * q + u, IMG, stride=PLACES), :] * masks[u] for u in range(2)]
                c = jnp.concatenate(c, axis=0)
                CM[rows, lanes(g)] = c.astype(bf16)
                b = (c * scale[:, lanes(g)]).astype(bf16)
                BC[rows, lanes(g)] = b
                b = b.astype(f32)
                sums[g] = sums[g] + (b[:IMG] + b[IMG:])
            return tuple(sums)

        zero = jnp.zeros((IMG, LANES), f32)
        sums = lax.fori_loop(0, PLACES // 2, body, (zero,) * G)
        for g in range(G):
            ACC[3, g] = sums[g]

    def load_taps():
        for g in range(G):
            for t in range(TAPS):
                KB[g, place(t), :] = jnp.broadcast_to(
                    taps_ref[t : t + 1, lanes(g)].astype(f32), (IMG, LANES)
                )

    def conv(src, dst, bias, flipped, post, between):
        def one(g, carry):
            for r in range(SIDE):
                acc = [None] * SIDE if bias is None else [bias[g]] * SIDE
                for rr in range(max(0, r - MARGIN), min(SIDE, r + MARGIN + 1)):
                    xs = [src[g, place(rr * SIDE + c), :] for c in range(SIDE)]
                    for dc in range(KERNEL):
                        t = (rr - r + MARGIN) * KERNEL + dc
                        k = KB[g, place(TAPS - 1 - t if flipped else t), :]
                        for c in range(SIDE):
                            cc = c + dc - MARGIN
                            if 0 <= cc < SIDE:
                                v = xs[cc] * k
                                acc[c] = v if acc[c] is None else acc[c] + v
                if post is None:
                    for c in range(SIDE):
                        dst[g, place(r * SIDE + c), :] = acc[c]
                else:
                    post(g, r, acc)
            between(g)
            return carry

        lax.fori_loop(0, G, one, 0)

    def layernorm():
        gain = gain_ref[...].astype(f32)
        shift = shift_ref[...].astype(f32)

        def body(q, c):
            rows = pl.ds(pl.multiple_of(q * 16, 16), 16)
            v = [XH[g, rows, :] for g in range(G)]
            total = functools.reduce(jnp.add, v)
            mean = jnp.sum(total, axis=1, keepdims=True) * (1.0 / D)
            v = [a - mean for a in v]
            total = functools.reduce(jnp.add, [a * a for a in v])
            rstd = lax.rsqrt(jnp.sum(total, axis=1, keepdims=True) * (1.0 / D) + norm_eps)
            RSTD[rows, :] = jnp.broadcast_to(rstd, (16, LANES))
            for g in range(G):
                xh = v[g] * rstd
                XH[g, rows, :] = xh
                NM[rows, lanes(g)] = (xh * gain[:, lanes(g)] + shift[:, lanes(g)]).astype(bf16)
            return c

        lax.fori_loop(0, ROWS // 16, body, 0, unroll=2)

    def layernorm_back():
        gain = gain_ref[...].astype(f32)

        def body(q, sums):
            gains, shifts, biases = [list(part) for part in sums]
            rows = pl.ds(pl.multiple_of(q * 16, 16), 16)
            rstd = RSTD[rows, :]
            xh = [XH[g, rows, :] for g in range(G)]
            nc = [NC[g, rows, :] for g in range(G)]
            d = [nc[g] * gain[:, lanes(g)] for g in range(G)]
            s1 = functools.reduce(jnp.add, d)
            s2 = functools.reduce(jnp.add, [d[g] * xh[g] for g in range(G)])
            m1 = jnp.sum(s1, axis=1, keepdims=True) * (1.0 / D)
            m2 = jnp.sum(s2, axis=1, keepdims=True) * (1.0 / D)
            for g in range(G):
                dm = rstd * (d[g] - m1 - xh[g] * m2)
                NC[g, rows, :] = dm
                gx = nc[g] * xh[g]
                gains[g] = gains[g] + (gx[:8] + gx[8:])
                shifts[g] = shifts[g] + (nc[g][:8] + nc[g][8:])
                biases[g] = biases[g] + (dm[:8] + dm[8:])
            return tuple(gains), tuple(shifts), tuple(biases)

        zeros = (jnp.zeros((8, LANES), f32),) * G
        sums = lax.fori_loop(0, ROWS // 16, body, (zeros, zeros, zeros))
        for i in range(3):
            for g in range(G):
                ACC[i, g] = sums[i][g]

    def kernel_grad():
        def one(g, carry):
            for dr in range(KERNEL):
                acc = [[None, None] for _ in range(KERNEL)]
                for r in range(SIDE):
                    rr = r + dr - MARGIN
                    if not 0 <= rr < SIDE:
                        continue
                    ds = [NC[g, place(r * SIDE + c), :] for c in range(SIDE)]
                    xs = [X[g, place(rr * SIDE + c), :] for c in range(SIDE)]
                    for dc in range(KERNEL):
                        a = acc[dc]
                        for c in range(SIDE):
                            cc = c + dc - MARGIN
                            if 0 <= cc < SIDE:
                                v = ds[c] * xs[cc]
                                a[c % 2] = v if a[c % 2] is None else a[c % 2] + v
                for dc in range(KERNEL):
                    KG[g, place(dr * KERNEL + dc), :] = acc[dc][0] + acc[dc][1]
            return carry

        lax.fori_loop(0, G, one, 0)

    def hidden_block(s, j):
        cols = slice(j * BLOCK, (j + 1) * BLOCK)
        h = dot(NM[...], WE[s, :, cols])
        stage[0] = h[:, :LANES]
        stage[1] = h[:, LANES:]
        a = dot_t(BC[...], WR[s, cols, :])
        stage[2] = a[:, :LANES]
        stage[3] = a[:, LANES:]

        def body(i, sums):
            rows = pl.ds(pl.multiple_of(i * 16, 16), 16)
            out = []
            for u in range(2):
                mine = slice(j * BLOCK + u * LANES, j * BLOCK + (u + 1) * LANES)
                value, slope = gelu_both(stage[u, rows, :] + EB[s, 0:1, mine])
                ACT[s, rows, mine] = value.astype(bf16)
                w = (stage[2 + u, rows, :] * slope).astype(bf16)
                HC[s, rows, mine] = w
                w = w.astype(f32)
                out.append(sums[u] + (w[:8] + w[8:]))
            return tuple(out)

        zero = jnp.zeros((8, LANES), f32)
        sums = lax.fori_loop(0, ROWS // 16, body, (zero, zero), unroll=5)
        for u in range(2):
            EBG[s, :, j * BLOCK + u * LANES : j * BLOCK + (u + 1) * LANES] = sums[u]

    def grad_block(s, j):
        cols = slice(j * BLOCK, (j + 1) * BLOCK)
        GS[s, 0, :, cols] = dot(BT[...], ACT[s, :, cols]).astype(bf16)
        GS[s, 1, :, cols] = dot(NT[...], HC[s, :, cols]).astype(bf16)

    def back_to_normed():
        for n in range(D // BLOCK):
            cols = slice(n * BLOCK, (n + 1) * BLOCK)
            total = dot_t(HC[0], WE[0, cols, :])
            for s in range(1, SLOTS):
                total = total + dot_t(HC[s], WE[s, cols, :])
            NC[2 * n] = total[:, :LANES]
            NC[2 * n + 1] = total[:, LANES:]

    def to_branch():
        for n in range(D // BLOCK):
            cols = slice(n * BLOCK, (n + 1) * BLOCK)
            total = dot(ACT[0], WR[0, :, cols])
            for s in range(1, SLOTS):
                total = total + dot(ACT[s], WR[s, :, cols])
            XH[2 * n] = total[:, :LANES]
            XH[2 * n + 1] = total[:, LANES:]

    def block_output():
        scale = scale_ref[...].astype(f32)
        shift = rb_ref[...].astype(f32)

        def body(q, sums):
            sums = list(sums)
            rows = pl.ds(pl.multiple_of(q * 2 * IMG, 2 * IMG), 2 * IMG)
            masks = jnp.concatenate([mask_at(2 * q + u) for u in range(2)], axis=0)
            for g in range(G):
                branch = XH[g, rows, :] + shift[:, lanes(g)]
                v = CM[rows, lanes(g)].astype(f32) * branch
                sums[g] = sums[g] + (v[:IMG] + v[IMG:])
                value = X[g, rows, :] + masks * (scale[:, lanes(g)] * branch)
                for u in range(2):
                    stage[g, pl.ds(2 * q + u, IMG, stride=PLACES), :] = value[u * IMG : (u + 1) * IMG]
            return tuple(sums)

        zero = jnp.zeros((IMG, LANES), f32)
        sums = lax.fori_loop(0, PLACES // 2, body, (zero,) * G)
        for g in range(G):
            ACC[4, g] = sums[g]

        def narrow(i, c):
            rows = pl.ds(pl.multiple_of(i * 80, 16), 80)
            for g in range(G):
                NM[rows, lanes(g)] = stage[g, rows, :].astype(bf16)
            return c

        lax.fori_loop(0, ROWS // 80, narrow, 0)

    def small_sums():
        S[...] = jnp.zeros_like(S)
        for g in range(G):
            for t in range(TAPS):
                S[t : t + 1, lanes(g)] = jnp.sum(KG[g, place(t), :], axis=0, keepdims=True)
            for r, i in ((ROW_BIAS, 2), (ROW_GAIN, 0), (ROW_SHIFT, 1), (ROW_REDUCE, 3), (ROW_SCALE, 4)):
                S[r : r + 1, lanes(g)] = jnp.sum(ACC[i, g], axis=0, keepdims=True)
        for s in range(SLOTS):
            r = ROW_EXPAND + lax.rem(tz + OFF[s], n_tensor)
            S[pl.ds(r, 1), :] = jnp.sum(EBG[s], axis=0, keepdims=True)

    loads[0].wait()
    spread(NM)
    load_pixels()
    load_taps()
    w_plan = [[(1, 1)], [(2, 1), (1, 2)], [(1, 3)], [(2, 2)], [(3, 1)], [(2, 3), (1, 4)]]

    def during_conv(g):
        for i in range(G):
            @pl.when(g == i)
            def _():
                for s, level in w_plan[i] if i < len(w_plan) else []:
                    w_step(s, level)

    biases = depth_bias_ref[...].astype(f32)
    for g in range(G):
        ACC[0, g] = jnp.broadcast_to(biases[:, lanes(g)], (8, LANES))
    conv(X, XH, ACC.at[0], False, None, during_conv)
    loads[1].wait()
    spread(BC)
    load_cot()
    layernorm()
    w_step(3, 2)
    NT[...] = NM[...].T
    BT[...] = BC[...].T
    loads[2].wait()
    loads[3].wait()
    for s in range(SLOTS):
        if s == 2:
            w_step(2, 4)
        if s == 3:
            w_step(3, 4)
        for j in range(D // BLOCK):
            hidden_block(s, j)
            if s == 0 and j == 0:
                w_step(3, 3)
            if s > 0 and j == 0:
                g_step(s - 1, 1)
            if s > 1 and j == 1:
                g_step(s - 2, 3)
        for j in range(D // BLOCK):
            grad_block(s, j)
        g_step(s, 0)
        if s > 0:
            g_step(s - 1, 2)
    last = SLOTS - 1
    back_to_normed()
    g_step(last, 1)
    g_step(last - 1, 3)
    layernorm_back()
    g_step(last, 2)
    kernel_grad()
    g_step(last, 3)
    to_branch()
    finish_sum()
    block_output()
    pltpu.make_async_copy(NM, out_hbm, out_sem.at[0]).start()
    small_sums()
    small_step(0)
    a_step(1)
    small_step(1)

    def finish_input(g, r, acc):
        cols = pl.ds(pl.multiple_of(g * LANES, LANES), LANES)
        for c in range(0, SIDE, 2):
            p = r * SIDE + c
            cot = CM[pl.ds(p * IMG, 2 * IMG), cols].astype(f32)
            for u in range(2):
                XH[g, pl.ds(p + u, IMG, stride=PLACES), :] = (
                    acc[c + u] * mask_at(p + u) + cot[u * IMG : (u + 1) * IMG]
                )

    def out_copy(g):
        return pltpu.make_async_copy(
            XH.at[g], in_grad_hbm.at[:, pl.ds(pl.multiple_of(g * LANES, LANES), LANES)], out_sem.at[1 + g]
        )

    def during_back(g):
        out_copy(g).start()

        @pl.when(g == 1)
        def _():
            a_step(2)
            small_step(2)

        @pl.when(g == 4)
        def _():
            a_step(3)

    conv(NC, None, None, True, finish_input, during_back)
    small_step(3)
    tail = [
        pltpu.make_async_copy(OUTB.at[0], gr_hbm, load_sem.at[0]),
        pltpu.make_async_copy(OUTB.at[1], ge_hbm, load_sem.at[1]),
        pltpu.make_async_copy(SALL, small_hbm, load_sem.at[2]),
    ]
    for copy in tail:
        copy.start()
    for s in range(1, SLOTS):
        e_copy(s).wait_send()
        for m in range(2):
            for level in range(4):
                w_copy(s, m, level).wait_send()
            z_copy(s, m).wait_send()
    for s in range(SLOTS):
        for m in range(2):
            for level in range(3):
                g_copy(s, m, level).wait_send()
    for m in range(2):
        for level in range(3):
            a_copy(m, level).wait_send()
    for j in range(1, 8):
        sr_copy(j).wait_send()
        sa_copy(j).wait_send()
    for o in range(1, n_tensor):
        sz_copy(o).wait_send()
    pltpu.make_async_copy(NM, out_hbm, out_sem.at[0]).wait()
    for g in range(G):
        out_copy(g).wait()
    for copy in tail:
        copy.wait()


def per_device(
    n_dp,
    n_tensor,
    pixels,
    crop_sides,
    out_cotangent,
    depth_kernel,
    depth_bias,
    norm_gain,
    norm_shift,
    expand_weight,
    expand_bias,
    reduce_weight,
    reduce_bias,
    layer_scale,
):
    rows, D = pixels.shape
    G = D // LANES
    img = rows // PLACES
    slots = n_tensor
    extra = max(n_dp.bit_length() - 4, 1)
    vmem = pl.BlockSpec(memory_space=pltpu.VMEM)
    hbm = pl.BlockSpec(memory_space=pl.ANY)
    smem = pl.BlockSpec(memory_space=pltpu.SMEM)
    V = pltpu.VMEM
    DMA = pltpu.SemaphoreType.DMA
    scratch = [
        V((G, rows, LANES), f32),
        V((G, rows, LANES), f32),
        V((G, rows, LANES), f32),
        V((rows, LANES), f32),
        V((rows, D), bf16),
        V((rows, D), bf16),
        V((rows, D), bf16),
        V((G, TAPS * img, LANES), f32),
        V((D, rows), bf16),
        V((D, rows), bf16),
        V((slots, D, D), bf16),
        V((slots, D, D), bf16),
        V((slots, 8, D), f32),
        V((slots, rows, D), bf16),
        V((slots, rows, D), bf16),
        V((slots, 8, D), f32),
        V((G, rows, LANES), f32),
        V((G, TAPS * img, LANES), f32),
        V((5, G, 8, LANES), f32),
        V((slots, 2, D, D), bf16),
        V((slots, 2, D // 2, D), bf16),
        V((slots, 2, D // 4, D), bf16),
        V((slots, 2, D // 8, D), bf16),
        V((slots - 1, 2, D // 8, D), bf16),
        V((extra, 2, D // 8 if n_dp > 8 else 16, D), bf16),
        V((2, D, D), bf16),
        V((SMALL, D), f32),
        V((7, 8, D), f32),
        V((slots, 8, D), f32),
        V((extra, 8, D), f32),
        V((SMALL, D), f32),
        DMA((4,)),
        DMA((1 + G,)),
        DMA((slots - 1, 2, 4)),
        DMA((slots - 1, 2, 4)),
        DMA((slots - 1,)),
        DMA((slots - 1,)),
        DMA((slots, 2, 6)),
        DMA((slots, 2, 6)),
        DMA((extra, 2)),
        DMA((extra, 2)),
        DMA((4, 8)),
        DMA((4, 8)),
    ]
    block_out, input_grad, gr, ge, small = pl.pallas_call(
        functools.partial(kernel, n_dp, n_tensor),
        out_shape=[
            jax.ShapeDtypeStruct((rows, D), bf16),
            jax.ShapeDtypeStruct((rows, D), f32),
            jax.ShapeDtypeStruct((D, D), bf16),
            jax.ShapeDtypeStruct((D, D), bf16),
            jax.ShapeDtypeStruct((SMALL, D), f32),
        ],
        in_specs=[hbm, smem, hbm, vmem, vmem, vmem, vmem, hbm, vmem, hbm, vmem, vmem],
        out_specs=[hbm] * 5,
        scratch_shapes=scratch,
        compiler_params=pltpu.CompilerParams(
            collective_id=0, has_side_effects=True, vmem_limit_bytes=61 << 20
        ),
        cost_estimate=pl.CostEstimate(
            flops=12 * rows * D * D * slots, bytes_accessed=20 * rows * D, transcendentals=0
        ),
    )(
        pixels,
        crop_sides,
        out_cotangent,
        depth_kernel,
        depth_bias.reshape(1, D),
        norm_gain.reshape(1, D),
        norm_shift.reshape(1, D),
        expand_weight,
        expand_bias.reshape(1, D),
        reduce_weight,
        reduce_bias.reshape(1, D),
        layer_scale.reshape(1, D),
    )
    expand_bias_grad = lax.dynamic_slice(
        small, (ROW_EXPAND + lax.axis_index("tensor"), 0), (1, D)
    ).reshape(D)
    return (
        block_out,
        input_grad,
        small[:TAPS],
        small[ROW_BIAS],
        small[ROW_GAIN],
        small[ROW_SHIFT],
        ge.astype(f32),
        expand_bias_grad,
        gr.T.astype(f32),
        small[ROW_REDUCE],
        small[ROW_SCALE],
    )


def solution(mesh):
    in_specs = (
        P(("dp", "tensor"), None),
        P(("dp", "tensor")),
        P(("dp", "tensor"), None),
        P(),
        P(),
        P(),
        P(),
        P(None, "tensor"),
        P("tensor"),
        P("tensor", None),
        P(),
        P(),
    )
    out_specs = (
        P(("dp", "tensor"), None),
        P(("dp", "tensor"), None),
        P(),
        P(),
        P(),
        P(),
        P(None, "tensor"),
        P("tensor"),
        P("tensor", None),
        P(),
        P(),
    )
    return jax.shard_map(
        functools.partial(per_device, mesh.shape["dp"], mesh.shape["tensor"]),
        mesh=mesh,
        in_specs=in_specs,
        out_specs=out_specs,
        check_vma=False,
    )
```

```python
import functools
import math
import jax
import jax.numpy as jnp
from jax import lax
from jax.experimental import pallas as pl
from jax.experimental.pallas import tpu as pltpu
from jax.sharding import PartitionSpec as P

KERNEL = 7
SIDE = 10
PLACES = SIDE * SIDE
TAPS = KERNEL * KERNEL
MARGIN = KERNEL // 2
LANES = 128
BLOCK = 256
norm_eps = 1e-06
f32 = jnp.float32
bf16 = jnp.bfloat16
MESH = pl.DeviceIdType.MESH
ROW_BIAS, ROW_GAIN, ROW_SHIFT, ROW_REDUCE, ROW_SCALE, ROW_EXPAND = 49, 50, 51, 52, 53, 54
SMALL = 64
PLAN = (
    "W0.0.0", "taps", "pix", "W0.0.1", "conv:0", "W1.2.0", "W1.1.1", "W1.1.0", "conv:1", "W1.2.1",
    "conv:2", "conv:3", "W2.1.1", "conv:4", "W2.1.0", "conv:5", "W1.3.1", "cot", "ln:0", "ln:1",
    "ln:2", "W1.3.0", "ln:3", "h:0:0", "h:0:1", "W2.2.1", "W3.1.0", "W3.1.1", "W2.2.0", "h:0:2",
    "h:0:3", "h:1:0", "gr:0:0", "W2.3.1", "gr:0:1", "W2.3.0", "h:1:1", "h:1:2", "gr:0:2", "h:1:3",
    "W3.2.1", "gr:1:0", "W3.2.0", "gr:1:1", "gr:1:2", "G0.1.0", "G0.1.1", "h:2:0", "h:2:1",
    "G1.1.0", "h:2:2", "h:2:3", "W3.3.1", "G1.1.1", "W3.3.0", "gr:2:0", "gr:2:1", "gr:2:2",
    "G0.2.0", "G0.2.1", "h:3:0", "h:3:1", "h:3:2", "G1.2.1", "G1.2.0", "h:3:3", "ncot", "G0.0.0",
    "G2.1.1", "G2.1.0", "lnb:0", "gr:3:0", "G2.2.0", "gr:3:1", "G2.2.1", "gr:3:2", "G0.3.0",
    "G0.3.1", "lnb:1", "G0.0.1", "G1.3.0", "G1.3.1", "kg:0", "G3.2.0", "kg:1", "kg:2", "G1.0.0",
    "G3.2.1", "kg:3", "G3.1.1", "G3.1.0", "kg:4", "kg:5", "G2.3.0", "branch", "G1.0.1", "G2.3.1",
    "bout", "G3.3.0", "small", "G2.0.0", "convb:0", "S0", "G3.3.1", "G2.0.1", "S1", "convb:1",
    "A0.0", "S2", "A0.1", "S3", "A1.0", "A1.1", "convb:2", "convb:3", "convb:4", "convb:5", "A2.0",
    "A2.1",
)


def gelu_both(h):
    phi = 0.5 + 0.5 * lax.erf(h * math.sqrt(0.5))
    bell = jnp.exp2(h * h * (-0.5 * math.log2(math.e)))
    return h * phi, phi + h * (1.0 / math.sqrt(2.0 * math.pi)) * bell


def dot(a, b):
    return jnp.dot(a, b, preferred_element_type=f32)


def dot_rows(a, b):
    return lax.dot_general(a, b, (((0,), (0,)), ((), ())), preferred_element_type=f32)


def dot_t(a, b):
    return lax.dot_general(a, b, (((1,), (1,)), ((), ())), preferred_element_type=f32)


def kernel(
    n_dp,
    n_tensor,
    pix_hbm,
    side_ref,
    cot_hbm,
    taps_ref,
    depth_bias_ref,
    gain_ref,
    shift_ref,
    we_hbm,
    eb_ref,
    wr_hbm,
    rb_ref,
    scale_ref,
    out_hbm,
    in_grad_hbm,
    gr_hbm,
    ge_hbm,
    small_hbm,
    stage,
    X,
    XH,
    RSTD,
    NM,
    CM,
    BC,
    KB,
    WE,
    WR,
    EB,
    ACT,
    HC,
    EBG,
    NC,
    KG,
    ACC,
    GS,
    R0,
    R1,
    R2,
    RZ,
    RX,
    OUTB,
    S,
    SR,
    SZ,
    SX,
    SALL,
    load_sem,
    out_sem,
    w_send,
    w_recv,
    e_send,
    e_recv,
    g_send,
    g_recv,
    x_send,
    x_recv,
    s_send,
    s_recv,
):
    D = NM.shape[1]
    G = D // LANES
    ROWS = NM.shape[0]
    IMG = ROWS // PLACES
    HALF, QUART, PIECE = D // 2, D // 4, D // 8
    SLOTS = n_tensor
    extra = n_dp.bit_length() - 4
    dp = lax.axis_index("dp")
    tz = lax.axis_index("tensor")
    core = lax.rem(dp, 2)
    xb = lax.rem(lax.div(dp, 2), 2)
    yb = lax.rem(lax.div(dp, 4), 2)
    low = lax.rem(dp, 8)
    bits = (core, xb, yb)

    def flip(b):
        bit = bits[b] if b < 3 else lax.rem(lax.div(dp, 1 << b), 2)
        return dp + (1 - 2 * bit) * (1 << b)

    def flip_low(j):
        d = dp
        for b in range(3):
            if j >> b & 1:
                d = d + (1 - 2 * bits[b]) * (1 << b)
        return d


    t_low = lax.rem(tz, 2)
    t_high = lax.div(tz, 2)
    partner = tz + 1 - 2 * t_low
    middle = t_low + t_high - 2 * t_low * t_high
    across = 3 - tz

    def shard_of(s):
        return (tz, partner, 2 - t_high, 3 - 3 * t_high)[s]

    peers = [(flip_low(j), tz) for j in range(1, 8)]
    peers += [(dp, lax.rem(tz + o, n_tensor)) for o in range(1, n_tensor)]
    peers += [(flip(b), tz) for b in range(3, 3 + extra)]
    barrier = pltpu.get_barrier_semaphore()
    for peer in peers:
        pl.semaphore_signal(barrier, inc=1, device_id=peer, device_id_type=MESH)

    loads = [
        pltpu.make_async_copy(pix_hbm, NM, load_sem.at[0]),
        pltpu.make_async_copy(cot_hbm, BC, load_sem.at[1]),
        pltpu.make_async_copy(we_hbm, WE.at[0], load_sem.at[2]),
        pltpu.make_async_copy(wr_hbm, WR.at[0], load_sem.at[3]),
    ]
    for copy in loads:
        copy.start()

    def vector(ref):
        return ref[...].astype(f32).reshape(1, D)

    def remote(src, dst, send, recv, device):
        return pltpu.make_async_remote_copy(
            src_ref=src, dst_ref=dst, send_sem=send, recv_sem=recv,
            device_id=device, device_id_type=MESH,
        )

    W = (WE, WR)
    first = (xb, yb)
    second = (yb, xb)
    first_peer = (flip(1), flip(2))
    second_peer = (flip(2), flip(1))

    def w_rows(m, level):
        start = core * HALF
        if level <= 2:
            start = start + second[m] * QUART
        if level <= 1:
            start = start + first[m] * PIECE
        size = (PIECE, PIECE, QUART, HALF)[level]
        return pl.ds(pl.multiple_of(start, 16), size)

    def w_copy(s, m, level):
        here = W[m].at[s, w_rows(m, level), :]
        device = ((first_peer[m], tz), (second_peer[m], tz), (flip(0), tz))[level - 1]
        return remote(here, here, w_send.at[s, m, level], w_recv.at[s, m, level], device)

    def z_piece(m, source, slot, device):
        rows = w_rows(m, 0)
        src = (we_hbm, wr_hbm)[m].at[rows, :] if source == 0 else W[m].at[source, rows, :]
        send = w_send.at[0, m, slot] if source == 0 else w_send.at[source, m, 0]
        return remote(src, W[m].at[slot, rows, :], send, w_recv.at[slot, m, 0], (dp, device))

    def own_pieces(m):
        return z_piece(m, 0, 1, partner), z_piece(m, 0, 2, across)

    def relay(s, m):
        return z_piece(m, 1, 3, across) if s == 1 else z_piece(m, s, s, partner)

    def in_middle(act):
        @pl.when(middle == 1)
        def _():
            act()

    def e_copy(o):
        own = EB.at[tz]
        return remote(own, own, e_send.at[o], e_recv.at[tz], (dp, lax.rem(tz + o, n_tensor)))

    def e_arrival(s):
        there = EB.at[shard_of(s)]
        return remote(there, there, e_send.at[s], e_recv.at[shard_of(s)], (dp, partner))

    def w_step(level, s, m):
        if level == 0:
            to_partner, to_other = own_pieces(m)
            to_partner.start()
            in_middle(to_other.start)
            return
        if level == 1:
            z_piece(m, 0, s, partner).wait_recv()
            in_middle(relay(s, m).start)
        else:
            w_copy(s, m, level - 1).wait_recv()
        if level < 4:
            w_copy(s, m, level).start()

    EB[tz] = jnp.broadcast_to(vector(eb_ref), (8, D))
    pl.semaphore_wait(barrier, len(peers))
    for o in range(1, n_tensor):
        e_copy(o).start()

    g_first = (yb, xb)
    g_second = (xb, yb)
    g_first_peer = (flip(2), flip(1))
    g_second_peer = (flip(1), flip(2))

    def g_start(m, level):
        start = core * HALF
        if level >= 1:
            start = start + g_first[m] * QUART
        if level >= 2:
            start = start + g_second[m] * PIECE
        return start

    def g_copy(s, m, level):
        if level == 0:
            start, size, peer, dst = (1 - core) * HALF, HALF, flip(0), R0
        elif level == 1:
            start = g_start(m, 0) + (1 - g_first[m]) * QUART
            size, peer, dst = QUART, g_first_peer[m], R1
        else:
            start = g_start(m, 1) + (1 - g_second[m]) * PIECE
            size, peer, dst = PIECE, g_second_peer[m], R2
        src = GS.at[s, m, pl.ds(pl.multiple_of(start, 16), size), :]
        return remote(
            src, dst.at[s, m], g_send.at[s, m, level], g_recv.at[s, m, level], (peer, tz)
        )

    def z_copy(s, m):
        src = GS.at[s, m, pl.ds(pl.multiple_of(g_start(m, 2), 16), PIECE), :]
        slot = 1 if s == 1 else 3 - middle
        return remote(
            src, RZ.at[slot - 1, m], g_send.at[s, m, 3], g_recv.at[slot, m, 3], (dp, shard_of(s))
        )

    def z_arrival(s, m):
        src = GS.at[s, m, pl.ds(pl.multiple_of(g_start(m, 2), 16), PIECE), :]
        return remote(src, RZ.at[s - 1, m], g_send.at[s, m, 3], g_recv.at[s, m, 3], (dp, partner))

    def g_step(level, s, m):
        if level > 0:
            g_copy(s, m, level - 1).wait_recv()
            got = (R0, R1, R2)[level - 1]
            start = g_start(m, level - 1)
            size = (HALF, QUART, PIECE)[level - 1]

            def add(i, c):
                rows = pl.ds(pl.multiple_of(start + i * 16, 16), 16)
                GS[s, m, rows, :] = (
                    GS[s, m, rows, :] + got[s, m, pl.ds(pl.multiple_of(i * 16, 16), 16), :]
                )
                return c

            lax.fori_loop(0, size // 16, add, 0, unroll=2)
        if level < 3:
            g_copy(s, m, level).start()
        elif s > 0:
            z_copy(s, m).start()

    def a_copy(m, level):
        if level == 0:
            start, size, peer = g_start(m, 2), PIECE, g_second_peer[m]
        elif level == 1:
            start, size, peer = g_start(m, 1), QUART, g_first_peer[m]
        else:
            start, size, peer = g_start(m, 0), HALF, flip(0)
        here = OUTB.at[m, pl.ds(pl.multiple_of(start, 16), size), :]
        return remote(here, here, g_send.at[0, m, 3 + level], g_recv.at[0, m, 3 + level], (peer, tz))

    def x_copy(m, b):
        here = OUTB.at[m, pl.ds(pl.multiple_of(g_start(m, 2), 16), PIECE), :]
        return remote(here, RX.at[b - 3, m], x_send.at[b - 3, m], x_recv.at[b - 3, m], (flip(b), tz))

    def finish_sum(m):
        g_step(3, 0, m)
        for s in range(1, SLOTS):
            z_arrival(s, m).wait_recv()
        start = g_start(m, 2)

        def add(i, c):
            rows = pl.ds(pl.multiple_of(start + i * 16, 16), 16)
            own = pl.ds(pl.multiple_of(i * 16, 16), 16)
            total = GS[0, m, rows, :].astype(f32)
            for s in range(1, SLOTS):
                total = total + RZ[s - 1, m, own, :].astype(f32)
            OUTB[m, rows, :] = total.astype(bf16)
            return c

        lax.fori_loop(0, PIECE // 16, add, 0)
        for b in range(3, 3 + extra):
            x_copy(m, b).start()
            x_copy(m, b).wait()

            def add_x(i, c):
                rows = pl.ds(pl.multiple_of(start + i * 16, 16), 16)
                OUTB[m, rows, :] = (
                    OUTB[m, rows, :] + RX[b - 3, m, pl.ds(pl.multiple_of(i * 16, 16), 16), :]
                )
                return c

            lax.fori_loop(0, PIECE // 16, add_x, 0)

    def a_step(level, m):
        if level == 0:
            finish_sum(m)
        else:
            a_copy(m, level - 1).wait_recv()
        if level < 3:
            a_copy(m, level).start()

    def sr_copy(j):
        dst_low = flip_low(j)
        rows = pl.ds(pl.multiple_of(lax.rem(dst_low, 8) * 8, 8), 8)
        return remote(S.at[rows, :], SR.at[j - 1], s_send.at[0, j], s_recv.at[0, j], (dst_low, tz))

    def sz_copy(o):
        return remote(
            SZ.at[tz], SZ.at[tz], s_send.at[1, o], s_recv.at[1, o],
            (dp, lax.rem(tz + o, n_tensor)),
        )

    own_small = pl.ds(pl.multiple_of(low * 8, 8), 8)

    def sa_copy(j):
        here = SALL.at[own_small, :]
        return remote(here, here, s_send.at[2, j], s_recv.at[2, j], (flip_low(j), tz))

    def sx_copy(b):
        return remote(
            SALL.at[own_small, :], SX.at[b - 3], s_send.at[3, b], s_recv.at[3, b], (flip(b), tz)
        )

    def small_step(level):
        if level == 0:
            for j in range(1, 8):
                sr_copy(j).start()
        elif level == 1:
            total = S[own_small, :]
            for j in range(1, 8):
                sr_copy(j).wait_recv()
                total = total + SR[j - 1]
            SZ[tz] = total
            for o in range(1, n_tensor):
                sz_copy(o).start()
        elif level == 2:
            for o in range(1, n_tensor):
                sz_copy(o).wait_recv()
            total = SZ[0]
            for o in range(1, n_tensor):
                total = total + SZ[o]
            SALL[own_small, :] = total
            for b in range(3, 3 + extra):
                sx_copy(b).start()
                sx_copy(b).wait()
                SALL[own_small, :] = SALL[own_small, :] + SX[b - 3]
            for j in range(1, 8):
                sa_copy(j).start()
        else:
            for j in range(1, 8):
                sa_copy(j).wait_recv()

    row = lax.broadcasted_iota(jnp.int32, (IMG, LANES), 0)
    sides = jnp.zeros((IMG, LANES), jnp.int32)
    for i in range(IMG):
        sides = jnp.where(row == i, side_ref[i], sides)

    def mask_at(p):
        if isinstance(p, int):
            return jnp.where(sides > max(p // SIDE, p % SIDE), 1.0, 0.0)
        return jnp.where(sides > jnp.maximum(lax.div(p, SIDE), lax.rem(p, SIDE)), 1.0, 0.0)

    def lanes(g):
        return slice(g * LANES, (g + 1) * LANES)

    def place(p):
        return pl.ds(p * IMG, IMG)

    def spread(src):
        def body(i, c):
            rows = pl.ds(pl.multiple_of(i * 80, 16), 80)
            for g in range(G):
                stage[g, rows, :] = src[rows, lanes(g)].astype(f32)
            return c

        lax.fori_loop(0, ROWS // 80, body, 0)

    def load_pixels():
        def body(p, c):
            m = mask_at(p)
            rows = pl.ds(pl.multiple_of(p * IMG, IMG), IMG)
            for g in range(G):
                X[g, rows, :] = stage[g, pl.ds(p, IMG, stride=PLACES), :] * m
            return c

        lax.fori_loop(0, PLACES, body, 0, unroll=2)

    def load_cot():
        scale = vector(scale_ref)

        def body(q, sums):
            sums = list(sums)
            masks = [mask_at(2 * q + u) for u in range(2)]
            rows = pl.ds(pl.multiple_of(q * 2 * IMG, 2 * IMG), 2 * IMG)
            for g in range(G):
                c = [stage[g, pl.ds(2 * q + u, IMG, stride=PLACES), :] * masks[u] for u in range(2)]
                c = jnp.concatenate(c, axis=0)
                CM[rows, lanes(g)] = c.astype(bf16)
                b = (c * scale[:, lanes(g)]).astype(bf16)
                BC[rows, lanes(g)] = b
                b = b.astype(f32)
                sums[g] = sums[g] + (b[:IMG] + b[IMG:])
            return tuple(sums)

        zero = jnp.zeros((IMG, LANES), f32)
        sums = lax.fori_loop(0, PLACES // 2, body, (zero,) * G)
        for g in range(G):
            ACC[3, g] = sums[g]

    def load_taps():
        for g in range(G):
            for t in range(TAPS):
                KB[g, place(t), :] = jnp.broadcast_to(
                    taps_ref[t : t + 1, lanes(g)].astype(f32), (IMG, LANES)
                )

    def conv(src, dst, bias, flipped, post, between):
        def one(g, carry):
            for r in range(SIDE):
                acc = [None] * SIDE if bias is None else [bias[g]] * SIDE
                for rr in range(max(0, r - MARGIN), min(SIDE, r + MARGIN + 1)):
                    xs = [src[g, place(rr * SIDE + c), :] for c in range(SIDE)]
                    for dc in range(KERNEL):
                        t = (rr - r + MARGIN) * KERNEL + dc
                        k = KB[g, place(TAPS - 1 - t if flipped else t), :]
                        for c in range(SIDE):
                            cc = c + dc - MARGIN
                            if 0 <= cc < SIDE:
                                v = xs[cc] * k
                                acc[c] = v if acc[c] is None else acc[c] + v
                if post is None:
                    for c in range(SIDE):
                        dst[g, place(r * SIDE + c), :] = acc[c]
                else:
                    post(g, r, acc)
            between(g)
            return carry

        lax.fori_loop(0, G, one, 0)

    def layernorm(lo, hi):
        gain = vector(gain_ref)
        shift = vector(shift_ref)

        def body(q, c):
            rows = pl.ds(pl.multiple_of(q * 16, 16), 16)
            v = [XH[g, rows, :] for g in range(G)]
            total = functools.reduce(jnp.add, v)
            mean = jnp.sum(total, axis=1, keepdims=True) * (1.0 / D)
            v = [a - mean for a in v]
            total = functools.reduce(jnp.add, [a * a for a in v])
            rstd = lax.rsqrt(jnp.sum(total, axis=1, keepdims=True) * (1.0 / D) + norm_eps)
            RSTD[rows, :] = jnp.broadcast_to(rstd, (16, LANES))
            for g in range(G):
                xh = v[g] * rstd
                XH[g, rows, :] = xh
                NM[rows, lanes(g)] = (xh * gain[:, lanes(g)] + shift[:, lanes(g)]).astype(bf16)
            return c

        lax.fori_loop(lo, hi, body, 0, unroll=5)

    def layernorm_back(lo, hi):
        gain = vector(gain_ref)

        def body(q, sums):
            gains, shifts, biases = [list(part) for part in sums]
            rows = pl.ds(pl.multiple_of(q * 16, 16), 16)
            rstd = RSTD[rows, :]
            xh = [XH[g, rows, :] for g in range(G)]
            nc = [NC[g, rows, :] for g in range(G)]
            d = [nc[g] * gain[:, lanes(g)] for g in range(G)]
            s1 = functools.reduce(jnp.add, d)
            s2 = functools.reduce(jnp.add, [d[g] * xh[g] for g in range(G)])
            m1 = jnp.sum(s1, axis=1, keepdims=True) * (1.0 / D)
            m2 = jnp.sum(s2, axis=1, keepdims=True) * (1.0 / D)
            for g in range(G):
                dm = rstd * (d[g] - m1 - xh[g] * m2)
                NC[g, rows, :] = dm
                gx = nc[g] * xh[g]
                gains[g] = gains[g] + (gx[:8] + gx[8:])
                shifts[g] = shifts[g] + (nc[g][:8] + nc[g][8:])
                biases[g] = biases[g] + (dm[:8] + dm[8:])
            return tuple(gains), tuple(shifts), tuple(biases)

        zeros = (jnp.zeros((8, LANES), f32),) * G
        sums = lax.fori_loop(lo, hi, body, (zeros, zeros, zeros), unroll=5)
        for i in range(3):
            for g in range(G):
                ACC[i, g] = sums[i][g] if lo == 0 else ACC[i, g] + sums[i][g]

    def kernel_grad(between):
        def one(g, carry):
            for dr in range(KERNEL):
                acc = [[None, None] for _ in range(KERNEL)]
                for r in range(SIDE):
                    rr = r + dr - MARGIN
                    if not 0 <= rr < SIDE:
                        continue
                    ds = [NC[g, place(r * SIDE + c), :] for c in range(SIDE)]
                    xs = [X[g, place(rr * SIDE + c), :] for c in range(SIDE)]
                    for dc in range(KERNEL):
                        a = acc[dc]
                        for c in range(SIDE):
                            cc = c + dc - MARGIN
                            if 0 <= cc < SIDE:
                                v = ds[c] * xs[cc]
                                a[c % 2] = v if a[c % 2] is None else a[c % 2] + v
                for dc in range(KERNEL):
                    t = dr * KERNEL + dc
                    KG[g, t : t + 1, :] = jnp.sum(acc[dc][0] + acc[dc][1], axis=0, keepdims=True)
            between(g)
            return carry

        lax.fori_loop(0, G, one, 0)

    def hidden_block(s, j):
        if j < D // BLOCK:
            cols = slice(j * BLOCK, (j + 1) * BLOCK)
            base = j % 2 * 4
            h = dot(NM[...], WE[s, :, cols])
            stage[base] = h[:, :LANES]
            stage[base + 1] = h[:, LANES:]
            a = dot_t(BC[...], WR[s, cols, :])
            stage[base + 2] = a[:, :LANES]
            stage[base + 3] = a[:, LANES:]
        if j > 0:
            base = (j - 1) % 2 * 4
            for u in range(2):
                mine = slice((j - 1) * BLOCK + u * LANES, (j - 1) * BLOCK + (u + 1) * LANES)
                bias = EB[shard_of(s), :, mine]
                bias = jnp.concatenate([bias, bias], axis=0)
                total = None
                for i in range(ROWS // 16):
                    rows = slice(i * 16, (i + 1) * 16)
                    value, slope = gelu_both(stage[base + u, rows, :] + bias)
                    ACT[s, rows, mine] = value.astype(bf16)
                    w = (stage[base + 2 + u, rows, :] * slope).astype(bf16)
                    HC[s, rows, mine] = w
                    w = w.astype(f32)
                    w = w[:8] + w[8:]
                    total = w if total is None else total + w
                EBG[s, :, mine] = total

    def grad_block(s, j):
        cols = slice(j * BLOCK, (j + 1) * BLOCK)
        GS[s, 0, cols, :] = dot_rows(ACT[s, :, cols], BC[...]).astype(bf16)
        GS[s, 1, :, cols] = dot_rows(NM[...], HC[s, :, cols]).astype(bf16)

    def back_to_normed():
        for n in range(D // BLOCK):
            cols = slice(n * BLOCK, (n + 1) * BLOCK)
            total = dot_t(HC[0], WE[0, cols, :])
            for s in range(1, SLOTS):
                total = total + dot_t(HC[s], WE[s, cols, :])
            NC[2 * n] = total[:, :LANES]
            NC[2 * n + 1] = total[:, LANES:]

    def to_branch():
        for n in range(D // BLOCK):
            cols = slice(n * BLOCK, (n + 1) * BLOCK)
            total = dot(ACT[0], WR[0, :, cols])
            for s in range(1, SLOTS):
                total = total + dot(ACT[s], WR[s, :, cols])
            XH[2 * n] = total[:, :LANES]
            XH[2 * n + 1] = total[:, LANES:]

    def block_output():
        scale = vector(scale_ref)
        shift = vector(rb_ref)

        def body(q, sums):
            sums = list(sums)
            rows = pl.ds(pl.multiple_of(q * 2 * IMG, 2 * IMG), 2 * IMG)
            masks = jnp.concatenate([mask_at(2 * q + u) for u in range(2)], axis=0)
            for g in range(G):
                branch = XH[g, rows, :] + shift[:, lanes(g)]
                v = CM[rows, lanes(g)].astype(f32) * branch
                sums[g] = sums[g] + (v[:IMG] + v[IMG:])
                value = X[g, rows, :] + masks * (scale[:, lanes(g)] * branch)
                for u in range(2):
                    stage[g, pl.ds(2 * q + u, IMG, stride=PLACES), :] = value[u * IMG : (u + 1) * IMG]
            return tuple(sums)

        zero = jnp.zeros((IMG, LANES), f32)
        sums = lax.fori_loop(0, PLACES // 2, body, (zero,) * G)
        for g in range(G):
            ACC[4, g] = sums[g]

        def narrow(i, c):
            rows = pl.ds(pl.multiple_of(i * 80, 16), 80)
            for g in range(G):
                NM[rows, lanes(g)] = stage[g, rows, :].astype(bf16)
            return c

        lax.fori_loop(0, ROWS // 80, narrow, 0)

    def small_sums():
        S[...] = jnp.zeros_like(S)
        for g in range(G):
            S[:TAPS, lanes(g)] = KG[g, :TAPS, :]
            for r, i in ((ROW_BIAS, 2), (ROW_GAIN, 0), (ROW_SHIFT, 1), (ROW_REDUCE, 3), (ROW_SCALE, 4)):
                S[r : r + 1, lanes(g)] = jnp.sum(ACC[i, g], axis=0, keepdims=True)
        for s in range(SLOTS):
            r = ROW_EXPAND + shard_of(s)
            S[pl.ds(r, 1), :] = jnp.sum(EBG[s], axis=0, keepdims=True)

    def tell(name):
        kind, _, rest = name.partition(".")
        where = [int(v) for v in rest.split(".")] if rest else []
        if kind[0] == "W":
            w_step(int(kind[1]), *where)
        elif kind[0] == "G":
            g_step(int(kind[1]), *where)
        elif kind[0] == "A":
            a_step(int(kind[1]), *where)
        else:
            small_step(int(kind[1]))

    loads[0].wait()
    biases = vector(depth_bias_ref)
    for g in range(G):
        ACC[0, g] = jnp.broadcast_to(biases[:, lanes(g)], (8, LANES))

    def finish_input(g, r, acc):
        cols = pl.ds(pl.multiple_of(g * LANES, LANES), LANES)
        for c in range(0, SIDE, 2):
            p = r * SIDE + c
            cot = CM[pl.ds(p * IMG, 2 * IMG), cols].astype(f32)
            for u in range(2):
                XH[g, pl.ds(p + u, IMG, stride=PLACES), :] = (
                    acc[c + u] * mask_at(p + u) + cot[u * IMG : (u + 1) * IMG]
                )

    def out_copy(g):
        return pltpu.make_async_copy(
            XH.at[g], in_grad_hbm.at[:, pl.ds(pl.multiple_of(g * LANES, LANES), LANES)], out_sem.at[1 + g]
        )

    def over_groups(names, call):
        kind = names[0].partition(":")[0]
        after = {}
        group = 0
        for name in names:
            if name.startswith(kind + ":"):
                group = int(name.partition(":")[2])
            else:
                after.setdefault(group, []).append(name)

        def between(g):
            if kind == "convb":
                out_copy(g).start()
            for i, told in after.items():
                @pl.when(g == i)
                def _():
                    for name in told:
                        tell(name)

        call(between)

    looped = {
        "conv": lambda between: conv(X, XH, ACC.at[0], False, None, between),
        "kg": kernel_grad,
        "convb": lambda between: conv(NC, None, None, True, finish_input, between),
    }

    def start_output():
        block_output()
        pltpu.make_async_copy(NM, out_hbm, out_sem.at[0]).start()

    def pixels_in():
        spread(NM)
        load_pixels()

    def cot_in():
        loads[1].wait()
        spread(BC)
        load_cot()

    def linears_ready(s):
        if s == 0:
            loads[2].wait()
            loads[3].wait()
        else:
            for m in range(2):
                w_step(4, s, m)
            e_arrival(s).wait_recv()

    def step(name):
        kind, _, rest = name.partition(":")
        where = [int(v) for v in rest.split(":")] if rest else []
        if "." in name or kind[0] == "S":
            tell(name)
        elif kind == "ln":
            n = ROWS // 16
            layernorm(n * where[0] // 20 * 5, n * (where[0] + 1) // 20 * 5)
        elif kind == "lnb":
            n = ROWS // 16
            layernorm_back(n * where[0] // 2, n * (where[0] + 1) // 2)
        elif kind == "h":
            if where[1] == 0:
                linears_ready(where[0])
            hidden_block(*where)
        elif kind == "gr":
            grad_block(*where)
        else:
            {
                "pix": pixels_in,
                "taps": load_taps,
                "cot": cot_in,
                "ncot": back_to_normed,
                "branch": to_branch,
                "bout": start_output,
                "small": small_sums,
            }[kind]()

    at = 0
    while at < len(PLAN):
        kind = PLAN[at].partition(":")[0]
        if kind in looped:
            last = max(i for i, name in enumerate(PLAN) if name.startswith(kind + ":"))
            over_groups(PLAN[at : last + 1], looped[kind])
            at = last + 1
        else:
            step(PLAN[at])
            at += 1
    for m in range(2):
        a_step(3, m)
    tail = [
        pltpu.make_async_copy(OUTB.at[0], gr_hbm, load_sem.at[0]),
        pltpu.make_async_copy(OUTB.at[1], ge_hbm, load_sem.at[1]),
        pltpu.make_async_copy(SALL, small_hbm, load_sem.at[2]),
    ]
    for copy in tail:
        copy.start()
    for m in range(2):
        own_pieces(m)[0].wait_send()
        in_middle(own_pieces(m)[1].wait_send)
    for s in range(1, SLOTS):
        e_copy(s).wait_send()
        for m in range(2):
            in_middle(relay(s, m).wait_send)
            for level in range(1, 4):
                w_copy(s, m, level).wait_send()
            z_copy(s, m).wait_send()
    for s in range(SLOTS):
        for m in range(2):
            for level in range(3):
                g_copy(s, m, level).wait_send()
    for m in range(2):
        for level in range(3):
            a_copy(m, level).wait_send()
    for j in range(1, 8):
        sr_copy(j).wait_send()
        sa_copy(j).wait_send()
    for o in range(1, n_tensor):
        sz_copy(o).wait_send()
    pltpu.make_async_copy(NM, out_hbm, out_sem.at[0]).wait()
    for g in range(G):
        out_copy(g).wait()
    for copy in tail:
        copy.wait()


def hand_over(
    out_in, grad_in, gr, ge, small,
    block_out, input_grad, kernel_grad, bias_grad, gain_grad, shift_grad,
    expand_grad, expand_bias_grad, reduce_grad, reduce_bias_grad, scale_grad,
    narrow, wide, whole_sem, in_sem, out_sem,
):
    D = gr.shape[0]
    third = D // 3
    whole = [
        pltpu.make_async_copy(grad_in, input_grad, whole_sem.at[0]),
        pltpu.make_async_copy(out_in, block_out, whole_sem.at[1]),
    ]
    parts = [(i, m) for i in range(3) for m in range(2)]

    def rows(i):
        return pl.ds(i * third, third)

    reads = {
        (i, m): pltpu.make_async_copy((gr, ge)[m].at[rows(i)], narrow.at[m, rows(i)], in_sem.at[m, i])
        for i, m in parts
    }
    writes = {
        (i, m): pltpu.make_async_copy(
            wide.at[m, rows(i)], (reduce_grad, expand_grad)[m].at[rows(i)], out_sem.at[m, i]
        )
        for i, m in parts
    }
    for part in parts:
        reads[part].start()
    for copy in whole:
        copy.start()
    kernel_grad[...] = small[:TAPS, :]
    own = ROW_EXPAND + lax.axis_index("tensor")
    for row, ref in (
        (ROW_BIAS, bias_grad), (ROW_GAIN, gain_grad), (ROW_SHIFT, shift_grad),
        (ROW_REDUCE, reduce_bias_grad), (ROW_SCALE, scale_grad),
    ):
        ref[...] = small[row : row + 1, :].reshape(D)
    expand_bias_grad[...] = small[pl.ds(own, 1), :].reshape(D)
    for i, m in parts:
        reads[i, m].wait()

        def widen(k, c):
            at = pl.ds(pl.multiple_of(i * third + k * 32, 32), 32)
            wide[m, at, :] = narrow[m, at, :].astype(f32)
            return c

        lax.fori_loop(0, third // 32, widen, 0)
        writes[i, m].start()
    for part in parts:
        writes[part].wait()
    for copy in whole:
        copy.wait()


def per_device(
    n_dp,
    n_tensor,
    pixels,
    crop_sides,
    out_cotangent,
    depth_kernel,
    depth_bias,
    norm_gain,
    norm_shift,
    expand_weight,
    expand_bias,
    reduce_weight,
    reduce_bias,
    layer_scale,
):
    rows, D = pixels.shape
    G = D // LANES
    img = rows // PLACES
    slots = n_tensor
    extra = max(n_dp.bit_length() - 4, 1)
    vmem = pl.BlockSpec(memory_space=pltpu.VMEM)
    hbm = pl.BlockSpec(memory_space=pltpu.HBM)
    smem = pl.BlockSpec(memory_space=pltpu.SMEM)
    V = pltpu.VMEM
    DMA = pltpu.SemaphoreType.DMA
    scratch = [
        V((8, rows, LANES), f32),
        V((G, rows, LANES), f32),
        V((G, rows, LANES), f32),
        V((rows, LANES), f32),
        V((rows, D), bf16),
        V((rows, D), bf16),
        V((rows, D), bf16),
        V((G, TAPS * img, LANES), f32),
        V((slots, D, D), bf16),
        V((slots, D, D), bf16),
        V((slots, 8, D), f32),
        V((slots, rows, D), bf16),
        V((slots, rows, D), bf16),
        V((slots, 8, D), f32),
        V((G, rows, LANES), f32),
        V((G, 56, LANES), f32),
        V((5, G, 8, LANES), f32),
        V((slots, 2, D, D), bf16),
        V((slots, 2, D // 2, D), bf16),
        V((slots, 2, D // 4, D), bf16),
        V((slots, 2, D // 8, D), bf16),
        V((slots - 1, 2, D // 8, D), bf16),
        V((extra, 2, D // 8 if n_dp > 8 else 16, D), bf16),
        V((2, D, D), bf16),
        V((SMALL, D), f32),
        V((7, 8, D), f32),
        V((slots, 8, D), f32),
        V((extra, 8, D), f32),
        V((SMALL, D), f32),
        DMA((4,)),
        DMA((1 + G,)),
        DMA((slots, 2, 4)),
        DMA((slots, 2, 4)),
        DMA((slots,)),
        DMA((slots,)),
        DMA((slots, 2, 6)),
        DMA((slots, 2, 6)),
        DMA((extra, 2)),
        DMA((extra, 2)),
        DMA((4, 8)),
        DMA((4, 8)),
    ]
    block_out, input_grad, gr, ge, small = pl.pallas_call(
        functools.partial(kernel, n_dp, n_tensor),
        out_shape=[
            jax.ShapeDtypeStruct((rows, D), bf16),
            jax.ShapeDtypeStruct((rows, D), f32),
            jax.ShapeDtypeStruct((D, D), bf16),
            jax.ShapeDtypeStruct((D, D), bf16),
            jax.ShapeDtypeStruct((SMALL, D), f32),
        ],
        in_specs=[hbm, smem, hbm, vmem, vmem, vmem, vmem, hbm, vmem, hbm, vmem, vmem],
        out_specs=[hbm] * 5,
        scratch_shapes=scratch,
        compiler_params=pltpu.CompilerParams(
            collective_id=0, has_side_effects=True, vmem_limit_bytes=61 << 20
        ),
        cost_estimate=pl.CostEstimate(
            flops=12 * rows * D * D * slots, bytes_accessed=20 * rows * D, transcendentals=0
        ),
    )(
        pixels,
        crop_sides,
        out_cotangent,
        depth_kernel,
        depth_bias,
        norm_gain,
        norm_shift,
        expand_weight,
        expand_bias,
        reduce_weight,
        reduce_bias,
        layer_scale,
    )
    vec = jax.ShapeDtypeStruct((D,), f32)
    square = jax.ShapeDtypeStruct((D, D), f32)
    return pl.pallas_call(
        hand_over,
        out_shape=[
            jax.ShapeDtypeStruct((rows, D), bf16),
            jax.ShapeDtypeStruct((rows, D), f32),
            jax.ShapeDtypeStruct((TAPS, D), f32),
            vec, vec, vec, square, vec, square, vec, vec,
        ],
        in_specs=[hbm, hbm, hbm, hbm, vmem],
        out_specs=[hbm, hbm, vmem, vmem, vmem, vmem, hbm, vmem, hbm, vmem, vmem],
        scratch_shapes=[
            V((2, D, D), bf16),
            V((2, D, D), f32),
            DMA((2,)),
            DMA((2, 3)),
            DMA((2, 3)),
        ],
        compiler_params=pltpu.CompilerParams(vmem_limit_bytes=60 << 20),
    )(block_out, input_grad, gr, ge, small)


def solution(mesh):
    in_specs = (
        P(("dp", "tensor"), None),
        P(("dp", "tensor")),
        P(("dp", "tensor"), None),
        P(),
        P(),
        P(),
        P(),
        P(None, "tensor"),
        P("tensor"),
        P("tensor", None),
        P(),
        P(),
    )
    out_specs = (
        P(("dp", "tensor"), None),
        P(("dp", "tensor"), None),
        P(),
        P(),
        P(),
        P(),
        P(None, "tensor"),
        P("tensor"),
        P("tensor", None),
        P(),
        P(),
    )
    return jax.shard_map(
        functools.partial(per_device, mesh.shape["dp"], mesh.shape["tensor"]),
        mesh=mesh,
        in_specs=in_specs,
        out_specs=out_specs,
        check_vma=False,
    )
```

```python
import functools
import math
import jax
import jax.numpy as jnp
from jax import lax
from jax.experimental import pallas as pl
from jax.experimental.pallas import tpu as pltpu
from jax.sharding import PartitionSpec as P

KERNEL = 7
SIDE = 10
PLACES = SIDE * SIDE
TAPS = KERNEL * KERNEL
MARGIN = KERNEL // 2
LANES = 128
BLOCK = 256
norm_eps = 1e-06
f32 = jnp.float32
bf16 = jnp.bfloat16
MESH = pl.DeviceIdType.MESH
ROW_BIAS, ROW_GAIN, ROW_SHIFT, ROW_REDUCE, ROW_SCALE, ROW_EXPAND = 49, 50, 51, 52, 53, 54
SMALL = 64
PLAN = (
    "taps", "pix", "conv:0", "conv:1", "W1.1.0", "conv:2", "conv:3", "W1.1.1", "W1.2.0", "conv:4",
    "W2.1.0", "conv:5", "W2.1.1", "W1.2.1", "cot", "ln", "h:0:0", "h:0:1", "W1.3.0", "h:0:2",
    "W3.1.0", "W2.2.0", "h:0:3", "W3.1.1", "W1.3.1", "W2.2.1", "h:1:0", "h:1:1", "h:1:2", "h:1:3",
    "gr:1:0", "gr:1:1", "gr:1:2", "G0.1.1", "gr:0:0", "W3.2.0", "W2.3.0", "gr:0:1", "G1.1.1",
    "W3.2.1", "W2.3.1", "h:2:0", "G0.1.0", "h:2:1", "h:2:2", "h:2:3", "gr:2:0", "gr:2:1", "gr:2:2",
    "G0.2.0", "gr:0:2", "G0.2.1", "W3.3.0", "G1.2.0", "W3.3.1", "G1.2.1", "G1.1.0", "h:3:0",
    "h:3:1", "h:3:2", "h:3:3", "gr:3:0", "gr:3:1", "gr:3:2", "G2.2.0", "G0.0.1", "G0.3.1",
    "G0.3.0", "G2.2.1", "ncot", "G1.3.1", "G3.2.0", "G1.3.0", "G1.0.1", "G3.2.1", "lnb", "kg:0",
    "kg:1", "G0.0.0", "kg:2", "G2.3.1", "kg:3", "kg:4", "G1.0.0", "kg:5", "G2.3.0", "G3.3.1",
    "branch", "bout", "G2.0.1", "G3.3.0", "G2.0.0", "small", "convb:0", "A0.1", "S0", "A0.0", "S1",
    "A1.1", "A1.0", "convb:1", "convb:2", "convb:3", "S2", "convb:4", "convb:5", "A2.1", "S3",
    "A2.0",
)


def gelu_both(h):
    phi = 0.5 + 0.5 * lax.erf(h * math.sqrt(0.5))
    bell = jnp.exp2(h * h * (-0.5 * math.log2(math.e)))
    return h * phi, phi + h * (1.0 / math.sqrt(2.0 * math.pi)) * bell


def dot(a, b):
    return jnp.dot(a, b, preferred_element_type=f32)


def dot_rows(a, b):
    return lax.dot_general(a, b, (((0,), (0,)), ((), ())), preferred_element_type=f32)


def dot_t(a, b):
    return lax.dot_general(a, b, (((1,), (1,)), ((), ())), preferred_element_type=f32)


def kernel(
    n_dp,
    n_tensor,
    pix_hbm,
    side_hbm,
    cot_hbm,
    taps_hbm,
    depth_bias_hbm,
    gain_hbm,
    shift_hbm,
    we_hbm,
    eb_hbm,
    wr_hbm,
    rb_hbm,
    scale_hbm,
    out_hbm,
    in_grad_hbm,
    gr_hbm,
    ge_hbm,
    small_hbm,
    side_ref,
    taps_ref,
    depth_bias_ref,
    gain_ref,
    shift_ref,
    eb_ref,
    rb_ref,
    scale_ref,
    stage,
    X,
    XH,
    RSTD,
    NM,
    CM,
    BC,
    KB,
    WE,
    WR,
    EB,
    ACT,
    HC,
    EBG,
    NC,
    KG,
    ACC,
    GS,
    R0,
    R1,
    R2,
    RP,
    RZ,
    RX,
    OUTB,
    S,
    SR,
    SZ,
    SX,
    SALL,
    load_sem,
    out_sem,
    w_send,
    w_recv,
    e_send,
    e_recv,
    g_send,
    g_recv,
    x_send,
    x_recv,
    s_send,
    s_recv,
):
    D = NM.shape[1]
    G = D // LANES
    ROWS = NM.shape[0]
    IMG = ROWS // PLACES
    HALF, QUART, PIECE = D // 2, D // 4, D // 8
    SLOTS = n_tensor
    extra = n_dp.bit_length() - 4
    dp = lax.axis_index("dp")
    tz = lax.axis_index("tensor")
    core = lax.rem(dp, 2)
    xb = lax.rem(lax.div(dp, 2), 2)
    yb = lax.rem(lax.div(dp, 4), 2)
    low = lax.rem(dp, 8)
    bits = (core, xb, yb)

    def flip(b):
        bit = bits[b] if b < 3 else lax.rem(lax.div(dp, 1 << b), 2)
        return dp + (1 - 2 * bit) * (1 << b)

    def flip_low(j):
        d = dp
        for b in range(3):
            if j >> b & 1:
                d = d + (1 - 2 * bits[b]) * (1 << b)
        return d


    t_low = lax.rem(tz, 2)
    t_high = lax.div(tz, 2)
    partner = tz + 1 - 2 * t_low
    middle = t_low + t_high - 2 * t_low * t_high
    across = 3 - tz

    def shard_of(s):
        return (tz, partner, 2 - t_high, 3 - 3 * t_high)[s]

    peers = [(flip_low(j), tz) for j in range(1, 8)]
    peers += [(dp, lax.rem(tz + o, n_tensor)) for o in range(1, n_tensor)]
    peers += [(flip(b), tz) for b in range(3, 3 + extra)]
    barrier = pltpu.get_barrier_semaphore()
    for peer in peers:
        pl.semaphore_signal(barrier, inc=1, device_id=peer, device_id_type=MESH)

    loads = [
        pltpu.make_async_copy(pix_hbm, NM, load_sem.at[0]),
        pltpu.make_async_copy(cot_hbm, BC, load_sem.at[1]),
        pltpu.make_async_copy(we_hbm, WE.at[0], load_sem.at[2]),
        pltpu.make_async_copy(wr_hbm, WR.at[0], load_sem.at[3]),
    ]
    rows_in = [
        (eb_hbm, eb_ref), (depth_bias_hbm, depth_bias_ref), (gain_hbm, gain_ref),
        (shift_hbm, shift_ref), (rb_hbm, rb_ref), (scale_hbm, scale_ref), (side_hbm, side_ref),
        (taps_hbm, taps_ref),
    ]
    rows_in = [pltpu.make_async_copy(a, b, load_sem.at[4 + i]) for i, (a, b) in enumerate(rows_in)]
    for copy in rows_in + loads:
        copy.start()

    def vector(ref):
        return ref[...].astype(f32).reshape(1, D)

    def remote(src, dst, send, recv, device):
        return pltpu.make_async_remote_copy(
            src_ref=src, dst_ref=dst, send_sem=send, recv_sem=recv,
            device_id=device, device_id_type=MESH,
        )

    W = (WE, WR)
    first = (xb, yb)
    second = (yb, xb)
    first_peer = (flip(1), flip(2))
    second_peer = (flip(2), flip(1))

    def w_rows(m, level):
        start = core * HALF
        if level <= 2:
            start = start + second[m] * QUART
        if level <= 1:
            start = start + first[m] * PIECE
        size = (PIECE, PIECE, QUART, HALF)[level]
        return pl.ds(pl.multiple_of(start, 16), size)

    def w_copy(s, m, level):
        here = W[m].at[s, w_rows(m, level), :]
        device = ((first_peer[m], tz), (second_peer[m], tz), (flip(0), tz))[level - 1]
        return remote(here, here, w_send.at[s, m, level], w_recv.at[s, m, level], device)

    def z_piece(m, source, slot, device):
        rows = w_rows(m, 0)
        src = (we_hbm, wr_hbm)[m].at[rows, :] if source == 0 else W[m].at[source, rows, :]
        send = w_send.at[0, m, slot] if source == 0 else w_send.at[source, m, 0]
        return remote(src, W[m].at[slot, rows, :], send, w_recv.at[slot, m, 0], (dp, device))

    def own_pieces(m):
        return z_piece(m, 0, 1, partner), z_piece(m, 0, 2, across)

    def relay(s, m):
        return z_piece(m, 1, 3, across) if s == 1 else z_piece(m, s, s, partner)

    def in_middle(act):
        @pl.when(middle == 1)
        def _():
            act()

    def e_copy(o):
        own = EB.at[tz]
        return remote(own, own, e_send.at[o], e_recv.at[tz], (dp, lax.rem(tz + o, n_tensor)))

    def e_arrival(s):
        there = EB.at[shard_of(s)]
        return remote(there, there, e_send.at[s], e_recv.at[shard_of(s)], (dp, partner))

    def w_step(level, s, m):
        if level == 0:
            to_partner, to_other = own_pieces(m)
            to_partner.start()
            in_middle(to_other.start)
            return
        if level == 1:
            z_piece(m, 0, s, partner).wait_recv()
            in_middle(relay(s, m).start)
        else:
            w_copy(s, m, level - 1).wait_recv()
        if level < 4:
            w_copy(s, m, level).start()

    pl.semaphore_wait(barrier, len(peers))
    for m in range(2):
        w_step(0, 0, m)
    for copy in rows_in:
        copy.wait()
    EB[tz] = jnp.broadcast_to(vector(eb_ref), (8, D))
    for o in range(1, n_tensor):
        e_copy(o).start()

    g_first = (yb, xb)
    g_second = (xb, yb)
    g_first_peer = (flip(2), flip(1))
    g_second_peer = (flip(1), flip(2))

    def g_start(m, level):
        start = core * HALF
        if level >= 1:
            start = start + g_first[m] * QUART
        if level >= 2:
            start = start + g_second[m] * PIECE
        return start

    PLANE = {0: 0, 2: 1, 3: 2}

    def g_copy(s, m, level):
        if level == 0:
            start, size, peer, dst = (1 - core) * HALF, HALF, flip(0), R0.at[s, m]
        elif level == 1:
            start = g_start(m, 0) + (1 - g_first[m]) * QUART
            size, peer, dst = QUART, g_first_peer[m], R1.at[PLANE[s], m]
        else:
            start = g_start(m, 1) + (1 - g_second[m]) * PIECE
            size, peer, dst = PIECE, g_second_peer[m], R2.at[PLANE[s], m]
        src = GS.at[s, m, pl.ds(pl.multiple_of(start, 16), size), :]
        return remote(src, dst, g_send.at[s, m, level], g_recv.at[s, m, level], (peer, tz))

    def p_copy(m):
        src = GS.at[1, m, pl.ds(pl.multiple_of(core * HALF, 16), HALF), :]
        return remote(src, RP.at[m], g_send.at[1, m, 1], g_recv.at[1, m, 1], (dp, partner))

    def z_copy(s, m):
        src = GS.at[s, m, pl.ds(pl.multiple_of(g_start(m, 2), 16), PIECE), :]
        slot = 3 - middle
        return remote(
            src, RZ.at[slot - 2, m], g_send.at[s, m, 3], g_recv.at[slot, m, 3], (dp, shard_of(s))
        )

    def z_arrival(s, m):
        src = GS.at[s, m, pl.ds(pl.multiple_of(g_start(m, 2), 16), PIECE), :]
        return remote(src, RZ.at[s - 2, m], g_send.at[s, m, 3], g_recv.at[s, m, 3], (dp, partner))

    def g_step(level, s, m):
        if level > 0:
            g_copy(s, m, level - 1).wait_recv()
            got = [(R0.at[s, m], R1.at[PLANE.get(s, 0), m], R2.at[PLANE.get(s, 0), m])[level - 1]]
            if s == 0 and level == 1:
                p_copy(m).wait_recv()
                got.append(RP.at[m])
            start = g_start(m, level - 1)
            size = (HALF, QUART, PIECE)[level - 1]

            def add(i, c):
                rows = pl.ds(pl.multiple_of(start + i * 16, 16), 16)
                mine = pl.ds(pl.multiple_of(i * 16, 16), 16)
                total = GS[s, m, rows, :].astype(f32)
                for ref in got:
                    total = total + ref[mine, :].astype(f32)
                GS[s, m, rows, :] = total.astype(bf16)
                return c

            lax.fori_loop(0, size // 16, add, 0, unroll=2)
        if s == 1 and level == 1:
            p_copy(m).start()
        elif level < 3:
            g_copy(s, m, level).start()
        elif s > 0:
            z_copy(s, m).start()

    def o_rows(m, level):
        start = 0
        if level <= 1:
            start = start + g_first[m] * QUART
        if level == 0:
            start = start + g_second[m] * PIECE
        return pl.ds(pl.multiple_of(start, 16), (PIECE, QUART, HALF)[level])

    core_half = pl.ds(pl.multiple_of(core * HALF, 16), HALF)

    def a_copy(m, level):
        here = OUTB.at[m, o_rows(m, level), :]
        there = here if level < 2 else (gr_hbm, ge_hbm)[m].at[core_half, :]
        peer = (g_second_peer[m], g_first_peer[m], flip(0))[level]
        return remote(here, there, g_send.at[0, m, 3 + level], g_recv.at[0, m, 3 + level], (peer, tz))

    def own_half(m):
        return pltpu.make_async_copy(
            OUTB.at[m], (gr_hbm, ge_hbm)[m].at[core_half, :], load_sem.at[m]
        )

    def x_copy(m, b):
        here = OUTB.at[m, o_rows(m, 0), :]
        return remote(here, RX.at[b - 3, m], x_send.at[b - 3, m], x_recv.at[b - 3, m], (flip(b), tz))

    def finish_sum(m):
        g_step(3, 0, m)
        for s in range(2, SLOTS):
            z_arrival(s, m).wait_recv()
        start = g_start(m, 2)
        there = start - core * HALF

        def add(i, c):
            rows = pl.ds(pl.multiple_of(start + i * 16, 16), 16)
            own = pl.ds(pl.multiple_of(i * 16, 16), 16)
            total = GS[0, m, rows, :].astype(f32)
            for s in range(2, SLOTS):
                total = total + RZ[s - 2, m, own, :].astype(f32)
            OUTB[m, pl.ds(pl.multiple_of(there + i * 16, 16), 16), :] = total.astype(bf16)
            return c

        lax.fori_loop(0, PIECE // 16, add, 0)
        for b in range(3, 3 + extra):
            x_copy(m, b).start()
            x_copy(m, b).wait()

            def add_x(i, c):
                rows = pl.ds(pl.multiple_of(there + i * 16, 16), 16)
                OUTB[m, rows, :] = (
                    OUTB[m, rows, :] + RX[b - 3, m, pl.ds(pl.multiple_of(i * 16, 16), 16), :]
                )
                return c

            lax.fori_loop(0, PIECE // 16, add_x, 0)

    def a_step(level, m):
        if level == 0:
            finish_sum(m)
        else:
            a_copy(m, level - 1).wait_recv()
        if level < 3:
            a_copy(m, level).start()
        if level == 2:
            own_half(m).start()

    def sr_copy(j):
        dst_low = flip_low(j)
        rows = pl.ds(pl.multiple_of(lax.rem(dst_low, 8) * 8, 8), 8)
        return remote(S.at[rows, :], SR.at[j - 1], s_send.at[0, j], s_recv.at[0, j], (dst_low, tz))

    def sz_copy(o):
        return remote(
            SZ.at[tz], SZ.at[tz], s_send.at[1, o], s_recv.at[1, o],
            (dp, lax.rem(tz + o, n_tensor)),
        )

    own_small = pl.ds(pl.multiple_of(low * 8, 8), 8)

    def sa_copy(j):
        here = SALL.at[own_small, :]
        return remote(here, here, s_send.at[2, j], s_recv.at[2, j], (flip_low(j), tz))

    def sx_copy(b):
        return remote(
            SALL.at[own_small, :], SX.at[b - 3], s_send.at[3, b], s_recv.at[3, b], (flip(b), tz)
        )

    def small_step(level):
        if level == 0:
            for j in range(1, 8):
                sr_copy(j).start()
        elif level == 1:
            total = S[own_small, :]
            for j in range(1, 8):
                sr_copy(j).wait_recv()
                total = total + SR[j - 1]
            SZ[tz] = total
            for o in range(1, n_tensor):
                sz_copy(o).start()
        elif level == 2:
            for o in range(1, n_tensor):
                sz_copy(o).wait_recv()
            total = SZ[0]
            for o in range(1, n_tensor):
                total = total + SZ[o]
            SALL[own_small, :] = total
            for b in range(3, 3 + extra):
                sx_copy(b).start()
                sx_copy(b).wait()
                SALL[own_small, :] = SALL[own_small, :] + SX[b - 3]
            for j in range(1, 8):
                sa_copy(j).start()
        else:
            for j in range(1, 8):
                sa_copy(j).wait_recv()

    row = lax.broadcasted_iota(jnp.int32, (IMG, LANES), 0)
    sides = jnp.zeros((IMG, LANES), jnp.int32)
    for i in range(IMG):
        sides = jnp.where(row == i, side_ref[i], sides)

    def mask_at(p):
        if isinstance(p, int):
            return jnp.where(sides > max(p // SIDE, p % SIDE), 1.0, 0.0)
        return jnp.where(sides > jnp.maximum(lax.div(p, SIDE), lax.rem(p, SIDE)), 1.0, 0.0)

    def lanes(g):
        return slice(g * LANES, (g + 1) * LANES)

    def place(p):
        return pl.ds(p * IMG, IMG)

    def spread(src):
        def body(i, c):
            rows = pl.ds(pl.multiple_of(i * 80, 16), 80)
            for g in range(G):
                stage[g, rows, :] = src[rows, lanes(g)].astype(f32)
            return c

        lax.fori_loop(0, ROWS // 80, body, 0)

    def load_pixels():
        def body(p, c):
            m = mask_at(p)
            rows = pl.ds(pl.multiple_of(p * IMG, IMG), IMG)
            for g in range(G):
                X[g, rows, :] = stage[g, pl.ds(p, IMG, stride=PLACES), :] * m
            return c

        lax.fori_loop(0, PLACES, body, 0, unroll=2)

    def load_cot():
        scale = vector(scale_ref)

        def body(q, sums):
            sums = list(sums)
            masks = [mask_at(2 * q + u) for u in range(2)]
            rows = pl.ds(pl.multiple_of(q * 2 * IMG, 2 * IMG), 2 * IMG)
            for g in range(G):
                c = [stage[g, pl.ds(2 * q + u, IMG, stride=PLACES), :] * masks[u] for u in range(2)]
                c = jnp.concatenate(c, axis=0)
                CM[rows, lanes(g)] = c.astype(bf16)
                b = (c * scale[:, lanes(g)]).astype(bf16)
                BC[rows, lanes(g)] = b
                b = b.astype(f32)
                sums[g] = sums[g] + (b[:IMG] + b[IMG:])
            return tuple(sums)

        zero = jnp.zeros((IMG, LANES), f32)
        sums = lax.fori_loop(0, PLACES // 2, body, (zero,) * G)
        for g in range(G):
            ACC[3, g] = sums[g]

    def load_taps():
        for g in range(G):
            for t in range(TAPS):
                KB[g, place(t), :] = jnp.broadcast_to(
                    taps_ref[t : t + 1, lanes(g)].astype(f32), (IMG, LANES)
                )

    def conv(src, dst, bias, flipped, post, between):
        def one(g, carry):
            for r in range(SIDE):
                acc = [None] * SIDE if bias is None else [bias[g]] * SIDE
                for rr in range(max(0, r - MARGIN), min(SIDE, r + MARGIN + 1)):
                    xs = [src[g, place(rr * SIDE + c), :] for c in range(SIDE)]
                    for dc in range(KERNEL):
                        t = (rr - r + MARGIN) * KERNEL + dc
                        k = KB[g, place(TAPS - 1 - t if flipped else t), :]
                        for c in range(SIDE):
                            cc = c + dc - MARGIN
                            if 0 <= cc < SIDE:
                                v = xs[cc] * k
                                acc[c] = v if acc[c] is None else acc[c] + v
                if post is None:
                    for c in range(SIDE):
                        dst[g, place(r * SIDE + c), :] = acc[c]
                else:
                    post(g, r, acc)
            between(g)
            return carry

        lax.fori_loop(0, G, one, 0)

    def tree(parts):
        parts = list(parts)
        while len(parts) > 1:
            parts = [
                parts[i] + parts[i + 1] if i + 1 < len(parts) else parts[i]
                for i in range(0, len(parts), 2)
            ]
        return parts[0]

    def fold(v):
        return tree(v[i : i + 8] for i in range(0, v.shape[0], 8))

    def layernorm():
        gain = vector(gain_ref)
        shift = vector(shift_ref)

        def body(q, c):
            rows = pl.ds(pl.multiple_of(q * 32, 32), 32)
            v = [XH[g, rows, :] for g in range(G)]
            mean = jnp.sum(tree(v), axis=1, keepdims=True) * (1.0 / D)
            v = [a - mean for a in v]
            total = tree([a * a for a in v])
            rstd = lax.rsqrt(jnp.sum(total, axis=1, keepdims=True) * (1.0 / D) + norm_eps)
            RSTD[rows, :] = jnp.broadcast_to(rstd, (32, LANES))
            for g in range(G):
                xh = v[g] * rstd
                XH[g, rows, :] = xh
                NM[rows, lanes(g)] = (xh * gain[:, lanes(g)] + shift[:, lanes(g)]).astype(bf16)
            return c

        lax.fori_loop(0, ROWS // 32, body, 0, unroll=5)

    def layernorm_back():
        gain = vector(gain_ref)

        def body(q, sums):
            rows = pl.ds(pl.multiple_of(q * 160, 32), 160)
            rstd = RSTD[rows, :]
            xh = [XH[g, rows, :] for g in range(G)]
            nc = [NC[g, rows, :] for g in range(G)]
            d = [nc[g] * gain[:, lanes(g)] for g in range(G)]
            m1 = jnp.sum(tree(d), axis=1, keepdims=True) * (1.0 / D)
            m2 = jnp.sum(tree([a * b for a, b in zip(d, xh)]), axis=1, keepdims=True) * (1.0 / D)
            out = []
            for g in range(G):
                dm = rstd * (d[g] - m1 - xh[g] * m2)
                NC[g, rows, :] = dm
                old = sums[g]
                out.append((old[0] + fold(nc[g] * xh[g]), old[1] + fold(nc[g]), old[2] + fold(dm)))
            return tuple(out)

        zero = jnp.zeros((8, LANES), f32)
        sums = lax.fori_loop(0, ROWS // 160, body, ((zero, zero, zero),) * G)
        for i in range(3):
            for g in range(G):
                ACC[i, g] = sums[g][i]

    def kernel_grad(between):
        def one(g, carry):
            for dr in range(KERNEL):
                acc = [[None, None] for _ in range(KERNEL)]
                for r in range(SIDE):
                    rr = r + dr - MARGIN
                    if not 0 <= rr < SIDE:
                        continue
                    ds = [NC[g, place(r * SIDE + c), :] for c in range(SIDE)]
                    xs = [X[g, place(rr * SIDE + c), :] for c in range(SIDE)]
                    for dc in range(KERNEL):
                        a = acc[dc]
                        for c in range(SIDE):
                            cc = c + dc - MARGIN
                            if 0 <= cc < SIDE:
                                v = ds[c] * xs[cc]
                                a[c % 2] = v if a[c % 2] is None else a[c % 2] + v
                for dc in range(KERNEL):
                    t = dr * KERNEL + dc
                    KG[g, t : t + 1, :] = jnp.sum(acc[dc][0] + acc[dc][1], axis=0, keepdims=True)
            between(g)
            return carry

        lax.fori_loop(0, G, one, 0)

    def hidden_block(s, j):
        if j < D // BLOCK:
            cols = slice(j * BLOCK, (j + 1) * BLOCK)
            base = j % 2 * 4
            h = dot(NM[...], WE[s, :, cols])
            stage[base] = h[:, :LANES]
            stage[base + 1] = h[:, LANES:]
            a = dot_t(BC[...], WR[s, cols, :])
            stage[base + 2] = a[:, :LANES]
            stage[base + 3] = a[:, LANES:]
        if j > 0:
            base = (j - 1) % 2 * 4
            for u in range(2):
                mine = slice((j - 1) * BLOCK + u * LANES, (j - 1) * BLOCK + (u + 1) * LANES)
                bias = EB[shard_of(s), :, mine]
                bias = jnp.concatenate([bias, bias], axis=0)
                total = None
                for i in range(ROWS // 16):
                    rows = slice(i * 16, (i + 1) * 16)
                    value, slope = gelu_both(stage[base + u, rows, :] + bias)
                    ACT[s, rows, mine] = value.astype(bf16)
                    w = (stage[base + 2 + u, rows, :] * slope).astype(bf16)
                    HC[s, rows, mine] = w
                    w = w.astype(f32)
                    w = w[:8] + w[8:]
                    total = w if total is None else total + w
                EBG[s, :, mine] = total

    def grad_block(s, j):
        cols = slice(j * BLOCK, (j + 1) * BLOCK)
        GS[s, 0, cols, :] = dot_rows(ACT[s, :, cols], BC[...]).astype(bf16)
        GS[s, 1, :, cols] = dot_rows(NM[...], HC[s, :, cols]).astype(bf16)

    def back_to_normed():
        for n in range(D // BLOCK):
            cols = slice(n * BLOCK, (n + 1) * BLOCK)
            total = dot_t(HC[0], WE[0, cols, :])
            for s in range(1, SLOTS):
                total = total + dot_t(HC[s], WE[s, cols, :])
            NC[2 * n] = total[:, :LANES]
            NC[2 * n + 1] = total[:, LANES:]

    def to_branch():
        for n in range(D // BLOCK):
            cols = slice(n * BLOCK, (n + 1) * BLOCK)
            total = dot(ACT[0], WR[0, :, cols])
            for s in range(1, SLOTS):
                total = total + dot(ACT[s], WR[s, :, cols])
            XH[2 * n] = total[:, :LANES]
            XH[2 * n + 1] = total[:, LANES:]

    def block_output():
        scale = vector(scale_ref)
        shift = vector(rb_ref)

        def body(q, sums):
            sums = list(sums)
            rows = pl.ds(pl.multiple_of(q * 2 * IMG, 2 * IMG), 2 * IMG)
            masks = jnp.concatenate([mask_at(2 * q + u) for u in range(2)], axis=0)
            for g in range(G):
                branch = XH[g, rows, :] + shift[:, lanes(g)]
                v = CM[rows, lanes(g)].astype(f32) * branch
                sums[g] = sums[g] + (v[:IMG] + v[IMG:])
                value = X[g, rows, :] + masks * (scale[:, lanes(g)] * branch)
                for u in range(2):
                    stage[g, pl.ds(2 * q + u, IMG, stride=PLACES), :] = value[u * IMG : (u + 1) * IMG]
            return tuple(sums)

        zero = jnp.zeros((IMG, LANES), f32)
        sums = lax.fori_loop(0, PLACES // 2, body, (zero,) * G)
        for g in range(G):
            ACC[4, g] = sums[g]

        def narrow(i, c):
            rows = pl.ds(pl.multiple_of(i * 80, 16), 80)
            for g in range(G):
                NM[rows, lanes(g)] = stage[g, rows, :].astype(bf16)
            return c

        lax.fori_loop(0, ROWS // 80, narrow, 0)

    def small_sums():
        S[...] = jnp.zeros_like(S)
        for g in range(G):
            S[:TAPS, lanes(g)] = KG[g, :TAPS, :]
            for r, i in ((ROW_BIAS, 2), (ROW_GAIN, 0), (ROW_SHIFT, 1), (ROW_REDUCE, 3), (ROW_SCALE, 4)):
                S[r : r + 1, lanes(g)] = jnp.sum(ACC[i, g], axis=0, keepdims=True)
        for s in range(SLOTS):
            r = ROW_EXPAND + shard_of(s)
            S[pl.ds(r, 1), :] = jnp.sum(EBG[s], axis=0, keepdims=True)

    def tell(name):
        kind, _, rest = name.partition(".")
        where = [int(v) for v in rest.split(".")] if rest else []
        if kind[0] == "W":
            w_step(int(kind[1]), *where)
        elif kind[0] == "G":
            g_step(int(kind[1]), *where)
        elif kind[0] == "A":
            a_step(int(kind[1]), *where)
        else:
            small_step(int(kind[1]))

    loads[0].wait()
    biases = vector(depth_bias_ref)
    for g in range(G):
        ACC[0, g] = jnp.broadcast_to(biases[:, lanes(g)], (8, LANES))

    def finish_input(g, r, acc):
        cols = pl.ds(pl.multiple_of(g * LANES, LANES), LANES)
        for c in range(0, SIDE, 2):
            p = r * SIDE + c
            cot = CM[pl.ds(p * IMG, 2 * IMG), cols].astype(f32)
            for u in range(2):
                XH[g, pl.ds(p + u, IMG, stride=PLACES), :] = (
                    acc[c + u] * mask_at(p + u) + cot[u * IMG : (u + 1) * IMG]
                )

    def out_copy(g):
        return pltpu.make_async_copy(
            XH.at[g], in_grad_hbm.at[:, pl.ds(pl.multiple_of(g * LANES, LANES), LANES)], out_sem.at[1 + g]
        )

    def over_groups(names, call):
        kind = names[0].partition(":")[0]
        after = {}
        group = 0
        for name in names:
            if name.startswith(kind + ":"):
                group = int(name.partition(":")[2])
            else:
                after.setdefault(group, []).append(name)

        def between(g):
            if kind == "convb":
                out_copy(g).start()
            for i, told in after.items():
                @pl.when(g == i)
                def _():
                    for name in told:
                        tell(name)

        call(between)

    looped = {
        "conv": lambda between: conv(X, XH, ACC.at[0], False, None, between),
        "kg": kernel_grad,
        "convb": lambda between: conv(NC, None, None, True, finish_input, between),
    }

    def start_output():
        block_output()
        pltpu.make_async_copy(NM, out_hbm, out_sem.at[0]).start()

    def pixels_in():
        spread(NM)
        load_pixels()

    def cot_in():
        loads[1].wait()
        spread(BC)
        load_cot()

    def linears_ready(s):
        if s == 0:
            loads[2].wait()
            loads[3].wait()
        else:
            for m in range(2):
                w_step(4, s, m)
            e_arrival(s).wait_recv()

    def step(name):
        kind, _, rest = name.partition(":")
        where = [int(v) for v in rest.split(":")] if rest else []
        if "." in name or kind[0] == "S":
            tell(name)
        elif kind == "h":
            if where[1] == 0:
                linears_ready(where[0])
            hidden_block(*where)
        elif kind == "gr":
            grad_block(*where)
        else:
            {
                "pix": pixels_in,
                "taps": load_taps,
                "cot": cot_in,
                "ln": layernorm,
                "lnb": layernorm_back,
                "ncot": back_to_normed,
                "branch": to_branch,
                "bout": start_output,
                "small": small_sums,
            }[kind]()

    at = 0
    while at < len(PLAN):
        kind = PLAN[at].partition(":")[0]
        if kind in looped:
            last = max(i for i, name in enumerate(PLAN) if name.startswith(kind + ":"))
            over_groups(PLAN[at : last + 1], looped[kind])
            at = last + 1
        else:
            step(PLAN[at])
            at += 1
    tail = [
        pltpu.make_async_copy(SALL, small_hbm, load_sem.at[2]),
    ]
    for copy in tail:
        copy.start()
    for m in range(2):
        a_step(3, m)
    for m in range(2):
        own_pieces(m)[0].wait_send()
        in_middle(own_pieces(m)[1].wait_send)
    for s in range(1, SLOTS):
        e_copy(s).wait_send()
        for m in range(2):
            in_middle(relay(s, m).wait_send)
            for level in range(1, 4):
                w_copy(s, m, level).wait_send()
            if s > 1:
                z_copy(s, m).wait_send()
    for s in range(SLOTS):
        for m in range(2):
            for level in range(3 if s != 1 else 1):
                g_copy(s, m, level).wait_send()
    for m in range(2):
        p_copy(m).wait_send()
        for level in range(3):
            a_copy(m, level).wait_send()
    for j in range(1, 8):
        sr_copy(j).wait_send()
        sa_copy(j).wait_send()
    for o in range(1, n_tensor):
        sz_copy(o).wait_send()
    pltpu.make_async_copy(NM, out_hbm, out_sem.at[0]).wait()
    for g in range(G):
        out_copy(g).wait()
    for copy in tail:
        copy.wait()
    for m in range(2):
        own_half(m).wait()


def hand_over(
    out_in, grad_in, gr, ge, small,
    block_out, input_grad, kernel_grad, bias_grad, gain_grad, shift_grad,
    expand_grad, expand_bias_grad, reduce_grad, reduce_bias_grad, scale_grad,
    narrow, wide, grad_rows, out_rows, there_sem, back_sem, in_sem, out_sem,
):
    D = gr.shape[0]
    third = D // 3
    half = out_in.shape[0] // 2
    halves = [
        (held.at[pl.ds(i * half, half)], src.at[pl.ds(i * half, half)], dst.at[pl.ds(i * half, half)])
        for i in range(2)
        for held, src, dst in ((grad_rows, grad_in, input_grad), (out_rows, out_in, block_out))
    ]
    there = [pltpu.make_async_copy(v[1], v[0], there_sem.at[i]) for i, v in enumerate(halves)]
    back = [pltpu.make_async_copy(v[0], v[2], back_sem.at[i]) for i, v in enumerate(halves)]
    parts = [(i, m) for i in range(3) for m in range(2)]

    def rows(i):
        return pl.ds(i * third, third)

    reads = {
        (i, m): pltpu.make_async_copy((gr, ge)[m].at[rows(i)], narrow.at[m, rows(i)], in_sem.at[m, i])
        for i, m in parts
    }
    writes = {
        (i, m): pltpu.make_async_copy(
            wide.at[m, rows(i)], (reduce_grad, expand_grad)[m].at[rows(i)], out_sem.at[m, i]
        )
        for i, m in parts
    }
    for part in parts:
        reads[part].start()
    kernel_grad[...] = small[:TAPS, :]
    own = ROW_EXPAND + lax.axis_index("tensor")
    for row, ref in (
        (ROW_BIAS, bias_grad), (ROW_GAIN, gain_grad), (ROW_SHIFT, shift_grad),
        (ROW_REDUCE, reduce_bias_grad), (ROW_SCALE, scale_grad),
    ):
        ref[...] = small[row : row + 1, :].reshape(D)
    expand_bias_grad[...] = small[pl.ds(own, 1), :].reshape(D)
    for i, m in parts:
        reads[i, m].wait()
        if i == 0 and m == 0:
            for copy in there:
                copy.start()

        def widen(k, c):
            at = pl.ds(pl.multiple_of(i * third + k * 32, 32), 32)
            wide[m, at, :] = narrow[m, at, :].astype(f32)
            return c

        lax.fori_loop(0, third // 32, widen, 0)
        writes[i, m].start()
    for arrived, copy in zip(there, back):
        arrived.wait()
        copy.start()
    for part in parts:
        writes[part].wait()
    for copy in back:
        copy.wait()


def per_device(
    n_dp,
    n_tensor,
    pixels,
    crop_sides,
    out_cotangent,
    depth_kernel,
    depth_bias,
    norm_gain,
    norm_shift,
    expand_weight,
    expand_bias,
    reduce_weight,
    reduce_bias,
    layer_scale,
):
    rows, D = pixels.shape
    G = D // LANES
    img = rows // PLACES
    slots = n_tensor
    extra = max(n_dp.bit_length() - 4, 1)
    vmem = pl.BlockSpec(memory_space=pltpu.VMEM)
    hbm = pl.BlockSpec(memory_space=pltpu.HBM)
    V = pltpu.VMEM
    DMA = pltpu.SemaphoreType.DMA
    scratch = [pltpu.SMEM((img,), jnp.int32), V((TAPS, D), bf16)] + [V((D,), bf16) for _ in range(6)] + [
        V((8, rows, LANES), f32),
        V((G, rows, LANES), f32),
        V((G, rows, LANES), f32),
        V((rows, LANES), f32),
        V((rows, D), bf16),
        V((rows, D), bf16),
        V((rows, D), bf16),
        V((G, TAPS * img, LANES), f32),
        V((slots, D, D), bf16),
        V((slots, D, D), bf16),
        V((slots, 8, D), f32),
        V((slots, rows, D), bf16),
        V((slots, rows, D), bf16),
        V((slots, 8, D), f32),
        V((G, rows, LANES), f32),
        V((G, 56, LANES), f32),
        V((5, G, 8, LANES), f32),
        V((slots, 2, D, D), bf16),
        V((slots, 2, D // 2, D), bf16),
        V((slots - 1, 2, D // 4, D), bf16),
        V((slots - 1, 2, D // 8, D), bf16),
        V((2, D // 2, D), bf16),
        V((slots - 2, 2, D // 8, D), bf16),
        V((extra, 2, D // 8 if n_dp > 8 else 16, D), bf16),
        V((2, D // 2, D), bf16),
        V((SMALL, D), f32),
        V((7, 8, D), f32),
        V((slots, 8, D), f32),
        V((extra, 8, D), f32),
        V((SMALL, D), f32),
        DMA((12,)),
        DMA((1 + G,)),
        DMA((slots, 2, 4)),
        DMA((slots, 2, 4)),
        DMA((slots,)),
        DMA((slots,)),
        DMA((slots, 2, 6)),
        DMA((slots, 2, 6)),
        DMA((extra, 2)),
        DMA((extra, 2)),
        DMA((4, 8)),
        DMA((4, 8)),
    ]
    block_out, input_grad, gr, ge, small = pl.pallas_call(
        functools.partial(kernel, n_dp, n_tensor),
        out_shape=[
            jax.ShapeDtypeStruct((rows, D), bf16),
            jax.ShapeDtypeStruct((rows, D), f32),
            jax.ShapeDtypeStruct((D, D), bf16),
            jax.ShapeDtypeStruct((D, D), bf16),
            jax.ShapeDtypeStruct((SMALL, D), f32),
        ],
        in_specs=[hbm] * 12,
        out_specs=[hbm] * 5,
        scratch_shapes=scratch,
        compiler_params=pltpu.CompilerParams(
            collective_id=0, has_side_effects=True, vmem_limit_bytes=63 << 20
        ),
        cost_estimate=pl.CostEstimate(
            flops=12 * rows * D * D * slots, bytes_accessed=20 * rows * D, transcendentals=0
        ),
    )(
        pixels,
        crop_sides,
        out_cotangent,
        depth_kernel,
        depth_bias,
        norm_gain,
        norm_shift,
        expand_weight,
        expand_bias,
        reduce_weight,
        reduce_bias,
        layer_scale,
    )
    vec = jax.ShapeDtypeStruct((D,), f32)
    square = jax.ShapeDtypeStruct((D, D), f32)
    return pl.pallas_call(
        hand_over,
        out_shape=[
            jax.ShapeDtypeStruct((rows, D), bf16),
            jax.ShapeDtypeStruct((rows, D), f32),
            jax.ShapeDtypeStruct((TAPS, D), f32),
            vec, vec, vec, square, vec, square, vec, vec,
        ],
        in_specs=[hbm, hbm, hbm, hbm, vmem],
        out_specs=[hbm, hbm, vmem, vmem, vmem, vmem, hbm, vmem, hbm, vmem, vmem],
        scratch_shapes=[
            V((2, D, D), bf16),
            V((2, D, D), f32),
            V((rows, D), f32),
            V((rows, D), bf16),
            DMA((4,)),
            DMA((4,)),
            DMA((2, 3)),
            DMA((2, 3)),
        ],
        compiler_params=pltpu.CompilerParams(vmem_limit_bytes=60 << 20),
    )(block_out, input_grad, gr, ge, small)


def solution(mesh):
    in_specs = (
        P(("dp", "tensor"), None),
        P(("dp", "tensor")),
        P(("dp", "tensor"), None),
        P(),
        P(),
        P(),
        P(),
        P(None, "tensor"),
        P("tensor"),
        P("tensor", None),
        P(),
        P(),
    )
    out_specs = (
        P(("dp", "tensor"), None),
        P(("dp", "tensor"), None),
        P(),
        P(),
        P(),
        P(),
        P(None, "tensor"),
        P("tensor"),
        P("tensor", None),
        P(),
        P(),
    )
    return jax.shard_map(
        functools.partial(per_device, mesh.shape["dp"], mesh.shape["tensor"]),
        mesh=mesh,
        in_specs=in_specs,
        out_specs=out_specs,
        check_vma=False,
    )
```

```python
import functools
import math
import jax
import jax.numpy as jnp
from jax import lax
from jax.experimental import pallas as pl
from jax.experimental.pallas import tpu as pltpu
from jax.sharding import PartitionSpec as P

KERNEL = 7
SIDE = 10
PLACES = SIDE * SIDE
TAPS = KERNEL * KERNEL
MARGIN = KERNEL // 2
LANES = 128
BLOCK = 256
norm_eps = 1e-06
f32 = jnp.float32
bf16 = jnp.bfloat16
MESH = pl.DeviceIdType.MESH
ROW_BIAS, ROW_GAIN, ROW_SHIFT, ROW_REDUCE, ROW_SCALE, ROW_EXPAND = 49, 50, 51, 52, 53, 54
SMALL = 64
PLAN = (
    "taps", "pix", "conv:0", "conv:1", "W1.1.0", "W1.2.0", "conv:2", "W1.1.1", "conv:3", "W2.1.0",
    "W1.2.1", "conv:4", "W2.1.1", "conv:5", "cot", "W3.1.0", "W1.3.0", "ln", "W2.2.1", "h:0:0",
    "h:0:1", "W2.2.0", "W1.3.1", "W3.1.1", "h:0:2", "h:0:3", "h:1:0", "h:1:1", "h:1:2", "h:1:3",
    "gr:1:0", "G0.1.0", "W2.3.0", "W3.2.1", "gr:1:1", "W3.2.0", "G1.1.0", "W2.3.1", "gr:0:0",
    "h:2:0", "h:2:1", "W3.3.0", "h:2:2", "G0.1.1", "h:2:3", "gr:2:1", "W3.3.1", "gr:2:0", "G1.1.1",
    "G0.2.0", "h:3:0", "h:3:1", "G0.2.1", "G1.2.0", "h:3:2", "h:3:3", "gr:3:0", "G1.2.1", "ncot",
    "G0.3.0", "G2.2.0", "G0.0.0", "gr:3:1", "G2.2.1", "gr:0:1", "G0.3.1", "G1.3.0", "lnb",
    "G1.0.0", "G3.2.1", "G3.2.0", "branch", "G2.3.0", "bout", "G0.0.1", "G2.0.0", "G1.3.1", "kg:0",
    "G3.3.0", "G1.0.1", "kg:1", "kg:2", "kg:3", "G2.3.1", "kg:4", "kg:5", "A0.0", "small", "S0",
    "G2.0.1", "G3.3.1", "convb:0", "A1.0", "convb:1", "S1", "A0.1", "convb:2", "convb:3", "A1.1",
    "S2", "convb:4", "A2.0", "convb:5", "S3", "A2.1",
)


def gelu_both(h):
    phi = 0.5 + 0.5 * lax.erf(h * math.sqrt(0.5))
    bell = jnp.exp2(h * h * (-0.5 * math.log2(math.e)))
    return h * phi, phi + h * (1.0 / math.sqrt(2.0 * math.pi)) * bell


def dot(a, b):
    return jnp.dot(a, b, preferred_element_type=f32)


def dot_rows(a, b):
    return lax.dot_general(a, b, (((0,), (0,)), ((), ())), preferred_element_type=f32)


def dot_t(a, b):
    return lax.dot_general(a, b, (((1,), (1,)), ((), ())), preferred_element_type=f32)


def kernel(
    n_dp,
    n_tensor,
    pix_hbm,
    side_hbm,
    cot_hbm,
    taps_hbm,
    depth_bias_hbm,
    gain_hbm,
    shift_hbm,
    we_hbm,
    eb_hbm,
    wr_hbm,
    rb_hbm,
    scale_hbm,
    out_hbm,
    in_grad_hbm,
    gr_hbm,
    ge_hbm,
    small_hbm,
    side_ref,
    taps_ref,
    depth_bias_ref,
    gain_ref,
    shift_ref,
    eb_ref,
    rb_ref,
    scale_ref,
    stage,
    X,
    XH,
    RSTD,
    NM,
    CM,
    BC,
    KB,
    WE,
    WR,
    EB,
    ACT,
    HC,
    EBG,
    NC,
    KG,
    ACC,
    GS,
    R0,
    R1,
    R2,
    RP,
    RZ,
    RX,
    OUTB,
    S,
    SR,
    SZ,
    SX,
    SALL,
    load_sem,
    out_sem,
    w_send,
    w_recv,
    e_send,
    e_recv,
    g_send,
    g_recv,
    x_send,
    x_recv,
    s_send,
    s_recv,
):
    D = NM.shape[1]
    G = D // LANES
    ROWS = NM.shape[0]
    IMG = ROWS // PLACES
    HALF, QUART, PIECE, BIT = D // 2, D // 4, D // 8, D // 16
    SLOTS = n_tensor
    extra = n_dp.bit_length() - 4
    dp = lax.axis_index("dp")
    tz = lax.axis_index("tensor")
    core = lax.rem(dp, 2)
    xb = lax.rem(lax.div(dp, 2), 2)
    yb = lax.rem(lax.div(dp, 4), 2)
    low = lax.rem(dp, 8)
    bits = (core, xb, yb)

    def flip(b):
        bit = bits[b] if b < 3 else lax.rem(lax.div(dp, 1 << b), 2)
        return dp + (1 - 2 * bit) * (1 << b)

    def flip_low(j):
        d = dp
        for b in range(3):
            if j >> b & 1:
                d = d + (1 - 2 * bits[b]) * (1 << b)
        return d


    t_low = lax.rem(tz, 2)
    t_high = lax.div(tz, 2)
    partner = tz + 1 - 2 * t_low
    middle = t_low + t_high - 2 * t_low * t_high
    across = 3 - tz

    def shard_of(s):
        return (tz, partner, 2 - t_high, 3 - 3 * t_high)[s]

    peers = [(flip_low(j), tz) for j in range(1, 8)]
    peers += [(dp, lax.rem(tz + o, n_tensor)) for o in range(1, n_tensor)]
    peers += [(flip(b), tz) for b in range(3, 3 + extra)]
    barrier = pltpu.get_barrier_semaphore()
    for peer in peers:
        pl.semaphore_signal(barrier, inc=1, device_id=peer, device_id_type=MESH)

    loads = [
        pltpu.make_async_copy(pix_hbm, NM, load_sem.at[0]),
        pltpu.make_async_copy(cot_hbm, BC, load_sem.at[1]),
        pltpu.make_async_copy(we_hbm, WE.at[0], load_sem.at[2]),
        pltpu.make_async_copy(wr_hbm, WR.at[0], load_sem.at[3]),
    ]
    rows_in = [
        (eb_hbm, eb_ref), (depth_bias_hbm, depth_bias_ref), (gain_hbm, gain_ref),
        (shift_hbm, shift_ref), (rb_hbm, rb_ref), (scale_hbm, scale_ref), (side_hbm, side_ref),
        (taps_hbm, taps_ref),
    ]
    rows_in = [pltpu.make_async_copy(a, b, load_sem.at[4 + i]) for i, (a, b) in enumerate(rows_in)]
    for copy in rows_in + loads:
        copy.start()

    def vector(ref):
        return ref[...].astype(f32).reshape(1, D)

    def remote(src, dst, send, recv, device):
        return pltpu.make_async_remote_copy(
            src_ref=src, dst_ref=dst, send_sem=send, recv_sem=recv,
            device_id=device, device_id_type=MESH,
        )

    PARTS = (0, 1)
    first = (xb, yb)
    second = (yb, xb)
    first_peer = (flip(1), flip(2))
    second_peer = (flip(2), flip(1))
    W = (WE, WR)
    core_half = pl.ds(pl.multiple_of(core * HALF, 16), HALF)

    def w_rows(h, level):
        start = core * HALF + h * QUART + second[h] * PIECE
        if level <= 1:
            start = start + first[h] * BIT
        return pl.ds(pl.multiple_of(start, 16), (BIT, BIT, PIECE)[level])

    def w_copy(s, m, level, h=0):
        if level == 3:
            here, device, i = W[m].at[s, core_half, :], flip(0), 6
        else:
            here = W[m].at[s, w_rows(h, level), :]
            device, i = (first_peer[h], second_peer[h])[level - 1], 2 * level + h
        return remote(here, here, w_send.at[s, m, i], w_recv.at[s, m, i], (device, tz))

    def z_piece(m, h, source, slot, device):
        rows = w_rows(h, 0)
        src = (we_hbm, wr_hbm)[m].at[rows, :] if source == 0 else W[m].at[source, rows, :]
        send = w_send.at[0, m, 2 * slot + h] if source == 0 else w_send.at[source, m, h]
        return remote(src, W[m].at[slot, rows, :], send, w_recv.at[slot, m, h], (dp, device))

    def own_pieces(m, h):
        return z_piece(m, h, 0, 1, partner), z_piece(m, h, 0, 2, across)

    def relay(s, m, h):
        return z_piece(m, h, 1, 3, across) if s == 1 else z_piece(m, h, s, s, partner)

    def in_middle(act):
        @pl.when(middle == 1)
        def _():
            act()

    def e_copy(o):
        own = EB.at[tz]
        return remote(own, own, e_send.at[o], e_recv.at[tz], (dp, lax.rem(tz + o, n_tensor)))

    def e_arrival(s):
        there = EB.at[shard_of(s)]
        return remote(there, there, e_send.at[s], e_recv.at[shard_of(s)], (dp, partner))

    def w_step(level, s, m):
        if level == 0:
            for h in PARTS:
                own_pieces(m, h)[0].start()
            for h in PARTS:
                in_middle(own_pieces(m, h)[1].start)
        elif level == 1:
            for h in PARTS:
                z_piece(m, h, 0, s, partner).wait_recv()
                w_copy(s, m, 1, h).start()
                in_middle(relay(s, m, h).start)
        elif level == 2:
            for h in PARTS:
                w_copy(s, m, 1, h).wait_recv()
                w_copy(s, m, 2, h).start()
        elif level == 3:
            for h in PARTS:
                w_copy(s, m, 2, h).wait_recv()
            w_copy(s, m, 3).start()
        else:
            w_copy(s, m, 3).wait_recv()

    pl.semaphore_wait(barrier, len(peers))
    for m in range(2):
        w_step(0, 0, m)
    for copy in rows_in:
        copy.wait()
    EB[tz] = jnp.broadcast_to(vector(eb_ref), (8, D))
    for o in range(1, n_tensor):
        e_copy(o).start()

    def g_start(h, level):
        start = core * HALF + h * QUART
        if level >= 1:
            start = start + first[h] * PIECE
        if level >= 2:
            start = start + second[h] * BIT
        return start

    PLANE = {0: 0, 2: 1, 3: 2}

    def g_copy(s, m, level, h=0):
        if level == 0:
            start, size, peer, dst, i = (1 - core) * HALF, HALF, flip(0), R0.at[s, m], 0
        elif level == 1:
            start = g_start(h, 0) + (1 - first[h]) * PIECE
            size, peer, dst, i = PIECE, first_peer[h], R1.at[PLANE[s], m, h], 1 + h
        else:
            start = g_start(h, 1) + (1 - second[h]) * BIT
            size, peer, dst, i = BIT, second_peer[h], R2.at[PLANE[s], m, h], 3 + h
        src = GS.at[s, m, pl.ds(pl.multiple_of(start, 16), size), :]
        return remote(src, dst, g_send.at[s, m, i], g_recv.at[s, m, i], (peer, tz))

    def p_copy(m):
        src = GS.at[1, m, core_half, :]
        return remote(src, RP.at[m], g_send.at[1, m, 1], g_recv.at[1, m, 1], (dp, partner))

    def z_copy(s, m, h):
        src = GS.at[s, m, pl.ds(pl.multiple_of(g_start(h, 2), 16), BIT), :]
        slot = 3 - middle
        return remote(
            src, RZ.at[slot - 2, m, h], g_send.at[s, m, 5 + h], g_recv.at[slot, m, 5 + h],
            (dp, shard_of(s)),
        )

    def z_arrival(s, m, h):
        src = GS.at[s, m, pl.ds(pl.multiple_of(g_start(h, 2), 16), BIT), :]
        return remote(
            src, RZ.at[s - 2, m, h], g_send.at[s, m, 5 + h], g_recv.at[s, m, 5 + h], (dp, partner)
        )

    def add_rows(s, m, start, size, got):
        def add(i, c):
            rows = pl.ds(pl.multiple_of(start + i * 16, 16), 16)
            mine = pl.ds(pl.multiple_of(i * 16, 16), 16)
            total = GS[s, m, rows, :].astype(f32)
            for ref in got:
                total = total + ref[mine, :].astype(f32)
            GS[s, m, rows, :] = total.astype(bf16)
            return c

        lax.fori_loop(0, size // 16, add, 0, unroll=3)

    def g_step(level, s, m):
        if level == 0:
            g_copy(s, m, 0).start()
        elif level == 1:
            g_copy(s, m, 0).wait_recv()
            got = [R0.at[s, m]]
            if s == 0:
                p_copy(m).wait_recv()
                got.append(RP.at[m])
            if s == 1:
                add_rows(s, m, core * HALF, HALF, got)
                p_copy(m).start()
            else:
                for h in PARTS:
                    for side in range(2):
                        bit = 1 - first[h] if side == 0 else first[h]
                        at = h * QUART + bit * PIECE
                        add_rows(
                            s, m, core * HALF + at, PIECE,
                            [ref.at[pl.ds(pl.multiple_of(at, 16), PIECE), :] for ref in got],
                        )
                        if side == 0:
                            g_copy(s, m, 1, h).start()
        elif level == 2:
            for h in PARTS:
                g_copy(s, m, 1, h).wait_recv()
                add_rows(s, m, g_start(h, 1), PIECE, [R1.at[PLANE[s], m, h]])
                g_copy(s, m, 2, h).start()
        else:
            for h in PARTS:
                g_copy(s, m, 2, h).wait_recv()
                add_rows(s, m, g_start(h, 2), BIT, [R2.at[PLANE[s], m, h]])
                if s > 0:
                    z_copy(s, m, h).start()

    def o_rows(h, level):
        start = h * QUART + first[h] * PIECE
        if level == 0:
            start = start + second[h] * BIT
        return pl.ds(pl.multiple_of(start, 16), (BIT, PIECE)[level])

    def a_copy(m, level, h=0):
        if level == 2:
            here, there = OUTB.at[m], (gr_hbm, ge_hbm)[m].at[core_half, :]
            peer, i = flip(0), 11
        else:
            here = there = OUTB.at[m, o_rows(h, level), :]
            peer, i = (second_peer[h], first_peer[h])[level], 7 + 2 * level + h
        return remote(here, there, g_send.at[0, m, i], g_recv.at[0, m, i], (peer, tz))

    def own_half(m):
        return pltpu.make_async_copy(
            OUTB.at[m], (gr_hbm, ge_hbm)[m].at[core_half, :], load_sem.at[m]
        )

    def x_copy(m, b, h):
        here = OUTB.at[m, o_rows(h, 0), :]
        return remote(
            here, RX.at[b - 3, m, h], x_send.at[b - 3, m, h], x_recv.at[b - 3, m, h], (flip(b), tz)
        )

    def finish_sum(m, h):
        for s in range(2, SLOTS):
            z_arrival(s, m, h).wait_recv()
        start = g_start(h, 2)
        there = start - core * HALF

        def add(i, c):
            rows = pl.ds(pl.multiple_of(start + i * 16, 16), 16)
            own = pl.ds(pl.multiple_of(i * 16, 16), 16)
            total = GS[0, m, rows, :].astype(f32)
            for s in range(2, SLOTS):
                total = total + RZ[s - 2, m, h, own, :].astype(f32)
            OUTB[m, pl.ds(pl.multiple_of(there + i * 16, 16), 16), :] = total.astype(bf16)
            return c

        lax.fori_loop(0, BIT // 16, add, 0)
        for b in range(3, 3 + extra):
            x_copy(m, b, h).start()
            x_copy(m, b, h).wait()

            def add_x(i, c):
                rows = pl.ds(pl.multiple_of(there + i * 16, 16), 16)
                OUTB[m, rows, :] = (
                    OUTB[m, rows, :] + RX[b - 3, m, h, pl.ds(pl.multiple_of(i * 16, 16), 16), :]
                )
                return c

            lax.fori_loop(0, BIT // 16, add_x, 0)

    def a_step(level, m):
        if level == 0:
            g_step(3, 0, m)
            for h in PARTS:
                finish_sum(m, h)
                a_copy(m, 0, h).start()
        elif level == 1:
            for h in PARTS:
                a_copy(m, 0, h).wait_recv()
                a_copy(m, 1, h).start()
        elif level == 2:
            for h in PARTS:
                a_copy(m, 1, h).wait_recv()
            a_copy(m, 2).start()
            own_half(m).start()
        else:
            a_copy(m, 2).wait_recv()

    def sr_copy(j):
        dst_low = flip_low(j)
        rows = pl.ds(pl.multiple_of(lax.rem(dst_low, 8) * 8, 8), 8)
        return remote(S.at[rows, :], SR.at[j - 1], s_send.at[0, j], s_recv.at[0, j], (dst_low, tz))

    def sz_copy(o):
        return remote(
            SZ.at[tz], SZ.at[tz], s_send.at[1, o], s_recv.at[1, o],
            (dp, lax.rem(tz + o, n_tensor)),
        )

    own_small = pl.ds(pl.multiple_of(low * 8, 8), 8)

    def sa_copy(j):
        here = SALL.at[own_small, :]
        return remote(here, here, s_send.at[2, j], s_recv.at[2, j], (flip_low(j), tz))

    def sx_copy(b):
        return remote(
            SALL.at[own_small, :], SX.at[b - 3], s_send.at[3, b], s_recv.at[3, b], (flip(b), tz)
        )

    def small_step(level):
        if level == 0:
            for j in range(1, 8):
                sr_copy(j).start()
        elif level == 1:
            total = S[own_small, :]
            for j in range(1, 8):
                sr_copy(j).wait_recv()
                total = total + SR[j - 1]
            SZ[tz] = total
            for o in range(1, n_tensor):
                sz_copy(o).start()
        elif level == 2:
            for o in range(1, n_tensor):
                sz_copy(o).wait_recv()
            total = SZ[0]
            for o in range(1, n_tensor):
                total = total + SZ[o]
            SALL[own_small, :] = total
            for b in range(3, 3 + extra):
                sx_copy(b).start()
                sx_copy(b).wait()
                SALL[own_small, :] = SALL[own_small, :] + SX[b - 3]
            for j in range(1, 8):
                sa_copy(j).start()
        else:
            for j in range(1, 8):
                sa_copy(j).wait_recv()

    row = lax.broadcasted_iota(jnp.int32, (IMG, LANES), 0)
    sides = jnp.zeros((IMG, LANES), jnp.int32)
    for i in range(IMG):
        sides = jnp.where(row == i, side_ref[i], sides)

    def mask_at(p):
        if isinstance(p, int):
            return jnp.where(sides > max(p // SIDE, p % SIDE), 1.0, 0.0)
        return jnp.where(sides > jnp.maximum(lax.div(p, SIDE), lax.rem(p, SIDE)), 1.0, 0.0)

    def lanes(g):
        return slice(g * LANES, (g + 1) * LANES)

    def place(p):
        return pl.ds(p * IMG, IMG)

    def spread(src):
        def body(i, c):
            rows = pl.ds(pl.multiple_of(i * 80, 16), 80)
            for g in range(G):
                stage[g, rows, :] = src[rows, lanes(g)].astype(f32)
            return c

        lax.fori_loop(0, ROWS // 80, body, 0)

    def load_pixels():
        def body(p, c):
            m = mask_at(p)
            rows = pl.ds(pl.multiple_of(p * IMG, IMG), IMG)
            for g in range(G):
                X[g, rows, :] = stage[g, pl.ds(p, IMG, stride=PLACES), :] * m
            return c

        lax.fori_loop(0, PLACES, body, 0, unroll=2)

    def load_cot():
        scale = vector(scale_ref)

        def body(q, sums):
            sums = list(sums)
            masks = [mask_at(2 * q + u) for u in range(2)]
            rows = pl.ds(pl.multiple_of(q * 2 * IMG, 2 * IMG), 2 * IMG)
            for g in range(G):
                c = [stage[g, pl.ds(2 * q + u, IMG, stride=PLACES), :] * masks[u] for u in range(2)]
                c = jnp.concatenate(c, axis=0)
                CM[rows, lanes(g)] = c.astype(bf16)
                b = (c * scale[:, lanes(g)]).astype(bf16)
                BC[rows, lanes(g)] = b
                b = b.astype(f32)
                sums[g] = sums[g] + (b[:IMG] + b[IMG:])
            return tuple(sums)

        zero = jnp.zeros((IMG, LANES), f32)
        sums = lax.fori_loop(0, PLACES // 2, body, (zero,) * G)
        for g in range(G):
            ACC[3, g] = sums[g]

    def load_taps():
        for g in range(G):
            for t in range(TAPS):
                KB[g, place(t), :] = jnp.broadcast_to(
                    taps_ref[t : t + 1, lanes(g)].astype(f32), (IMG, LANES)
                )

    def conv(src, dst, bias, flipped, post, between):
        def one(g, carry):
            for r in range(SIDE):
                acc = [None] * SIDE if bias is None else [bias[g]] * SIDE
                for rr in range(max(0, r - MARGIN), min(SIDE, r + MARGIN + 1)):
                    xs = [src[g, place(rr * SIDE + c), :] for c in range(SIDE)]
                    for dc in range(KERNEL):
                        t = (rr - r + MARGIN) * KERNEL + dc
                        k = KB[g, place(TAPS - 1 - t if flipped else t), :]
                        for c in range(SIDE):
                            cc = c + dc - MARGIN
                            if 0 <= cc < SIDE:
                                v = xs[cc] * k
                                acc[c] = v if acc[c] is None else acc[c] + v
                if post is None:
                    for c in range(SIDE):
                        dst[g, place(r * SIDE + c), :] = acc[c]
                else:
                    post(g, r, acc)
            between(g)
            return carry

        lax.fori_loop(0, G, one, 0)

    def tree(parts):
        parts = list(parts)
        while len(parts) > 1:
            parts = [
                parts[i] + parts[i + 1] if i + 1 < len(parts) else parts[i]
                for i in range(0, len(parts), 2)
            ]
        return parts[0]

    def fold(v):
        return tree(v[i : i + 8] for i in range(0, v.shape[0], 8))

    def layernorm():
        gain = vector(gain_ref)
        shift = vector(shift_ref)

        def body(q, c):
            rows = pl.ds(pl.multiple_of(q * 32, 32), 32)
            v = [XH[g, rows, :] for g in range(G)]
            mean = jnp.sum(tree(v), axis=1, keepdims=True) * (1.0 / D)
            v = [a - mean for a in v]
            total = tree([a * a for a in v])
            rstd = lax.rsqrt(jnp.sum(total, axis=1, keepdims=True) * (1.0 / D) + norm_eps)
            RSTD[rows, :] = jnp.broadcast_to(rstd, (32, LANES))
            for g in range(G):
                xh = v[g] * rstd
                XH[g, rows, :] = xh
                NM[rows, lanes(g)] = (xh * gain[:, lanes(g)] + shift[:, lanes(g)]).astype(bf16)
            return c

        lax.fori_loop(0, ROWS // 32, body, 0, unroll=5)

    def layernorm_back():
        gain = vector(gain_ref)

        def body(q, sums):
            rows = pl.ds(pl.multiple_of(q * 160, 32), 160)
            rstd = RSTD[rows, :]
            xh = [XH[g, rows, :] for g in range(G)]
            nc = [NC[g, rows, :] for g in range(G)]
            d = [nc[g] * gain[:, lanes(g)] for g in range(G)]
            m1 = jnp.sum(tree(d), axis=1, keepdims=True) * (1.0 / D)
            m2 = jnp.sum(tree([a * b for a, b in zip(d, xh)]), axis=1, keepdims=True) * (1.0 / D)
            out = []
            for g in range(G):
                dm = rstd * (d[g] - m1 - xh[g] * m2)
                NC[g, rows, :] = dm
                old = sums[g]
                out.append((old[0] + fold(nc[g] * xh[g]), old[1] + fold(nc[g]), old[2] + fold(dm)))
            return tuple(out)

        zero = jnp.zeros((8, LANES), f32)
        sums = lax.fori_loop(0, ROWS // 160, body, ((zero, zero, zero),) * G)
        for i in range(3):
            for g in range(G):
                ACC[i, g] = sums[g][i]

    def kernel_grad(between):
        def one(g, carry):
            for dr in range(KERNEL):
                acc = [[None, None] for _ in range(KERNEL)]
                for r in range(SIDE):
                    rr = r + dr - MARGIN
                    if not 0 <= rr < SIDE:
                        continue
                    ds = [NC[g, place(r * SIDE + c), :] for c in range(SIDE)]
                    xs = [X[g, place(rr * SIDE + c), :] for c in range(SIDE)]
                    for dc in range(KERNEL):
                        a = acc[dc]
                        for c in range(SIDE):
                            cc = c + dc - MARGIN
                            if 0 <= cc < SIDE:
                                v = ds[c] * xs[cc]
                                a[c % 2] = v if a[c % 2] is None else a[c % 2] + v
                for dc in range(KERNEL):
                    t = dr * KERNEL + dc
                    KG[g, t : t + 1, :] = jnp.sum(acc[dc][0] + acc[dc][1], axis=0, keepdims=True)
            between(g)
            return carry

        lax.fori_loop(0, G, one, 0)

    def hidden_block(s, j):
        if j < D // BLOCK:
            cols = slice(j * BLOCK, (j + 1) * BLOCK)
            base = j % 2 * 4
            h = dot(NM[...], WE[s, :, cols])
            stage[base] = h[:, :LANES]
            stage[base + 1] = h[:, LANES:]
            a = dot_t(BC[...], WR[s, cols, :])
            stage[base + 2] = a[:, :LANES]
            stage[base + 3] = a[:, LANES:]
        if j > 0:
            base = (j - 1) % 2 * 4
            for u in range(2):
                mine = slice((j - 1) * BLOCK + u * LANES, (j - 1) * BLOCK + (u + 1) * LANES)
                bias = EB[shard_of(s), :, mine]
                bias = jnp.concatenate([bias, bias], axis=0)
                total = None
                for i in range(ROWS // 16):
                    rows = slice(i * 16, (i + 1) * 16)
                    value, slope = gelu_both(stage[base + u, rows, :] + bias)
                    ACT[s, rows, mine] = value.astype(bf16)
                    w = (stage[base + 2 + u, rows, :] * slope).astype(bf16)
                    HC[s, rows, mine] = w
                    w = w.astype(f32)
                    w = w[:8] + w[8:]
                    total = w if total is None else total + w
                EBG[s, :, mine] = total

    def grad_block(s, m):
        for j in range(D // BLOCK):
            cols = slice(j * BLOCK, (j + 1) * BLOCK)
            if m == 0:
                GS[s, 0, cols, :] = dot_rows(ACT[s, :, cols], BC[...]).astype(bf16)
            else:
                GS[s, 1, :, cols] = dot_rows(NM[...], HC[s, :, cols]).astype(bf16)

    def back_to_normed():
        for n in range(D // BLOCK):
            cols = slice(n * BLOCK, (n + 1) * BLOCK)
            total = dot_t(HC[0], WE[0, cols, :])
            for s in range(1, SLOTS):
                total = total + dot_t(HC[s], WE[s, cols, :])
            NC[2 * n] = total[:, :LANES]
            NC[2 * n + 1] = total[:, LANES:]

    def to_branch():
        for n in range(D // BLOCK):
            cols = slice(n * BLOCK, (n + 1) * BLOCK)
            total = dot(ACT[0], WR[0, :, cols])
            for s in range(1, SLOTS):
                total = total + dot(ACT[s], WR[s, :, cols])
            XH[2 * n] = total[:, :LANES]
            XH[2 * n + 1] = total[:, LANES:]

    def block_output():
        scale = vector(scale_ref)
        shift = vector(rb_ref)

        def body(q, sums):
            sums = list(sums)
            rows = pl.ds(pl.multiple_of(q * 2 * IMG, 2 * IMG), 2 * IMG)
            masks = jnp.concatenate([mask_at(2 * q + u) for u in range(2)], axis=0)
            for g in range(G):
                branch = XH[g, rows, :] + shift[:, lanes(g)]
                v = CM[rows, lanes(g)].astype(f32) * branch
                sums[g] = sums[g] + (v[:IMG] + v[IMG:])
                value = X[g, rows, :] + masks * (scale[:, lanes(g)] * branch)
                for u in range(2):
                    stage[g, pl.ds(2 * q + u, IMG, stride=PLACES), :] = value[u * IMG : (u + 1) * IMG]
            return tuple(sums)

        zero = jnp.zeros((IMG, LANES), f32)
        sums = lax.fori_loop(0, PLACES // 2, body, (zero,) * G)
        for g in range(G):
            ACC[4, g] = sums[g]

        def narrow(i, c):
            rows = pl.ds(pl.multiple_of(i * 80, 16), 80)
            for g in range(G):
                NM[rows, lanes(g)] = stage[g, rows, :].astype(bf16)
            return c

        lax.fori_loop(0, ROWS // 80, narrow, 0)

    def small_sums():
        S[...] = jnp.zeros_like(S)
        for g in range(G):
            S[:TAPS, lanes(g)] = KG[g, :TAPS, :]
            for r, i in ((ROW_BIAS, 2), (ROW_GAIN, 0), (ROW_SHIFT, 1), (ROW_REDUCE, 3), (ROW_SCALE, 4)):
                S[r : r + 1, lanes(g)] = jnp.sum(ACC[i, g], axis=0, keepdims=True)
        for s in range(SLOTS):
            r = ROW_EXPAND + shard_of(s)
            S[pl.ds(r, 1), :] = jnp.sum(EBG[s], axis=0, keepdims=True)

    def tell(name):
        kind, _, rest = name.partition(".")
        where = [int(v) for v in rest.split(".")] if rest else []
        if kind[0] == "W":
            w_step(int(kind[1]), *where)
        elif kind[0] == "G":
            g_step(int(kind[1]), *where)
        elif kind[0] == "A":
            a_step(int(kind[1]), *where)
        else:
            small_step(int(kind[1]))

    loads[0].wait()
    biases = vector(depth_bias_ref)
    for g in range(G):
        ACC[0, g] = jnp.broadcast_to(biases[:, lanes(g)], (8, LANES))

    def finish_input(g, r, acc):
        cols = pl.ds(pl.multiple_of(g * LANES, LANES), LANES)
        for c in range(0, SIDE, 2):
            p = r * SIDE + c
            cot = CM[pl.ds(p * IMG, 2 * IMG), cols].astype(f32)
            for u in range(2):
                XH[g, pl.ds(p + u, IMG, stride=PLACES), :] = (
                    acc[c + u] * mask_at(p + u) + cot[u * IMG : (u + 1) * IMG]
                )

    def out_copy(g):
        return pltpu.make_async_copy(
            XH.at[g], in_grad_hbm.at[:, pl.ds(pl.multiple_of(g * LANES, LANES), LANES)], out_sem.at[1 + g]
        )

    def over_groups(names, call):
        kind = names[0].partition(":")[0]
        after = {}
        group = 0
        for name in names:
            if name.startswith(kind + ":"):
                group = int(name.partition(":")[2])
            else:
                after.setdefault(group, []).append(name)

        def between(g):
            if kind == "convb":
                out_copy(g).start()
            for i, told in after.items():
                @pl.when(g == i)
                def _():
                    for name in told:
                        tell(name)

        call(between)

    looped = {
        "conv": lambda between: conv(X, XH, ACC.at[0], False, None, between),
        "kg": kernel_grad,
        "convb": lambda between: conv(NC, None, None, True, finish_input, between),
    }

    def start_output():
        block_output()
        pltpu.make_async_copy(NM, out_hbm, out_sem.at[0]).start()

    def pixels_in():
        spread(NM)
        load_pixels()

    def cot_in():
        loads[1].wait()
        spread(BC)
        load_cot()

    def linears_ready(s):
        if s == 0:
            loads[2].wait()
            loads[3].wait()
        else:
            for m in range(2):
                w_step(4, s, m)
            e_arrival(s).wait_recv()

    def step(name):
        kind, _, rest = name.partition(":")
        where = [int(v) for v in rest.split(":")] if rest else []
        if "." in name or kind[0] == "S":
            tell(name)
        elif kind == "h":
            if where[1] == 0:
                linears_ready(where[0])
            hidden_block(*where)
        elif kind == "gr":
            grad_block(*where)
        else:
            {
                "pix": pixels_in,
                "taps": load_taps,
                "cot": cot_in,
                "ln": layernorm,
                "lnb": layernorm_back,
                "ncot": back_to_normed,
                "branch": to_branch,
                "bout": start_output,
                "small": small_sums,
            }[kind]()

    at = 0
    while at < len(PLAN):
        kind = PLAN[at].partition(":")[0]
        if kind in looped:
            last = max(i for i, name in enumerate(PLAN) if name.startswith(kind + ":"))
            over_groups(PLAN[at : last + 1], looped[kind])
            at = last + 1
        else:
            step(PLAN[at])
            at += 1
    tail = [
        pltpu.make_async_copy(SALL, small_hbm, load_sem.at[2]),
    ]
    for copy in tail:
        copy.start()
    for m in range(2):
        a_step(3, m)
    for s in range(1, SLOTS):
        e_copy(s).wait_send()
    for m in range(2):
        for h in PARTS:
            own_pieces(m, h)[0].wait_send()
            in_middle(own_pieces(m, h)[1].wait_send)
            for s in range(1, SLOTS):
                in_middle(relay(s, m, h).wait_send)
                for level in (1, 2):
                    w_copy(s, m, level, h).wait_send()
            for s in PLANE:
                for level in (1, 2):
                    g_copy(s, m, level, h).wait_send()
                if s > 0:
                    z_copy(s, m, h).wait_send()
            for level in range(2):
                a_copy(m, level, h).wait_send()
        for s in range(SLOTS):
            if s > 0:
                w_copy(s, m, 3).wait_send()
            g_copy(s, m, 0).wait_send()
        p_copy(m).wait_send()
        a_copy(m, 2).wait_send()
    for j in range(1, 8):
        sr_copy(j).wait_send()
        sa_copy(j).wait_send()
    for o in range(1, n_tensor):
        sz_copy(o).wait_send()
    pltpu.make_async_copy(NM, out_hbm, out_sem.at[0]).wait()
    for g in range(G):
        out_copy(g).wait()
    for copy in tail:
        copy.wait()
    for m in range(2):
        own_half(m).wait()


def hand_over(
    out_in, grad_in, gr, ge, small,
    block_out, input_grad, kernel_grad, bias_grad, gain_grad, shift_grad,
    expand_grad, expand_bias_grad, reduce_grad, reduce_bias_grad, scale_grad,
    narrow, wide, grad_rows, out_rows, sums, taps, *rest,
):
    vectors, (there_sem, back_sem, in_sem, out_sem, small_sem) = rest[:6], rest[6:]
    D = gr.shape[0]
    third = D // 3
    half = out_in.shape[0] // 2
    halves = [
        (held.at[pl.ds(i * half, half)], src.at[pl.ds(i * half, half)], dst.at[pl.ds(i * half, half)])
        for i in range(2)
        for held, src, dst in ((grad_rows, grad_in, input_grad), (out_rows, out_in, block_out))
    ]
    there = [pltpu.make_async_copy(v[1], v[0], there_sem.at[i]) for i, v in enumerate(halves)]
    back = [pltpu.make_async_copy(v[0], v[2], back_sem.at[i]) for i, v in enumerate(halves)]
    parts = [(i, m) for i in range(3) for m in range(2)]

    def rows(i):
        return pl.ds(i * third, third)

    reads = {
        (i, m): pltpu.make_async_copy((gr, ge)[m].at[rows(i)], narrow.at[m, rows(i)], in_sem.at[m, i])
        for i, m in parts
    }
    writes = {
        (i, m): pltpu.make_async_copy(
            wide.at[m, rows(i)], (reduce_grad, expand_grad)[m].at[rows(i)], out_sem.at[m, i]
        )
        for i, m in parts
    }
    load = pltpu.make_async_copy(small, sums, small_sem.at[0])
    load.start()
    for part in parts:
        reads[part].start()
    load.wait()
    taps[...] = sums[:TAPS, :]
    own = ROW_EXPAND + lax.axis_index("tensor")
    given = [pltpu.make_async_copy(taps, kernel_grad, small_sem.at[0])]
    for i, (row, ref) in enumerate((
        (ROW_BIAS, bias_grad), (ROW_GAIN, gain_grad), (ROW_SHIFT, shift_grad),
        (ROW_REDUCE, reduce_bias_grad), (ROW_SCALE, scale_grad), (own, expand_bias_grad),
    )):
        vectors[i][...] = sums[pl.ds(row, 1), :].reshape(D)
        given.append(pltpu.make_async_copy(vectors[i], ref, small_sem.at[1 + i]))
    for i, m in parts:
        reads[i, m].wait()
        if i == 0 and m == 0:
            for copy in there:
                copy.start()

        def widen(k, c):
            at = pl.ds(pl.multiple_of(i * third + k * 32, 32), 32)
            wide[m, at, :] = narrow[m, at, :].astype(f32)
            return c

        lax.fori_loop(0, third // 32, widen, 0)
        writes[i, m].start()
    for arrived, copy in zip(there, back):
        arrived.wait()
        copy.start()
    for copy in given:
        copy.start()
    for part in parts:
        writes[part].wait()
    for copy in back + given:
        copy.wait()


def per_device(
    n_dp,
    n_tensor,
    pixels,
    crop_sides,
    out_cotangent,
    depth_kernel,
    depth_bias,
    norm_gain,
    norm_shift,
    expand_weight,
    expand_bias,
    reduce_weight,
    reduce_bias,
    layer_scale,
):
    rows, D = pixels.shape
    G = D // LANES
    img = rows // PLACES
    slots = n_tensor
    extra = max(n_dp.bit_length() - 4, 1)
    hbm = pl.BlockSpec(memory_space=pltpu.HBM)
    V = pltpu.VMEM
    DMA = pltpu.SemaphoreType.DMA
    scratch = [pltpu.SMEM((img,), jnp.int32), V((TAPS, D), bf16)] + [V((D,), bf16) for _ in range(6)] + [
        V((8, rows, LANES), f32),
        V((G, rows, LANES), f32),
        V((G, rows, LANES), f32),
        V((rows, LANES), f32),
        V((rows, D), bf16),
        V((rows, D), bf16),
        V((rows, D), bf16),
        V((G, TAPS * img, LANES), f32),
        V((slots, D, D), bf16),
        V((slots, D, D), bf16),
        V((slots, 8, D), f32),
        V((slots, rows, D), bf16),
        V((slots, rows, D), bf16),
        V((slots, 8, D), f32),
        V((G, rows, LANES), f32),
        V((G, 56, LANES), f32),
        V((5, G, 8, LANES), f32),
        V((slots, 2, D, D), bf16),
        V((slots, 2, D // 2, D), bf16),
        V((slots - 1, 2, 2, D // 8, D), bf16),
        V((slots - 1, 2, 2, D // 16, D), bf16),
        V((2, D // 2, D), bf16),
        V((slots - 2, 2, 2, D // 16, D), bf16),
        V((extra, 2, 2, D // 16 if n_dp > 8 else 16, D), bf16),
        V((2, D // 2, D), bf16),
        V((SMALL, D), f32),
        V((7, 8, D), f32),
        V((slots, 8, D), f32),
        V((extra, 8, D), f32),
        V((SMALL, D), f32),
        DMA((12,)),
        DMA((1 + G,)),
        DMA((slots, 2, 8)),
        DMA((slots, 2, 8)),
        DMA((slots,)),
        DMA((slots,)),
        DMA((slots, 2, 12)),
        DMA((slots, 2, 12)),
        DMA((extra, 2, 2)),
        DMA((extra, 2, 2)),
        DMA((4, 8)),
        DMA((4, 8)),
    ]
    block_out, input_grad, gr, ge, small = pl.pallas_call(
        functools.partial(kernel, n_dp, n_tensor),
        out_shape=[
            jax.ShapeDtypeStruct((rows, D), bf16),
            jax.ShapeDtypeStruct((rows, D), f32),
            jax.ShapeDtypeStruct((D, D), bf16),
            jax.ShapeDtypeStruct((D, D), bf16),
            jax.ShapeDtypeStruct((SMALL, D), f32),
        ],
        in_specs=[hbm] * 12,
        out_specs=[hbm] * 5,
        scratch_shapes=scratch,
        compiler_params=pltpu.CompilerParams(
            collective_id=0, has_side_effects=True, vmem_limit_bytes=63 << 20
        ),
        cost_estimate=pl.CostEstimate(
            flops=12 * rows * D * D * slots, bytes_accessed=20 * rows * D, transcendentals=0
        ),
    )(
        pixels,
        crop_sides,
        out_cotangent,
        depth_kernel,
        depth_bias,
        norm_gain,
        norm_shift,
        expand_weight,
        expand_bias,
        reduce_weight,
        reduce_bias,
        layer_scale,
    )
    vec = jax.ShapeDtypeStruct((D,), f32)
    square = jax.ShapeDtypeStruct((D, D), f32)
    return pl.pallas_call(
        hand_over,
        out_shape=[
            jax.ShapeDtypeStruct((rows, D), bf16),
            jax.ShapeDtypeStruct((rows, D), f32),
            jax.ShapeDtypeStruct((TAPS, D), f32),
            vec, vec, vec, square, vec, square, vec, vec,
        ],
        in_specs=[hbm] * 5,
        out_specs=[hbm] * 11,
        scratch_shapes=[
            V((2, D, D), bf16),
            V((2, D, D), f32),
            V((rows, D), f32),
            V((rows, D), bf16),
            V((SMALL, D), f32),
            V((TAPS, D), f32),
            *[V((D,), f32) for _ in range(6)],
            DMA((4,)),
            DMA((4,)),
            DMA((2, 3)),
            DMA((2, 3)),
            DMA((7,)),
        ],
        compiler_params=pltpu.CompilerParams(vmem_limit_bytes=60 << 20),
    )(block_out, input_grad, gr, ge, small)


def solution(mesh):
    in_specs = (
        P(("dp", "tensor"), None),
        P(("dp", "tensor")),
        P(("dp", "tensor"), None),
        P(),
        P(),
        P(),
        P(),
        P(None, "tensor"),
        P("tensor"),
        P("tensor", None),
        P(),
        P(),
    )
    out_specs = (
        P(("dp", "tensor"), None),
        P(("dp", "tensor"), None),
        P(),
        P(),
        P(),
        P(),
        P(None, "tensor"),
        P("tensor"),
        P("tensor", None),
        P(),
        P(),
    )
    return jax.shard_map(
        functools.partial(per_device, mesh.shape["dp"], mesh.shape["tensor"]),
        mesh=mesh,
        in_specs=in_specs,
        out_specs=out_specs,
        check_vma=False,
    )
```

```python
import functools
import math
import jax
import jax.numpy as jnp
from jax import lax
from jax.experimental import pallas as pl
from jax.experimental.pallas import tpu as pltpu
from jax.sharding import PartitionSpec as P

KERNEL = 7
SIDE = 10
PLACES = SIDE * SIDE
TAPS = KERNEL * KERNEL
MARGIN = KERNEL // 2
LANES = 128
BLOCK = 256
norm_eps = 1e-06
f32 = jnp.float32
bf16 = jnp.bfloat16
MESH = pl.DeviceIdType.MESH
ROW_BIAS, ROW_GAIN, ROW_SHIFT, ROW_REDUCE, ROW_SCALE, ROW_EXPAND = 49, 50, 51, 52, 53, 54
SMALL = 64
PLAN = (
    "taps", "pix", "conv:0", "conv:1", "W1.1.0", "W1.2.0", "conv:2", "W1.1.1", "conv:3", "W2.1.0",
    "W1.2.1", "conv:4", "W2.1.1", "conv:5", "cot", "W3.1.0", "W1.3.0", "ln", "W2.2.1", "h:0:0",
    "h:0:1", "W2.2.0", "W1.3.1", "W3.1.1", "h:0:2", "h:0:3", "h:1:0", "h:1:1", "h:1:2", "h:1:3",
    "gr:1:0", "G0.1.0", "W2.3.0", "W3.2.1", "gr:1:1", "W3.2.0", "G1.1.0", "W2.3.1", "gr:0:0",
    "h:2:0", "h:2:1", "W3.3.0", "h:2:2", "G0.1.1", "h:2:3", "gr:2:1", "W3.3.1", "gr:2:0", "G1.1.1",
    "G0.2.0", "h:3:0", "h:3:1", "G0.2.1", "G1.2.0", "h:3:2", "h:3:3", "gr:3:0", "G1.2.1", "ncot:0",
    "ncot:1", "ncot:2", "G0.3.0", "G2.2.0", "G0.0.0", "gr:3:1", "G2.2.1", "gr:0:1", "G0.3.1",
    "G1.3.0", "lnb", "G1.0.0", "G3.2.1", "G3.2.0", "branch:0", "branch:1", "branch:2", "G2.3.0",
    "bout:0", "bout:1", "G0.0.1", "G2.0.0", "G1.3.1", "kg:0", "G3.3.0", "G1.0.1", "kg:1", "kg:2",
    "kg:3", "G2.3.1", "kg:4", "kg:5", "A0.0", "small", "S0", "G2.0.1", "G3.3.1", "convb:0", "A1.0",
    "convb:1", "S1", "A0.1", "convb:2", "convb:3", "A1.1", "S2", "convb:4", "A2.0", "convb:5",
    "S3", "A2.1",
)


def gelu_both(h):
    phi = 0.5 + 0.5 * lax.erf(h * math.sqrt(0.5))
    bell = jnp.exp2(h * h * (-0.5 * math.log2(math.e)))
    return h * phi, phi + h * (1.0 / math.sqrt(2.0 * math.pi)) * bell


def dot(a, b):
    return jnp.dot(a, b, preferred_element_type=f32)


def dot_rows(a, b):
    return lax.dot_general(a, b, (((0,), (0,)), ((), ())), preferred_element_type=f32)


def dot_t(a, b):
    return lax.dot_general(a, b, (((1,), (1,)), ((), ())), preferred_element_type=f32)


def kernel(
    n_dp,
    n_tensor,
    pix_hbm,
    side_hbm,
    cot_hbm,
    taps_hbm,
    depth_bias_hbm,
    gain_hbm,
    shift_hbm,
    we_hbm,
    eb_hbm,
    wr_hbm,
    rb_hbm,
    scale_hbm,
    out_hbm,
    in_grad_hbm,
    gr_hbm,
    ge_hbm,
    small_hbm,
    side_ref,
    taps_ref,
    depth_bias_ref,
    gain_ref,
    shift_ref,
    eb_ref,
    rb_ref,
    scale_ref,
    stage,
    X,
    XH,
    RSTD,
    NM,
    CM,
    BC,
    KB,
    WE,
    WR,
    EB,
    ACT,
    HC,
    EBG,
    NC,
    KG,
    ACC,
    GS,
    R0,
    R1,
    R2,
    RP,
    RZ,
    RX,
    OUTB,
    S,
    SR,
    SZ,
    SX,
    SALL,
    load_sem,
    out_sem,
    w_send,
    w_recv,
    e_send,
    e_recv,
    g_send,
    g_recv,
    x_send,
    x_recv,
    s_send,
    s_recv,
):
    D = NM.shape[1]
    G = D // LANES
    ROWS = NM.shape[0]
    IMG = ROWS // PLACES
    HALF, QUART, PIECE, BIT = D // 2, D // 4, D // 8, D // 16
    SLOTS = n_tensor
    extra = n_dp.bit_length() - 4
    dp = lax.axis_index("dp")
    tz = lax.axis_index("tensor")
    core = lax.rem(dp, 2)
    xb = lax.rem(lax.div(dp, 2), 2)
    yb = lax.rem(lax.div(dp, 4), 2)
    low = lax.rem(dp, 8)
    bits = (core, xb, yb)

    def flip(b):
        bit = bits[b] if b < 3 else lax.rem(lax.div(dp, 1 << b), 2)
        return dp + (1 - 2 * bit) * (1 << b)

    def flip_low(j):
        d = dp
        for b in range(3):
            if j >> b & 1:
                d = d + (1 - 2 * bits[b]) * (1 << b)
        return d


    t_low = lax.rem(tz, 2)
    t_high = lax.div(tz, 2)
    partner = tz + 1 - 2 * t_low
    middle = t_low + t_high - 2 * t_low * t_high
    across = 3 - tz

    def shard_of(s):
        return (tz, partner, 2 - t_high, 3 - 3 * t_high)[s]

    peers = [(flip_low(j), tz) for j in range(1, 8)]
    peers += [(dp, lax.rem(tz + o, n_tensor)) for o in range(1, n_tensor)]
    peers += [(flip(b), tz) for b in range(3, 3 + extra)]
    barrier = pltpu.get_barrier_semaphore()
    for peer in peers:
        pl.semaphore_signal(barrier, inc=1, device_id=peer, device_id_type=MESH)

    loads = [
        pltpu.make_async_copy(pix_hbm, NM, load_sem.at[0]),
        pltpu.make_async_copy(cot_hbm, BC, load_sem.at[1]),
        pltpu.make_async_copy(we_hbm, WE.at[0], load_sem.at[2]),
        pltpu.make_async_copy(wr_hbm, WR.at[0], load_sem.at[3]),
    ]
    rows_in = [
        (eb_hbm, eb_ref), (depth_bias_hbm, depth_bias_ref), (gain_hbm, gain_ref),
        (shift_hbm, shift_ref), (rb_hbm, rb_ref), (scale_hbm, scale_ref), (side_hbm, side_ref),
        (taps_hbm, taps_ref),
    ]
    rows_in = [pltpu.make_async_copy(a, b, load_sem.at[4 + i]) for i, (a, b) in enumerate(rows_in)]
    for copy in rows_in + loads:
        copy.start()

    def vector(ref):
        return ref[...].astype(f32).reshape(1, D)

    def remote(src, dst, send, recv, device):
        return pltpu.make_async_remote_copy(
            src_ref=src, dst_ref=dst, send_sem=send, recv_sem=recv,
            device_id=device, device_id_type=MESH,
        )

    PARTS = (0, 1)
    first = (xb, yb)
    second = (yb, xb)
    first_peer = (flip(1), flip(2))
    second_peer = (flip(2), flip(1))
    W = (WE, WR)
    core_half = pl.ds(pl.multiple_of(core * HALF, 16), HALF)

    def w_rows(h, level):
        start = core * HALF + h * QUART + second[h] * PIECE
        if level <= 1:
            start = start + first[h] * BIT
        return pl.ds(pl.multiple_of(start, 16), (BIT, BIT, PIECE)[level])

    def w_copy(s, m, level, h=0):
        if level == 3:
            here, device, i = W[m].at[s, core_half, :], flip(0), 6
        else:
            here = W[m].at[s, w_rows(h, level), :]
            device, i = (first_peer[h], second_peer[h])[level - 1], 2 * level + h
        return remote(here, here, w_send.at[s, m, i], w_recv.at[s, m, i], (device, tz))

    def z_piece(m, h, source, slot, device):
        rows = w_rows(h, 0)
        src = (we_hbm, wr_hbm)[m].at[rows, :] if source == 0 else W[m].at[source, rows, :]
        send = w_send.at[0, m, 2 * slot + h] if source == 0 else w_send.at[source, m, h]
        return remote(src, W[m].at[slot, rows, :], send, w_recv.at[slot, m, h], (dp, device))

    def own_pieces(m, h):
        return z_piece(m, h, 0, 1, partner), z_piece(m, h, 0, 2, across)

    def relay(s, m, h):
        return z_piece(m, h, 1, 3, across) if s == 1 else z_piece(m, h, s, s, partner)

    def in_middle(act):
        @pl.when(middle == 1)
        def _():
            act()

    def e_copy(o):
        own = EB.at[tz]
        return remote(own, own, e_send.at[o], e_recv.at[tz], (dp, lax.rem(tz + o, n_tensor)))

    def e_arrival(s):
        there = EB.at[shard_of(s)]
        return remote(there, there, e_send.at[s], e_recv.at[shard_of(s)], (dp, partner))

    def w_step(level, s, m):
        if level == 0:
            for h in PARTS:
                own_pieces(m, h)[0].start()
            for h in PARTS:
                in_middle(own_pieces(m, h)[1].start)
        elif level == 1:
            for h in PARTS:
                z_piece(m, h, 0, s, partner).wait_recv()
                w_copy(s, m, 1, h).start()
                in_middle(relay(s, m, h).start)
        elif level == 2:
            for h in PARTS:
                w_copy(s, m, 1, h).wait_recv()
                w_copy(s, m, 2, h).start()
        elif level == 3:
            for h in PARTS:
                w_copy(s, m, 2, h).wait_recv()
            w_copy(s, m, 3).start()
        else:
            w_copy(s, m, 3).wait_recv()

    pl.semaphore_wait(barrier, len(peers))
    for m in range(2):
        w_step(0, 0, m)
    for copy in rows_in:
        copy.wait()
    EB[tz] = jnp.broadcast_to(vector(eb_ref), (8, D))
    for o in range(1, n_tensor):
        e_copy(o).start()

    def g_start(h, level):
        start = core * HALF + h * QUART
        if level >= 1:
            start = start + first[h] * PIECE
        if level >= 2:
            start = start + second[h] * BIT
        return start

    PLANE = {0: 0, 2: 1, 3: 2}

    def g_copy(s, m, level, h=0):
        if level == 0:
            start, size, peer, dst, i = (1 - core) * HALF, HALF, flip(0), R0.at[s, m], 0
        elif level == 1:
            start = g_start(h, 0) + (1 - first[h]) * PIECE
            size, peer, dst, i = PIECE, first_peer[h], R1.at[PLANE[s], m, h], 1 + h
        else:
            start = g_start(h, 1) + (1 - second[h]) * BIT
            size, peer, dst, i = BIT, second_peer[h], R2.at[PLANE[s], m, h], 3 + h
        src = GS.at[s, m, pl.ds(pl.multiple_of(start, 16), size), :]
        return remote(src, dst, g_send.at[s, m, i], g_recv.at[s, m, i], (peer, tz))

    def p_copy(m):
        src = GS.at[1, m, core_half, :]
        return remote(src, RP.at[m], g_send.at[1, m, 1], g_recv.at[1, m, 1], (dp, partner))

    def z_copy(s, m, h):
        src = GS.at[s, m, pl.ds(pl.multiple_of(g_start(h, 2), 16), BIT), :]
        slot = 3 - middle
        return remote(
            src, RZ.at[slot - 2, m, h], g_send.at[s, m, 5 + h], g_recv.at[slot, m, 5 + h],
            (dp, shard_of(s)),
        )

    def z_arrival(s, m, h):
        src = GS.at[s, m, pl.ds(pl.multiple_of(g_start(h, 2), 16), BIT), :]
        return remote(
            src, RZ.at[s - 2, m, h], g_send.at[s, m, 5 + h], g_recv.at[s, m, 5 + h], (dp, partner)
        )

    def add_rows(s, m, start, size, got):
        def add(i, c):
            rows = pl.ds(pl.multiple_of(start + i * 16, 16), 16)
            mine = pl.ds(pl.multiple_of(i * 16, 16), 16)
            total = GS[s, m, rows, :].astype(f32)
            for ref in got:
                total = total + ref[mine, :].astype(f32)
            GS[s, m, rows, :] = total.astype(bf16)
            return c

        lax.fori_loop(0, size // 16, add, 0, unroll=3)

    def g_step(level, s, m):
        if level == 0:
            g_copy(s, m, 0).start()
        elif level == 1:
            g_copy(s, m, 0).wait_recv()
            got = [R0.at[s, m]]
            if s == 0:
                p_copy(m).wait_recv()
                got.append(RP.at[m])
            if s == 1:
                add_rows(s, m, core * HALF, HALF, got)
                p_copy(m).start()
            else:
                for h in PARTS:
                    for side in range(2):
                        bit = 1 - first[h] if side == 0 else first[h]
                        at = h * QUART + bit * PIECE
                        add_rows(
                            s, m, core * HALF + at, PIECE,
                            [ref.at[pl.ds(pl.multiple_of(at, 16), PIECE), :] for ref in got],
                        )
                        if side == 0:
                            g_copy(s, m, 1, h).start()
        elif level == 2:
            for h in PARTS:
                g_copy(s, m, 1, h).wait_recv()
                add_rows(s, m, g_start(h, 1), PIECE, [R1.at[PLANE[s], m, h]])
                g_copy(s, m, 2, h).start()
        else:
            for h in PARTS:
                g_copy(s, m, 2, h).wait_recv()
                add_rows(s, m, g_start(h, 2), BIT, [R2.at[PLANE[s], m, h]])
                if s > 0:
                    z_copy(s, m, h).start()

    def o_rows(h, level):
        start = h * QUART + first[h] * PIECE
        if level == 0:
            start = start + second[h] * BIT
        return pl.ds(pl.multiple_of(start, 16), (BIT, PIECE)[level])

    def a_copy(m, level, h=0):
        if level == 2:
            here, there = OUTB.at[m], (gr_hbm, ge_hbm)[m].at[core_half, :]
            peer, i = flip(0), 11
        else:
            here = there = OUTB.at[m, o_rows(h, level), :]
            peer, i = (second_peer[h], first_peer[h])[level], 7 + 2 * level + h
        return remote(here, there, g_send.at[0, m, i], g_recv.at[0, m, i], (peer, tz))

    def own_half(m):
        return pltpu.make_async_copy(
            OUTB.at[m], (gr_hbm, ge_hbm)[m].at[core_half, :], load_sem.at[m]
        )

    def x_copy(m, b, h):
        here = OUTB.at[m, o_rows(h, 0), :]
        return remote(
            here, RX.at[b - 3, m, h], x_send.at[b - 3, m, h], x_recv.at[b - 3, m, h], (flip(b), tz)
        )

    def finish_sum(m, h):
        for s in range(2, SLOTS):
            z_arrival(s, m, h).wait_recv()
        start = g_start(h, 2)
        there = start - core * HALF

        def add(i, c):
            rows = pl.ds(pl.multiple_of(start + i * 16, 16), 16)
            own = pl.ds(pl.multiple_of(i * 16, 16), 16)
            total = GS[0, m, rows, :].astype(f32)
            for s in range(2, SLOTS):
                total = total + RZ[s - 2, m, h, own, :].astype(f32)
            OUTB[m, pl.ds(pl.multiple_of(there + i * 16, 16), 16), :] = total.astype(bf16)
            return c

        lax.fori_loop(0, BIT // 16, add, 0)
        for b in range(3, 3 + extra):
            x_copy(m, b, h).start()
            x_copy(m, b, h).wait()

            def add_x(i, c):
                rows = pl.ds(pl.multiple_of(there + i * 16, 16), 16)
                OUTB[m, rows, :] = (
                    OUTB[m, rows, :] + RX[b - 3, m, h, pl.ds(pl.multiple_of(i * 16, 16), 16), :]
                )
                return c

            lax.fori_loop(0, BIT // 16, add_x, 0)

    def a_step(level, m):
        if level == 0:
            g_step(3, 0, m)
            for h in PARTS:
                finish_sum(m, h)
                a_copy(m, 0, h).start()
        elif level == 1:
            for h in PARTS:
                a_copy(m, 0, h).wait_recv()
                a_copy(m, 1, h).start()
        elif level == 2:
            for h in PARTS:
                a_copy(m, 1, h).wait_recv()
            a_copy(m, 2).start()
            own_half(m).start()
        else:
            a_copy(m, 2).wait_recv()

    def sr_copy(j):
        dst_low = flip_low(j)
        rows = pl.ds(pl.multiple_of(lax.rem(dst_low, 8) * 8, 8), 8)
        return remote(S.at[rows, :], SR.at[j - 1], s_send.at[0, j], s_recv.at[0, j], (dst_low, tz))

    def sz_copy(o):
        return remote(
            SZ.at[tz], SZ.at[tz], s_send.at[1, o], s_recv.at[1, o],
            (dp, lax.rem(tz + o, n_tensor)),
        )

    own_small = pl.ds(pl.multiple_of(low * 8, 8), 8)

    def sa_copy(j):
        here = SALL.at[own_small, :]
        return remote(here, here, s_send.at[2, j], s_recv.at[2, j], (flip_low(j), tz))

    def sx_copy(b):
        return remote(
            SALL.at[own_small, :], SX.at[b - 3], s_send.at[3, b], s_recv.at[3, b], (flip(b), tz)
        )

    def small_step(level):
        if level == 0:
            for j in range(1, 8):
                sr_copy(j).start()
        elif level == 1:
            total = S[own_small, :]
            for j in range(1, 8):
                sr_copy(j).wait_recv()
                total = total + SR[j - 1]
            SZ[tz] = total
            for o in range(1, n_tensor):
                sz_copy(o).start()
        elif level == 2:
            for o in range(1, n_tensor):
                sz_copy(o).wait_recv()
            total = SZ[0]
            for o in range(1, n_tensor):
                total = total + SZ[o]
            SALL[own_small, :] = total
            for b in range(3, 3 + extra):
                sx_copy(b).start()
                sx_copy(b).wait()
                SALL[own_small, :] = SALL[own_small, :] + SX[b - 3]
            for j in range(1, 8):
                sa_copy(j).start()
        else:
            for j in range(1, 8):
                sa_copy(j).wait_recv()

    row = lax.broadcasted_iota(jnp.int32, (IMG, LANES), 0)
    sides = jnp.zeros((IMG, LANES), jnp.int32)
    for i in range(IMG):
        sides = jnp.where(row == i, side_ref[i], sides)

    def mask_at(p):
        if isinstance(p, int):
            return jnp.where(sides > max(p // SIDE, p % SIDE), 1.0, 0.0)
        return jnp.where(sides > jnp.maximum(lax.div(p, SIDE), lax.rem(p, SIDE)), 1.0, 0.0)

    def lanes(g):
        return slice(g * LANES, (g + 1) * LANES)

    def place(p):
        return pl.ds(p * IMG, IMG)

    def spread(src):
        def body(i, c):
            rows = pl.ds(pl.multiple_of(i * 80, 16), 80)
            for g in range(G):
                stage[g, rows, :] = src[rows, lanes(g)].astype(f32)
            return c

        lax.fori_loop(0, ROWS // 80, body, 0)

    def load_pixels():
        def body(p, c):
            m = mask_at(p)
            rows = pl.ds(pl.multiple_of(p * IMG, IMG), IMG)
            for g in range(G):
                X[g, rows, :] = stage[g, pl.ds(p, IMG, stride=PLACES), :] * m
            return c

        lax.fori_loop(0, PLACES, body, 0, unroll=2)

    def load_cot():
        scale = vector(scale_ref)

        def body(q, sums):
            sums = list(sums)
            masks = [mask_at(2 * q + u) for u in range(2)]
            rows = pl.ds(pl.multiple_of(q * 2 * IMG, 2 * IMG), 2 * IMG)
            for g in range(G):
                c = [stage[g, pl.ds(2 * q + u, IMG, stride=PLACES), :] * masks[u] for u in range(2)]
                c = jnp.concatenate(c, axis=0)
                CM[rows, lanes(g)] = c.astype(bf16)
                b = (c * scale[:, lanes(g)]).astype(bf16)
                BC[rows, lanes(g)] = b
                b = b.astype(f32)
                sums[g] = sums[g] + (b[:IMG] + b[IMG:])
            return tuple(sums)

        zero = jnp.zeros((IMG, LANES), f32)
        sums = lax.fori_loop(0, PLACES // 2, body, (zero,) * G)
        for g in range(G):
            ACC[3, g] = sums[g]

    def load_taps():
        for g in range(G):
            for t in range(TAPS):
                KB[g, place(t), :] = jnp.broadcast_to(
                    taps_ref[t : t + 1, lanes(g)].astype(f32), (IMG, LANES)
                )

    def conv(src, dst, bias, flipped, post, between):
        def one(g, carry):
            for r in range(SIDE):
                acc = [None] * SIDE if bias is None else [bias[g]] * SIDE
                for rr in range(max(0, r - MARGIN), min(SIDE, r + MARGIN + 1)):
                    xs = [src[g, place(rr * SIDE + c), :] for c in range(SIDE)]
                    for dc in range(KERNEL):
                        t = (rr - r + MARGIN) * KERNEL + dc
                        k = KB[g, place(TAPS - 1 - t if flipped else t), :]
                        for c in range(SIDE):
                            cc = c + dc - MARGIN
                            if 0 <= cc < SIDE:
                                v = xs[cc] * k
                                acc[c] = v if acc[c] is None else acc[c] + v
                if post is None:
                    for c in range(SIDE):
                        dst[g, place(r * SIDE + c), :] = acc[c]
                else:
                    post(g, r, acc)
            between(g)
            return carry

        lax.fori_loop(0, G, one, 0)

    def tree(parts):
        parts = list(parts)
        while len(parts) > 1:
            parts = [
                parts[i] + parts[i + 1] if i + 1 < len(parts) else parts[i]
                for i in range(0, len(parts), 2)
            ]
        return parts[0]

    def fold(v):
        return tree(v[i : i + 8] for i in range(0, v.shape[0], 8))

    def layernorm():
        gain = vector(gain_ref)
        shift = vector(shift_ref)

        def body(q, c):
            rows = pl.ds(pl.multiple_of(q * 32, 32), 32)
            v = [XH[g, rows, :] for g in range(G)]
            mean = jnp.sum(tree(v), axis=1, keepdims=True) * (1.0 / D)
            v = [a - mean for a in v]
            total = tree([a * a for a in v])
            rstd = lax.rsqrt(jnp.sum(total, axis=1, keepdims=True) * (1.0 / D) + norm_eps)
            RSTD[rows, :] = jnp.broadcast_to(rstd, (32, LANES))
            for g in range(G):
                xh = v[g] * rstd
                XH[g, rows, :] = xh
                NM[rows, lanes(g)] = (xh * gain[:, lanes(g)] + shift[:, lanes(g)]).astype(bf16)
            return c

        lax.fori_loop(0, ROWS // 32, body, 0, unroll=5)

    def layernorm_back():
        gain = vector(gain_ref)

        def body(q, sums):
            rows = pl.ds(pl.multiple_of(q * 160, 32), 160)
            rstd = RSTD[rows, :]
            xh = [XH[g, rows, :] for g in range(G)]
            nc = [NC[g, rows, :] for g in range(G)]
            d = [nc[g] * gain[:, lanes(g)] for g in range(G)]
            m1 = jnp.sum(tree(d), axis=1, keepdims=True) * (1.0 / D)
            m2 = jnp.sum(tree([a * b for a, b in zip(d, xh)]), axis=1, keepdims=True) * (1.0 / D)
            out = []
            for g in range(G):
                dm = rstd * (d[g] - m1 - xh[g] * m2)
                NC[g, rows, :] = dm
                old = sums[g]
                out.append((old[0] + fold(nc[g] * xh[g]), old[1] + fold(nc[g]), old[2] + fold(dm)))
            return tuple(out)

        zero = jnp.zeros((8, LANES), f32)
        sums = lax.fori_loop(0, ROWS // 160, body, ((zero, zero, zero),) * G)
        for i in range(3):
            for g in range(G):
                ACC[i, g] = sums[g][i]

    def kernel_grad(between):
        def one(g, carry):
            for dr in range(KERNEL):
                acc = [[None, None] for _ in range(KERNEL)]
                for r in range(SIDE):
                    rr = r + dr - MARGIN
                    if not 0 <= rr < SIDE:
                        continue
                    ds = [NC[g, place(r * SIDE + c), :] for c in range(SIDE)]
                    xs = [X[g, place(rr * SIDE + c), :] for c in range(SIDE)]
                    for dc in range(KERNEL):
                        a = acc[dc]
                        for c in range(SIDE):
                            cc = c + dc - MARGIN
                            if 0 <= cc < SIDE:
                                v = ds[c] * xs[cc]
                                a[c % 2] = v if a[c % 2] is None else a[c % 2] + v
                for dc in range(KERNEL):
                    t = dr * KERNEL + dc
                    KG[g, t : t + 1, :] = jnp.sum(acc[dc][0] + acc[dc][1], axis=0, keepdims=True)
            between(g)
            return carry

        lax.fori_loop(0, G, one, 0)

    def hidden_block(s, j):
        if j < D // BLOCK:
            cols = slice(j * BLOCK, (j + 1) * BLOCK)
            base = j % 2 * 4
            h = dot(NM[...], WE[s, :, cols])
            stage[base] = h[:, :LANES]
            stage[base + 1] = h[:, LANES:]
            a = dot_t(BC[...], WR[s, cols, :])
            stage[base + 2] = a[:, :LANES]
            stage[base + 3] = a[:, LANES:]
        if j > 0:
            base = (j - 1) % 2 * 4
            for u in range(2):
                mine = slice((j - 1) * BLOCK + u * LANES, (j - 1) * BLOCK + (u + 1) * LANES)
                bias = EB[shard_of(s), :, mine]
                bias = jnp.concatenate([bias, bias], axis=0)
                total = None
                for i in range(ROWS // 16):
                    rows = slice(i * 16, (i + 1) * 16)
                    value, slope = gelu_both(stage[base + u, rows, :] + bias)
                    ACT[s, rows, mine] = value.astype(bf16)
                    w = (stage[base + 2 + u, rows, :] * slope).astype(bf16)
                    HC[s, rows, mine] = w
                    w = w.astype(f32)
                    w = w[:8] + w[8:]
                    total = w if total is None else total + w
                EBG[s, :, mine] = total

    def grad_block(s, m):
        for j in range(D // BLOCK):
            cols = slice(j * BLOCK, (j + 1) * BLOCK)
            if m == 0:
                GS[s, 0, cols, :] = dot_rows(ACT[s, :, cols], BC[...]).astype(bf16)
            else:
                GS[s, 1, :, cols] = dot_rows(NM[...], HC[s, :, cols]).astype(bf16)

    def back_to_normed(n):
        cols = slice(n * BLOCK, (n + 1) * BLOCK)
        total = dot_t(HC[0], WE[0, cols, :])
        for s in range(1, SLOTS):
            total = total + dot_t(HC[s], WE[s, cols, :])
        NC[2 * n] = total[:, :LANES]
        NC[2 * n + 1] = total[:, LANES:]

    def to_branch(n):
        cols = slice(n * BLOCK, (n + 1) * BLOCK)
        total = dot(ACT[0], WR[0, :, cols])
        for s in range(1, SLOTS):
            total = total + dot(ACT[s], WR[s, :, cols])
        XH[2 * n] = total[:, :LANES]
        XH[2 * n + 1] = total[:, LANES:]

    def block_output(part):
        scale = vector(scale_ref)
        shift = vector(rb_ref)

        def body(q, sums):
            sums = list(sums)
            rows = pl.ds(pl.multiple_of(q * 2 * IMG, 2 * IMG), 2 * IMG)
            masks = jnp.concatenate([mask_at(2 * q + u) for u in range(2)], axis=0)
            for g in range(G):
                branch = XH[g, rows, :] + shift[:, lanes(g)]
                v = CM[rows, lanes(g)].astype(f32) * branch
                sums[g] = sums[g] + (v[:IMG] + v[IMG:])
                value = X[g, rows, :] + masks * (scale[:, lanes(g)] * branch)
                for u in range(2):
                    stage[g, pl.ds(2 * q + u, IMG, stride=PLACES), :] = value[u * IMG : (u + 1) * IMG]
            return tuple(sums)

        zero = jnp.zeros((IMG, LANES), f32)
        n = PLACES // 4
        sums = lax.fori_loop(part * n, part * n + n, body, (zero,) * G)
        for g in range(G):
            ACC[4, g] = sums[g] if part == 0 else ACC[4, g] + sums[g]
        if part == 0:
            return

        def narrow(i, c):
            rows = pl.ds(pl.multiple_of(i * 80, 16), 80)
            for g in range(G):
                NM[rows, lanes(g)] = stage[g, rows, :].astype(bf16)
            return c

        lax.fori_loop(0, ROWS // 80, narrow, 0)

    def small_sums():
        S[...] = jnp.zeros_like(S)
        for g in range(G):
            S[:TAPS, lanes(g)] = KG[g, :TAPS, :]
            for r, i in ((ROW_BIAS, 2), (ROW_GAIN, 0), (ROW_SHIFT, 1), (ROW_REDUCE, 3), (ROW_SCALE, 4)):
                S[r : r + 1, lanes(g)] = jnp.sum(ACC[i, g], axis=0, keepdims=True)
        for s in range(SLOTS):
            r = ROW_EXPAND + shard_of(s)
            S[pl.ds(r, 1), :] = jnp.sum(EBG[s], axis=0, keepdims=True)

    def tell(name):
        kind, _, rest = name.partition(".")
        where = [int(v) for v in rest.split(".")] if rest else []
        if kind[0] == "W":
            w_step(int(kind[1]), *where)
        elif kind[0] == "G":
            g_step(int(kind[1]), *where)
        elif kind[0] == "A":
            a_step(int(kind[1]), *where)
        else:
            small_step(int(kind[1]))

    loads[0].wait()
    biases = vector(depth_bias_ref)
    for g in range(G):
        ACC[0, g] = jnp.broadcast_to(biases[:, lanes(g)], (8, LANES))

    def finish_input(g, r, acc):
        cols = pl.ds(pl.multiple_of(g * LANES, LANES), LANES)
        for c in range(0, SIDE, 2):
            p = r * SIDE + c
            cot = CM[pl.ds(p * IMG, 2 * IMG), cols].astype(f32)
            for u in range(2):
                XH[g, pl.ds(p + u, IMG, stride=PLACES), :] = (
                    acc[c + u] * mask_at(p + u) + cot[u * IMG : (u + 1) * IMG]
                )

    def out_copy(g):
        return pltpu.make_async_copy(
            XH.at[g], in_grad_hbm.at[:, pl.ds(pl.multiple_of(g * LANES, LANES), LANES)], out_sem.at[1 + g]
        )

    def over_groups(names, call):
        kind = names[0].partition(":")[0]
        after = {}
        group = 0
        for name in names:
            if name.startswith(kind + ":"):
                group = int(name.partition(":")[2])
            else:
                after.setdefault(group, []).append(name)

        def between(g):
            if kind == "convb":
                out_copy(g).start()
            for i, told in after.items():
                @pl.when(g == i)
                def _():
                    for name in told:
                        tell(name)

        call(between)

    looped = {
        "conv": lambda between: conv(X, XH, ACC.at[0], False, None, between),
        "kg": kernel_grad,
        "convb": lambda between: conv(NC, None, None, True, finish_input, between),
    }

    def start_output(part):
        block_output(part)
        if part == 1:
            pltpu.make_async_copy(NM, out_hbm, out_sem.at[0]).start()

    def pixels_in():
        spread(NM)
        load_pixels()

    def cot_in():
        loads[1].wait()
        spread(BC)
        load_cot()

    def linears_ready(s):
        if s == 0:
            loads[2].wait()
            loads[3].wait()
        else:
            for m in range(2):
                w_step(4, s, m)
            e_arrival(s).wait_recv()

    def step(name):
        kind, _, rest = name.partition(":")
        where = [int(v) for v in rest.split(":")] if rest else []
        if "." in name or kind[0] == "S":
            tell(name)
        elif kind == "h":
            if where[1] == 0:
                linears_ready(where[0])
            hidden_block(*where)
        elif kind == "gr":
            grad_block(*where)
        else:
            {
                "pix": pixels_in,
                "taps": load_taps,
                "cot": cot_in,
                "ln": layernorm,
                "lnb": layernorm_back,
                "ncot": back_to_normed,
                "branch": to_branch,
                "bout": start_output,
                "small": small_sums,
            }[kind](*where)

    at = 0
    while at < len(PLAN):
        kind = PLAN[at].partition(":")[0]
        if kind in looped:
            last = max(i for i, name in enumerate(PLAN) if name.startswith(kind + ":"))
            over_groups(PLAN[at : last + 1], looped[kind])
            at = last + 1
        else:
            step(PLAN[at])
            at += 1
    tail = [
        pltpu.make_async_copy(SALL, small_hbm, load_sem.at[2]),
    ]
    for copy in tail:
        copy.start()
    for m in range(2):
        a_step(3, m)
    for s in range(1, SLOTS):
        e_copy(s).wait_send()
    for m in range(2):
        for h in PARTS:
            own_pieces(m, h)[0].wait_send()
            in_middle(own_pieces(m, h)[1].wait_send)
            for s in range(1, SLOTS):
                in_middle(relay(s, m, h).wait_send)
                for level in (1, 2):
                    w_copy(s, m, level, h).wait_send()
            for s in PLANE:
                for level in (1, 2):
                    g_copy(s, m, level, h).wait_send()
                if s > 0:
                    z_copy(s, m, h).wait_send()
            for level in range(2):
                a_copy(m, level, h).wait_send()
        for s in range(SLOTS):
            if s > 0:
                w_copy(s, m, 3).wait_send()
            g_copy(s, m, 0).wait_send()
        p_copy(m).wait_send()
        a_copy(m, 2).wait_send()
    for j in range(1, 8):
        sr_copy(j).wait_send()
        sa_copy(j).wait_send()
    for o in range(1, n_tensor):
        sz_copy(o).wait_send()
    pltpu.make_async_copy(NM, out_hbm, out_sem.at[0]).wait()
    for g in range(G):
        out_copy(g).wait()
    for copy in tail:
        copy.wait()
    for m in range(2):
        own_half(m).wait()


def hand_over(
    out_in, grad_in, gr, ge, small,
    block_out, input_grad, kernel_grad, bias_grad, gain_grad, shift_grad,
    expand_grad, expand_bias_grad, reduce_grad, reduce_bias_grad, scale_grad,
    narrow, wide, grad_rows, out_rows, sums, taps, *rest,
):
    vectors, (there_sem, back_sem, in_sem, out_sem, small_sem) = rest[:6], rest[6:]
    D = gr.shape[0]
    third = D // 3
    half = out_in.shape[0] // 2
    halves = [
        (held.at[pl.ds(i * half, half)], src.at[pl.ds(i * half, half)], dst.at[pl.ds(i * half, half)])
        for i in range(2)
        for held, src, dst in ((grad_rows, grad_in, input_grad), (out_rows, out_in, block_out))
    ]
    there = [pltpu.make_async_copy(v[1], v[0], there_sem.at[i]) for i, v in enumerate(halves)]
    back = [pltpu.make_async_copy(v[0], v[2], back_sem.at[i]) for i, v in enumerate(halves)]
    parts = [(i, m) for i in range(3) for m in range(2)]

    def rows(i):
        return pl.ds(i * third, third)

    reads = {
        (i, m): pltpu.make_async_copy((gr, ge)[m].at[rows(i)], narrow.at[m, rows(i)], in_sem.at[m, i])
        for i, m in parts
    }
    writes = {
        (i, m): pltpu.make_async_copy(
            wide.at[m, rows(i)], (reduce_grad, expand_grad)[m].at[rows(i)], out_sem.at[m, i]
        )
        for i, m in parts
    }
    load = pltpu.make_async_copy(small, sums, small_sem.at[0])
    for part in parts[:2]:
        reads[part].start()
    for copy in there:
        copy.start()
    load.start()
    for part in parts[2:]:
        reads[part].start()
    for i, m in parts:
        reads[i, m].wait()
        def widen(k, c):
            at = pl.ds(pl.multiple_of(i * third + k * 32, 32), 32)
            wide[m, at, :] = narrow[m, at, :].astype(f32)
            return c

        lax.fori_loop(0, third // 32, widen, 0)
        writes[i, m].start()
        if m == 1:
            for k in range(len(there)):
                if k * 3 // len(there) == i:
                    there[k].wait()
                    back[k].start()
    load.wait()
    taps[...] = sums[:TAPS, :]
    own = ROW_EXPAND + lax.axis_index("tensor")
    given = [pltpu.make_async_copy(taps, kernel_grad, small_sem.at[0])]
    for i, (row, ref) in enumerate((
        (ROW_BIAS, bias_grad), (ROW_GAIN, gain_grad), (ROW_SHIFT, shift_grad),
        (ROW_REDUCE, reduce_bias_grad), (ROW_SCALE, scale_grad), (own, expand_bias_grad),
    )):
        vectors[i][...] = sums[pl.ds(row, 1), :].reshape(D)
        given.append(pltpu.make_async_copy(vectors[i], ref, small_sem.at[1 + i]))
    for copy in given:
        copy.start()
    for part in parts:
        writes[part].wait()
    for copy in back + given:
        copy.wait()


def per_device(
    n_dp,
    n_tensor,
    pixels,
    crop_sides,
    out_cotangent,
    depth_kernel,
    depth_bias,
    norm_gain,
    norm_shift,
    expand_weight,
    expand_bias,
    reduce_weight,
    reduce_bias,
    layer_scale,
):
    rows, D = pixels.shape
    G = D // LANES
    img = rows // PLACES
    slots = n_tensor
    extra = max(n_dp.bit_length() - 4, 1)
    hbm = pl.BlockSpec(memory_space=pltpu.HBM)
    V = pltpu.VMEM
    DMA = pltpu.SemaphoreType.DMA
    scratch = [pltpu.SMEM((img,), jnp.int32), V((TAPS, D), bf16)] + [V((D,), bf16) for _ in range(6)] + [
        V((8, rows, LANES), f32),
        V((G, rows, LANES), f32),
        V((G, rows, LANES), f32),
        V((rows, LANES), f32),
        V((rows, D), bf16),
        V((rows, D), bf16),
        V((rows, D), bf16),
        V((G, TAPS * img, LANES), f32),
        V((slots, D, D), bf16),
        V((slots, D, D), bf16),
        V((slots, 8, D), f32),
        V((slots, rows, D), bf16),
        V((slots, rows, D), bf16),
        V((slots, 8, D), f32),
        V((G, rows, LANES), f32),
        V((G, 56, LANES), f32),
        V((5, G, 8, LANES), f32),
        V((slots, 2, D, D), bf16),
        V((slots, 2, D // 2, D), bf16),
        V((slots - 1, 2, 2, D // 8, D), bf16),
        V((slots - 1, 2, 2, D // 16, D), bf16),
        V((2, D // 2, D), bf16),
        V((slots - 2, 2, 2, D // 16, D), bf16),
        V((extra, 2, 2, D // 16 if n_dp > 8 else 16, D), bf16),
        V((2, D // 2, D), bf16),
        V((SMALL, D), f32),
        V((7, 8, D), f32),
        V((slots, 8, D), f32),
        V((extra, 8, D), f32),
        V((SMALL, D), f32),
        DMA((12,)),
        DMA((1 + G,)),
        DMA((slots, 2, 8)),
        DMA((slots, 2, 8)),
        DMA((slots,)),
        DMA((slots,)),
        DMA((slots, 2, 12)),
        DMA((slots, 2, 12)),
        DMA((extra, 2, 2)),
        DMA((extra, 2, 2)),
        DMA((4, 8)),
        DMA((4, 8)),
    ]
    block_out, input_grad, gr, ge, small = pl.pallas_call(
        functools.partial(kernel, n_dp, n_tensor),
        out_shape=[
            jax.ShapeDtypeStruct((rows, D), bf16),
            jax.ShapeDtypeStruct((rows, D), f32),
            jax.ShapeDtypeStruct((D, D), bf16),
            jax.ShapeDtypeStruct((D, D), bf16),
            jax.ShapeDtypeStruct((SMALL, D), f32),
        ],
        in_specs=[hbm] * 12,
        out_specs=[hbm] * 5,
        scratch_shapes=scratch,
        compiler_params=pltpu.CompilerParams(
            collective_id=0, has_side_effects=True, vmem_limit_bytes=63 << 20
        ),
        cost_estimate=pl.CostEstimate(
            flops=12 * rows * D * D * slots, bytes_accessed=20 * rows * D, transcendentals=0
        ),
    )(
        pixels,
        crop_sides,
        out_cotangent,
        depth_kernel,
        depth_bias,
        norm_gain,
        norm_shift,
        expand_weight,
        expand_bias,
        reduce_weight,
        reduce_bias,
        layer_scale,
    )
    vec = jax.ShapeDtypeStruct((D,), f32)
    square = jax.ShapeDtypeStruct((D, D), f32)
    return pl.pallas_call(
        hand_over,
        out_shape=[
            jax.ShapeDtypeStruct((rows, D), bf16),
            jax.ShapeDtypeStruct((rows, D), f32),
            jax.ShapeDtypeStruct((TAPS, D), f32),
            vec, vec, vec, square, vec, square, vec, vec,
        ],
        in_specs=[hbm] * 5,
        out_specs=[hbm] * 11,
        scratch_shapes=[
            V((2, D, D), bf16),
            V((2, D, D), f32),
            V((rows, D), f32),
            V((rows, D), bf16),
            V((SMALL, D), f32),
            V((TAPS, D), f32),
            *[V((D,), f32) for _ in range(6)],
            DMA((4,)),
            DMA((4,)),
            DMA((2, 3)),
            DMA((2, 3)),
            DMA((7,)),
        ],
        compiler_params=pltpu.CompilerParams(vmem_limit_bytes=60 << 20),
    )(block_out, input_grad, gr, ge, small)


def solution(mesh):
    in_specs = (
        P(("dp", "tensor"), None),
        P(("dp", "tensor")),
        P(("dp", "tensor"), None),
        P(),
        P(),
        P(),
        P(),
        P(None, "tensor"),
        P("tensor"),
        P("tensor", None),
        P(),
        P(),
    )
    out_specs = (
        P(("dp", "tensor"), None),
        P(("dp", "tensor"), None),
        P(),
        P(),
        P(),
        P(),
        P(None, "tensor"),
        P("tensor"),
        P("tensor", None),
        P(),
        P(),
    )
    return jax.shard_map(
        functools.partial(per_device, mesh.shape["dp"], mesh.shape["tensor"]),
        mesh=mesh,
        in_specs=in_specs,
        out_specs=out_specs,
        check_vma=False,
    )
```

```python
import functools
import math
import jax
import jax.numpy as jnp
from jax import lax
from jax.experimental import pallas as pl
from jax.experimental.pallas import tpu as pltpu
from jax.sharding import PartitionSpec as P

KERNEL = 7
SIDE = 10
PLACES = SIDE * SIDE
TAPS = KERNEL * KERNEL
MARGIN = KERNEL // 2
LANES = 128
BLOCK = 256
norm_eps = 1e-06
f32 = jnp.float32
bf16 = jnp.bfloat16
MESH = pl.DeviceIdType.MESH
ROW_BIAS, ROW_GAIN, ROW_SHIFT, ROW_REDUCE, ROW_SCALE, ROW_EXPAND = 49, 50, 51, 52, 53, 54
SMALL = 64
PLAN = (
    "taps", "pix", "conv:0", "conv:1", "W1.1.0", "W1.2.0", "conv:2", "W1.1.1", "conv:3", "W2.1.0",
    "W1.2.1", "conv:4", "W2.1.1", "conv:5", "cot", "W3.1.0", "W1.3.0", "ln", "W2.2.1", "h:0:0",
    "h:0:1", "W2.2.0", "W1.3.1", "W3.1.1", "h:0:2", "h:0:3", "h:1:0", "h:1:1", "h:1:2", "h:1:3",
    "gr:1:0", "G0.1.0", "W2.3.0", "W3.2.1", "gr:1:1", "W3.2.0", "G1.1.0", "W2.3.1", "gr:0:0",
    "h:2:0", "h:2:1", "W3.3.0", "h:2:2", "G0.1.1", "h:2:3", "gr:2:1", "W3.3.1", "gr:2:0", "G1.1.1",
    "G0.2.0", "h:3:0", "h:3:1", "G0.2.1", "G1.2.0", "h:3:2", "h:3:3", "gr:3:0", "G0.3.0", "G1.2.1",
    "gr:3:1", "G0.3.1", "ncot:0", "ncot:1", "G2.2.0", "ncot:2", "G0.0.0", "G2.2.1", "gr:0:1",
    "G0.0.1", "G1.3.0", "lnb", "G1.0.0", "G3.2.1", "G3.2.0", "branch:0", "branch:1", "branch:2",
    "G2.3.0", "bout:0", "bout:1", "G2.0.0", "G1.3.1", "kg:0", "G3.3.0", "G1.0.1", "kg:1", "kg:2",
    "kg:3", "G2.3.1", "kg:4", "kg:5", "A0.0", "small", "S0", "G2.0.1", "G3.3.1", "convb:0", "A1.0",
    "convb:1", "S1", "A0.1", "convb:2", "convb:3", "A1.1", "S2", "convb:4", "A2.0", "convb:5",
    "S3", "A2.1",
)


def gelu_both(h):
    phi = 0.5 + 0.5 * lax.erf(h * math.sqrt(0.5))
    bell = jnp.exp2(h * h * (-0.5 * math.log2(math.e)))
    return h * phi, phi + h * (1.0 / math.sqrt(2.0 * math.pi)) * bell


def dot(a, b):
    return jnp.dot(a, b, preferred_element_type=f32)


def dot_rows(a, b):
    return lax.dot_general(a, b, (((0,), (0,)), ((), ())), preferred_element_type=f32)


def dot_t(a, b):
    return lax.dot_general(a, b, (((1,), (1,)), ((), ())), preferred_element_type=f32)


def kernel(
    n_dp,
    n_tensor,
    pix_hbm,
    side_hbm,
    cot_hbm,
    taps_hbm,
    depth_bias_hbm,
    gain_hbm,
    shift_hbm,
    we_hbm,
    eb_hbm,
    wr_hbm,
    rb_hbm,
    scale_hbm,
    out_hbm,
    in_grad_hbm,
    gr_hbm,
    ge_hbm,
    small_hbm,
    side_ref,
    taps_ref,
    depth_bias_ref,
    gain_ref,
    shift_ref,
    eb_ref,
    rb_ref,
    scale_ref,
    stage,
    X,
    XH,
    RSTD,
    NM,
    CM,
    BC,
    KB,
    WE,
    WR,
    EB,
    ACT,
    HC,
    EBG,
    NC,
    KG,
    ACC,
    GS,
    R0,
    R1,
    R2,
    RP,
    RZ,
    RX,
    OUTB,
    S,
    SR,
    SZ,
    SX,
    SALL,
    load_sem,
    out_sem,
    w_send,
    w_recv,
    e_send,
    e_recv,
    g_send,
    g_recv,
    x_send,
    x_recv,
    s_send,
    s_recv,
):
    D = NM.shape[1]
    G = D // LANES
    ROWS = NM.shape[0]
    IMG = ROWS // PLACES
    HALF, QUART, PIECE, BIT = D // 2, D // 4, D // 8, D // 16
    SLOTS = n_tensor
    extra = n_dp.bit_length() - 4
    dp = lax.axis_index("dp")
    tz = lax.axis_index("tensor")
    core = lax.rem(dp, 2)
    xb = lax.rem(lax.div(dp, 2), 2)
    yb = lax.rem(lax.div(dp, 4), 2)
    low = lax.rem(dp, 8)
    bits = (core, xb, yb)

    def flip(b):
        bit = bits[b] if b < 3 else lax.rem(lax.div(dp, 1 << b), 2)
        return dp + (1 - 2 * bit) * (1 << b)

    def flip_low(j):
        d = dp
        for b in range(3):
            if j >> b & 1:
                d = d + (1 - 2 * bits[b]) * (1 << b)
        return d


    t_low = lax.rem(tz, 2)
    t_high = lax.div(tz, 2)
    partner = tz + 1 - 2 * t_low
    middle = t_low + t_high - 2 * t_low * t_high
    across = 3 - tz

    def shard_of(s):
        return (tz, partner, 2 - t_high, 3 - 3 * t_high)[s]

    peers = [(flip_low(j), tz) for j in range(1, 8)]
    peers += [(dp, lax.rem(tz + o, n_tensor)) for o in range(1, n_tensor)]
    peers += [(flip(b), tz) for b in range(3, 3 + extra)]
    barrier = pltpu.get_barrier_semaphore()
    for peer in peers:
        pl.semaphore_signal(barrier, inc=1, device_id=peer, device_id_type=MESH)

    loads = [
        pltpu.make_async_copy(pix_hbm, NM, load_sem.at[0]),
        pltpu.make_async_copy(cot_hbm, BC, load_sem.at[1]),
        pltpu.make_async_copy(we_hbm, WE.at[0], load_sem.at[2]),
        pltpu.make_async_copy(wr_hbm, WR.at[0], load_sem.at[3]),
    ]
    rows_in = [
        (eb_hbm, eb_ref), (depth_bias_hbm, depth_bias_ref), (gain_hbm, gain_ref),
        (shift_hbm, shift_ref), (rb_hbm, rb_ref), (scale_hbm, scale_ref), (side_hbm, side_ref),
        (taps_hbm, taps_ref),
    ]
    rows_in = [pltpu.make_async_copy(a, b, load_sem.at[4 + i]) for i, (a, b) in enumerate(rows_in)]
    for copy in rows_in + loads:
        copy.start()

    def vector(ref):
        return ref[...].astype(f32).reshape(1, D)

    def remote(src, dst, send, recv, device):
        return pltpu.make_async_remote_copy(
            src_ref=src, dst_ref=dst, send_sem=send, recv_sem=recv,
            device_id=device, device_id_type=MESH,
        )

    PARTS = (0, 1)
    first = (xb, yb)
    second = (yb, xb)
    first_peer = (flip(1), flip(2))
    second_peer = (flip(2), flip(1))
    W = (WE, WR)
    core_half = pl.ds(pl.multiple_of(core * HALF, 16), HALF)

    def w_rows(h, level):
        start = core * HALF + h * QUART + second[h] * PIECE
        if level <= 1:
            start = start + first[h] * BIT
        return pl.ds(pl.multiple_of(start, 16), (BIT, BIT, PIECE)[level])

    def w_copy(s, m, level, h=0):
        if level == 3:
            here, device, i = W[m].at[s, core_half, :], flip(0), 6
        else:
            here = W[m].at[s, w_rows(h, level), :]
            device, i = (first_peer[h], second_peer[h])[level - 1], 2 * level + h
        return remote(here, here, w_send.at[s, m, i], w_recv.at[s, m, i], (device, tz))

    def z_piece(m, h, source, slot, device):
        rows = w_rows(h, 0)
        src = (we_hbm, wr_hbm)[m].at[rows, :] if source == 0 else W[m].at[source, rows, :]
        send = w_send.at[0, m, 2 * slot + h] if source == 0 else w_send.at[source, m, h]
        return remote(src, W[m].at[slot, rows, :], send, w_recv.at[slot, m, h], (dp, device))

    def own_pieces(m, h):
        return z_piece(m, h, 0, 1, partner), z_piece(m, h, 0, 2, across)

    def relay(s, m, h):
        return z_piece(m, h, 1, 3, across) if s == 1 else z_piece(m, h, s, s, partner)

    def in_middle(act):
        @pl.when(middle == 1)
        def _():
            act()

    def e_copy(o):
        own = EB.at[tz]
        return remote(own, own, e_send.at[o], e_recv.at[tz], (dp, lax.rem(tz + o, n_tensor)))

    def e_arrival(s):
        there = EB.at[shard_of(s)]
        return remote(there, there, e_send.at[s], e_recv.at[shard_of(s)], (dp, partner))

    def w_step(level, s, m):
        if level == 0:
            for h in PARTS:
                own_pieces(m, h)[0].start()
            for h in PARTS:
                in_middle(own_pieces(m, h)[1].start)
        elif level == 1:
            for h in PARTS:
                z_piece(m, h, 0, s, partner).wait_recv()
                w_copy(s, m, 1, h).start()
                in_middle(relay(s, m, h).start)
        elif level == 2:
            for h in PARTS:
                w_copy(s, m, 1, h).wait_recv()
                w_copy(s, m, 2, h).start()
        elif level == 3:
            for h in PARTS:
                w_copy(s, m, 2, h).wait_recv()
            w_copy(s, m, 3).start()
        else:
            w_copy(s, m, 3).wait_recv()

    pl.semaphore_wait(barrier, len(peers))
    for m in range(2):
        w_step(0, 0, m)
    for copy in rows_in:
        copy.wait()
    EB[tz] = jnp.broadcast_to(vector(eb_ref), (8, D))
    for o in range(1, n_tensor):
        e_copy(o).start()

    def g_start(h, level):
        start = core * HALF + h * QUART
        if level >= 1:
            start = start + first[h] * PIECE
        if level >= 2:
            start = start + second[h] * BIT
        return start

    PLANE = {0: 0, 2: 1, 3: 2}

    def g_copy(s, m, level, h=0):
        if level == 0:
            start, size, peer, dst, i = (1 - core) * HALF, HALF, flip(0), R0.at[s, m], 0
        elif level == 1:
            start = g_start(h, 0) + (1 - first[h]) * PIECE
            size, peer, dst, i = PIECE, first_peer[h], R1.at[PLANE[s], m, h], 1 + h
        else:
            start = g_start(h, 1) + (1 - second[h]) * BIT
            size, peer, dst, i = BIT, second_peer[h], R2.at[PLANE[s], m, h], 3 + h
        src = GS.at[s, m, pl.ds(pl.multiple_of(start, 16), size), :]
        return remote(src, dst, g_send.at[s, m, i], g_recv.at[s, m, i], (peer, tz))

    def p_copy(m):
        src = GS.at[1, m, core_half, :]
        return remote(src, RP.at[m], g_send.at[1, m, 1], g_recv.at[1, m, 1], (dp, partner))

    def z_copy(s, m, h):
        src = GS.at[s, m, pl.ds(pl.multiple_of(g_start(h, 2), 16), BIT), :]
        slot = 3 - middle
        return remote(
            src, RZ.at[slot - 2, m, h], g_send.at[s, m, 5 + h], g_recv.at[slot, m, 5 + h],
            (dp, shard_of(s)),
        )

    def z_arrival(s, m, h):
        src = GS.at[s, m, pl.ds(pl.multiple_of(g_start(h, 2), 16), BIT), :]
        return remote(
            src, RZ.at[s - 2, m, h], g_send.at[s, m, 5 + h], g_recv.at[s, m, 5 + h], (dp, partner)
        )

    def add_rows(s, m, start, size, got):
        def add(i, c):
            rows = pl.ds(pl.multiple_of(start + i * 16, 16), 16)
            mine = pl.ds(pl.multiple_of(i * 16, 16), 16)
            total = GS[s, m, rows, :].astype(f32)
            for ref in got:
                total = total + ref[mine, :].astype(f32)
            GS[s, m, rows, :] = total.astype(bf16)
            return c

        lax.fori_loop(0, size // 16, add, 0, unroll=3)

    def g_step(level, s, m):
        if level == 0:
            g_copy(s, m, 0).start()
        elif level == 1:
            g_copy(s, m, 0).wait_recv()
            got = [R0.at[s, m]]
            if s == 0:
                p_copy(m).wait_recv()
                got.append(RP.at[m])
            if s == 1:
                add_rows(s, m, core * HALF, HALF, got)
                p_copy(m).start()
            else:
                for h in PARTS:
                    for side in range(2):
                        bit = 1 - first[h] if side == 0 else first[h]
                        at = h * QUART + bit * PIECE
                        add_rows(
                            s, m, core * HALF + at, PIECE,
                            [ref.at[pl.ds(pl.multiple_of(at, 16), PIECE), :] for ref in got],
                        )
                        if side == 0:
                            g_copy(s, m, 1, h).start()
        elif level == 2:
            for h in PARTS:
                g_copy(s, m, 1, h).wait_recv()
                add_rows(s, m, g_start(h, 1), PIECE, [R1.at[PLANE[s], m, h]])
                g_copy(s, m, 2, h).start()
        else:
            for h in PARTS:
                g_copy(s, m, 2, h).wait_recv()
                add_rows(s, m, g_start(h, 2), BIT, [R2.at[PLANE[s], m, h]])
                if s > 0:
                    z_copy(s, m, h).start()

    def o_rows(h, level):
        start = h * QUART + first[h] * PIECE
        if level == 0:
            start = start + second[h] * BIT
        return pl.ds(pl.multiple_of(start, 16), (BIT, PIECE)[level])

    def a_copy(m, level, h=0):
        if level == 2:
            here, there = OUTB.at[m], (gr_hbm, ge_hbm)[m].at[core_half, :]
            peer, i = flip(0), 11
        else:
            here = there = OUTB.at[m, o_rows(h, level), :]
            peer, i = (second_peer[h], first_peer[h])[level], 7 + 2 * level + h
        return remote(here, there, g_send.at[0, m, i], g_recv.at[0, m, i], (peer, tz))

    def own_half(m):
        return pltpu.make_async_copy(
            OUTB.at[m], (gr_hbm, ge_hbm)[m].at[core_half, :], load_sem.at[m]
        )

    def x_copy(m, b, h):
        here = OUTB.at[m, o_rows(h, 0), :]
        return remote(
            here, RX.at[b - 3, m, h], x_send.at[b - 3, m, h], x_recv.at[b - 3, m, h], (flip(b), tz)
        )

    def finish_sum(m, h):
        for s in range(2, SLOTS):
            z_arrival(s, m, h).wait_recv()
        start = g_start(h, 2)
        there = start - core * HALF

        def add(i, c):
            rows = pl.ds(pl.multiple_of(start + i * 16, 16), 16)
            own = pl.ds(pl.multiple_of(i * 16, 16), 16)
            total = GS[0, m, rows, :].astype(f32)
            for s in range(2, SLOTS):
                total = total + RZ[s - 2, m, h, own, :].astype(f32)
            OUTB[m, pl.ds(pl.multiple_of(there + i * 16, 16), 16), :] = total.astype(bf16)
            return c

        lax.fori_loop(0, BIT // 16, add, 0)
        for b in range(3, 3 + extra):
            x_copy(m, b, h).start()
            x_copy(m, b, h).wait()

            def add_x(i, c):
                rows = pl.ds(pl.multiple_of(there + i * 16, 16), 16)
                OUTB[m, rows, :] = (
                    OUTB[m, rows, :] + RX[b - 3, m, h, pl.ds(pl.multiple_of(i * 16, 16), 16), :]
                )
                return c

            lax.fori_loop(0, BIT // 16, add_x, 0)

    def a_step(level, m):
        if level == 0:
            g_step(3, 0, m)
            for h in PARTS:
                finish_sum(m, h)
                a_copy(m, 0, h).start()
        elif level == 1:
            for h in PARTS:
                a_copy(m, 0, h).wait_recv()
                a_copy(m, 1, h).start()
        elif level == 2:
            for h in PARTS:
                a_copy(m, 1, h).wait_recv()
            a_copy(m, 2).start()
            own_half(m).start()
        else:
            a_copy(m, 2).wait_recv()

    def sr_copy(j):
        dst_low = flip_low(j)
        rows = pl.ds(pl.multiple_of(lax.rem(dst_low, 8) * 8, 8), 8)
        return remote(S.at[rows, :], SR.at[j - 1], s_send.at[0, j], s_recv.at[0, j], (dst_low, tz))

    def sz_copy(o):
        return remote(
            SZ.at[tz], SZ.at[tz], s_send.at[1, o], s_recv.at[1, o],
            (dp, lax.rem(tz + o, n_tensor)),
        )

    own_small = pl.ds(pl.multiple_of(low * 8, 8), 8)

    def sa_copy(j):
        here = SALL.at[own_small, :]
        return remote(here, here, s_send.at[2, j], s_recv.at[2, j], (flip_low(j), tz))

    def sx_copy(b):
        return remote(
            SALL.at[own_small, :], SX.at[b - 3], s_send.at[3, b], s_recv.at[3, b], (flip(b), tz)
        )

    def small_step(level):
        if level == 0:
            for j in range(1, 8):
                sr_copy(j).start()
        elif level == 1:
            total = S[own_small, :]
            for j in range(1, 8):
                sr_copy(j).wait_recv()
                total = total + SR[j - 1]
            SZ[tz] = total
            for o in range(1, n_tensor):
                sz_copy(o).start()
        elif level == 2:
            for o in range(1, n_tensor):
                sz_copy(o).wait_recv()
            total = SZ[0]
            for o in range(1, n_tensor):
                total = total + SZ[o]
            SALL[own_small, :] = total
            for b in range(3, 3 + extra):
                sx_copy(b).start()
                sx_copy(b).wait()
                SALL[own_small, :] = SALL[own_small, :] + SX[b - 3]
            for j in range(1, 8):
                sa_copy(j).start()
        else:
            for j in range(1, 8):
                sa_copy(j).wait_recv()

    row = lax.broadcasted_iota(jnp.int32, (IMG, LANES), 0)
    sides = jnp.zeros((IMG, LANES), jnp.int32)
    for i in range(IMG):
        sides = jnp.where(row == i, side_ref[i], sides)

    def mask_at(p):
        if isinstance(p, int):
            return jnp.where(sides > max(p // SIDE, p % SIDE), 1.0, 0.0)
        return jnp.where(sides > jnp.maximum(lax.div(p, SIDE), lax.rem(p, SIDE)), 1.0, 0.0)

    def lanes(g):
        return slice(g * LANES, (g + 1) * LANES)

    def place(p):
        return pl.ds(p * IMG, IMG)

    def spread(src):
        def body(i, c):
            rows = pl.ds(pl.multiple_of(i * 80, 16), 80)
            for g in range(G):
                stage[g, rows, :] = src[rows, lanes(g)].astype(f32)
            return c

        lax.fori_loop(0, ROWS // 80, body, 0)

    def load_pixels():
        def body(p, c):
            m = mask_at(p)
            rows = pl.ds(pl.multiple_of(p * IMG, IMG), IMG)
            for g in range(G):
                X[g, rows, :] = stage[g, pl.ds(p, IMG, stride=PLACES), :] * m
            return c

        lax.fori_loop(0, PLACES, body, 0, unroll=2)

    def load_cot():
        scale = vector(scale_ref)

        def body(q, sums):
            sums = list(sums)
            masks = [mask_at(2 * q + u) for u in range(2)]
            rows = pl.ds(pl.multiple_of(q * 2 * IMG, 2 * IMG), 2 * IMG)
            for g in range(G):
                c = [stage[g, pl.ds(2 * q + u, IMG, stride=PLACES), :] * masks[u] for u in range(2)]
                c = jnp.concatenate(c, axis=0)
                CM[rows, lanes(g)] = c.astype(bf16)
                b = (c * scale[:, lanes(g)]).astype(bf16)
                BC[rows, lanes(g)] = b
                b = b.astype(f32)
                sums[g] = sums[g] + (b[:IMG] + b[IMG:])
            return tuple(sums)

        zero = jnp.zeros((IMG, LANES), f32)
        sums = lax.fori_loop(0, PLACES // 2, body, (zero,) * G)
        for g in range(G):
            ACC[3, g] = sums[g]

    def load_taps():
        for g in range(G):
            for t in range(TAPS):
                KB[g, place(t), :] = jnp.broadcast_to(
                    taps_ref[t : t + 1, lanes(g)].astype(f32), (IMG, LANES)
                )

    def conv(src, dst, bias, flipped, post, between):
        def one(g, carry):
            for r in range(SIDE):
                acc = [None] * SIDE if bias is None else [bias[g]] * SIDE
                for rr in range(max(0, r - MARGIN), min(SIDE, r + MARGIN + 1)):
                    xs = [src[g, place(rr * SIDE + c), :] for c in range(SIDE)]
                    for dc in range(KERNEL):
                        t = (rr - r + MARGIN) * KERNEL + dc
                        k = KB[g, place(TAPS - 1 - t if flipped else t), :]
                        for c in range(SIDE):
                            cc = c + dc - MARGIN
                            if 0 <= cc < SIDE:
                                v = xs[cc] * k
                                acc[c] = v if acc[c] is None else acc[c] + v
                if post is None:
                    for c in range(SIDE):
                        dst[g, place(r * SIDE + c), :] = acc[c]
                else:
                    post(g, r, acc)
            between(g)
            return carry

        lax.fori_loop(0, G, one, 0)

    def tree(parts):
        parts = list(parts)
        while len(parts) > 1:
            parts = [
                parts[i] + parts[i + 1] if i + 1 < len(parts) else parts[i]
                for i in range(0, len(parts), 2)
            ]
        return parts[0]

    def fold(v):
        return tree(v[i : i + 8] for i in range(0, v.shape[0], 8))

    def layernorm():
        gain = vector(gain_ref)
        shift = vector(shift_ref)

        def body(q, c):
            rows = pl.ds(pl.multiple_of(q * 32, 32), 32)
            v = [XH[g, rows, :] for g in range(G)]
            mean = jnp.sum(tree(v), axis=1, keepdims=True) * (1.0 / D)
            v = [a - mean for a in v]
            total = tree([a * a for a in v])
            rstd = lax.rsqrt(jnp.sum(total, axis=1, keepdims=True) * (1.0 / D) + norm_eps)
            RSTD[rows, :] = jnp.broadcast_to(rstd, (32, LANES))
            for g in range(G):
                xh = v[g] * rstd
                XH[g, rows, :] = xh
                NM[rows, lanes(g)] = (xh * gain[:, lanes(g)] + shift[:, lanes(g)]).astype(bf16)
            return c

        lax.fori_loop(0, ROWS // 32, body, 0, unroll=5)

    def layernorm_back():
        gain = vector(gain_ref)

        def body(q, sums):
            rows = pl.ds(pl.multiple_of(q * 160, 32), 160)
            rstd = RSTD[rows, :]
            xh = [XH[g, rows, :] for g in range(G)]
            nc = [NC[g, rows, :] for g in range(G)]
            d = [nc[g] * gain[:, lanes(g)] for g in range(G)]
            m1 = jnp.sum(tree(d), axis=1, keepdims=True) * (1.0 / D)
            m2 = jnp.sum(tree([a * b for a, b in zip(d, xh)]), axis=1, keepdims=True) * (1.0 / D)
            out = []
            for g in range(G):
                dm = rstd * (d[g] - m1 - xh[g] * m2)
                NC[g, rows, :] = dm
                old = sums[g]
                out.append((old[0] + fold(nc[g] * xh[g]), old[1] + fold(nc[g]), old[2] + fold(dm)))
            return tuple(out)

        zero = jnp.zeros((8, LANES), f32)
        sums = lax.fori_loop(0, ROWS // 160, body, ((zero, zero, zero),) * G)
        for i in range(3):
            for g in range(G):
                ACC[i, g] = sums[g][i]

    def kernel_grad(between):
        def one(g, carry):
            for dr in range(KERNEL):
                acc = [[None, None] for _ in range(KERNEL)]
                for r in range(SIDE):
                    rr = r + dr - MARGIN
                    if not 0 <= rr < SIDE:
                        continue
                    ds = [NC[g, place(r * SIDE + c), :] for c in range(SIDE)]
                    xs = [X[g, place(rr * SIDE + c), :] for c in range(SIDE)]
                    for dc in range(KERNEL):
                        a = acc[dc]
                        for c in range(SIDE):
                            cc = c + dc - MARGIN
                            if 0 <= cc < SIDE:
                                v = ds[c] * xs[cc]
                                a[c % 2] = v if a[c % 2] is None else a[c % 2] + v
                for dc in range(KERNEL):
                    t = dr * KERNEL + dc
                    KG[g, t : t + 1, :] = jnp.sum(acc[dc][0] + acc[dc][1], axis=0, keepdims=True)
            between(g)
            return carry

        lax.fori_loop(0, G, one, 0)

    def hidden_block(s, j):
        if j < D // BLOCK:
            cols = slice(j * BLOCK, (j + 1) * BLOCK)
            base = j % 2 * 4
            h = dot(NM[...], WE[s, :, cols])
            stage[base] = h[:, :LANES]
            stage[base + 1] = h[:, LANES:]
            a = dot_t(BC[...], WR[s, cols, :])
            stage[base + 2] = a[:, :LANES]
            stage[base + 3] = a[:, LANES:]
        if j > 0:
            base = (j - 1) % 2 * 4
            for u in range(2):
                mine = slice((j - 1) * BLOCK + u * LANES, (j - 1) * BLOCK + (u + 1) * LANES)
                bias = EB[shard_of(s), :, mine]
                bias = jnp.concatenate([bias, bias], axis=0)
                total = None
                for i in range(ROWS // 16):
                    rows = slice(i * 16, (i + 1) * 16)
                    value, slope = gelu_both(stage[base + u, rows, :] + bias)
                    ACT[s, rows, mine] = value.astype(bf16)
                    w = (stage[base + 2 + u, rows, :] * slope).astype(bf16)
                    HC[s, rows, mine] = w
                    w = w.astype(f32)
                    w = w[:8] + w[8:]
                    total = w if total is None else total + w
                EBG[s, :, mine] = total

    def grad_block(s, m):
        for j in range(D // BLOCK):
            cols = slice(j * BLOCK, (j + 1) * BLOCK)
            if m == 0:
                GS[s, 0, cols, :] = dot_rows(ACT[s, :, cols], BC[...]).astype(bf16)
            else:
                GS[s, 1, :, cols] = dot_rows(NM[...], HC[s, :, cols]).astype(bf16)

    def back_to_normed(n):
        cols = slice(n * BLOCK, (n + 1) * BLOCK)
        total = dot_t(HC[0], WE[0, cols, :])
        for s in range(1, SLOTS):
            total = total + dot_t(HC[s], WE[s, cols, :])
        NC[2 * n] = total[:, :LANES]
        NC[2 * n + 1] = total[:, LANES:]

    def to_branch(n):
        cols = slice(n * BLOCK, (n + 1) * BLOCK)
        total = dot(ACT[0], WR[0, :, cols])
        for s in range(1, SLOTS):
            total = total + dot(ACT[s], WR[s, :, cols])
        XH[2 * n] = total[:, :LANES]
        XH[2 * n + 1] = total[:, LANES:]

    def block_output(part):
        scale = vector(scale_ref)
        shift = vector(rb_ref)

        def body(q, sums):
            sums = list(sums)
            rows = pl.ds(pl.multiple_of(q * 2 * IMG, 2 * IMG), 2 * IMG)
            masks = jnp.concatenate([mask_at(2 * q + u) for u in range(2)], axis=0)
            for g in range(G):
                branch = XH[g, rows, :] + shift[:, lanes(g)]
                v = CM[rows, lanes(g)].astype(f32) * branch
                sums[g] = sums[g] + (v[:IMG] + v[IMG:])
                value = X[g, rows, :] + masks * (scale[:, lanes(g)] * branch)
                for u in range(2):
                    stage[g, pl.ds(2 * q + u, IMG, stride=PLACES), :] = value[u * IMG : (u + 1) * IMG]
            return tuple(sums)

        zero = jnp.zeros((IMG, LANES), f32)
        n = PLACES // 4
        sums = lax.fori_loop(part * n, part * n + n, body, (zero,) * G)
        for g in range(G):
            ACC[4, g] = sums[g] if part == 0 else ACC[4, g] + sums[g]
        if part == 0:
            return

        def narrow(i, c):
            rows = pl.ds(pl.multiple_of(i * 80, 16), 80)
            for g in range(G):
                NM[rows, lanes(g)] = stage[g, rows, :].astype(bf16)
            return c

        lax.fori_loop(0, ROWS // 80, narrow, 0)

    def small_sums():
        S[...] = jnp.zeros_like(S)
        for g in range(G):
            S[:TAPS, lanes(g)] = KG[g, :TAPS, :]
            for r, i in ((ROW_BIAS, 2), (ROW_GAIN, 0), (ROW_SHIFT, 1), (ROW_REDUCE, 3), (ROW_SCALE, 4)):
                S[r : r + 1, lanes(g)] = jnp.sum(ACC[i, g], axis=0, keepdims=True)
        for s in range(SLOTS):
            r = ROW_EXPAND + shard_of(s)
            S[pl.ds(r, 1), :] = jnp.sum(EBG[s], axis=0, keepdims=True)

    def tell(name):
        kind, _, rest = name.partition(".")
        where = [int(v) for v in rest.split(".")] if rest else []
        if kind[0] == "W":
            w_step(int(kind[1]), *where)
        elif kind[0] == "G":
            g_step(int(kind[1]), *where)
        elif kind[0] == "A":
            a_step(int(kind[1]), *where)
        else:
            small_step(int(kind[1]))

    loads[0].wait()
    biases = vector(depth_bias_ref)
    for g in range(G):
        ACC[0, g] = jnp.broadcast_to(biases[:, lanes(g)], (8, LANES))

    def finish_input(g, r, acc):
        cols = pl.ds(pl.multiple_of(g * LANES, LANES), LANES)
        for c in range(0, SIDE, 2):
            p = r * SIDE + c
            cot = CM[pl.ds(p * IMG, 2 * IMG), cols].astype(f32)
            for u in range(2):
                XH[g, pl.ds(p + u, IMG, stride=PLACES), :] = (
                    acc[c + u] * mask_at(p + u) + cot[u * IMG : (u + 1) * IMG]
                )

    def out_copy(g):
        return pltpu.make_async_copy(
            XH.at[g], in_grad_hbm.at[:, pl.ds(pl.multiple_of(g * LANES, LANES), LANES)], out_sem.at[1 + g]
        )

    def over_groups(names, call):
        kind = names[0].partition(":")[0]
        after = {}
        group = 0
        for name in names:
            if name.startswith(kind + ":"):
                group = int(name.partition(":")[2])
            else:
                after.setdefault(group, []).append(name)

        def between(g):
            if kind == "convb":
                out_copy(g).start()
            for i, told in after.items():
                @pl.when(g == i)
                def _():
                    for name in told:
                        tell(name)

        call(between)

    looped = {
        "conv": lambda between: conv(X, XH, ACC.at[0], False, None, between),
        "kg": kernel_grad,
        "convb": lambda between: conv(NC, None, None, True, finish_input, between),
    }

    def start_output(part):
        block_output(part)
        if part == 1:
            pltpu.make_async_copy(NM, out_hbm, out_sem.at[0]).start()

    def pixels_in():
        spread(NM)
        load_pixels()

    def cot_in():
        loads[1].wait()
        spread(BC)
        load_cot()

    def linears_ready(s):
        if s == 0:
            loads[2].wait()
            loads[3].wait()
        else:
            for m in range(2):
                w_step(4, s, m)
            e_arrival(s).wait_recv()

    def step(name):
        kind, _, rest = name.partition(":")
        where = [int(v) for v in rest.split(":")] if rest else []
        if "." in name or kind[0] == "S":
            tell(name)
        elif kind == "h":
            if where[1] == 0:
                linears_ready(where[0])
            hidden_block(*where)
        elif kind == "gr":
            grad_block(*where)
        else:
            {
                "pix": pixels_in,
                "taps": load_taps,
                "cot": cot_in,
                "ln": layernorm,
                "lnb": layernorm_back,
                "ncot": back_to_normed,
                "branch": to_branch,
                "bout": start_output,
                "small": small_sums,
            }[kind](*where)

    at = 0
    while at < len(PLAN):
        kind = PLAN[at].partition(":")[0]
        if kind in looped:
            last = max(i for i, name in enumerate(PLAN) if name.startswith(kind + ":"))
            over_groups(PLAN[at : last + 1], looped[kind])
            at = last + 1
        else:
            step(PLAN[at])
            at += 1
    tail = [
        pltpu.make_async_copy(SALL, small_hbm, load_sem.at[2]),
    ]
    for copy in tail:
        copy.start()
    for m in range(2):
        a_step(3, m)
    for s in range(1, SLOTS):
        e_copy(s).wait_send()
    for m in range(2):
        for h in PARTS:
            own_pieces(m, h)[0].wait_send()
            in_middle(own_pieces(m, h)[1].wait_send)
            for s in range(1, SLOTS):
                in_middle(relay(s, m, h).wait_send)
                for level in (1, 2):
                    w_copy(s, m, level, h).wait_send()
            for s in PLANE:
                for level in (1, 2):
                    g_copy(s, m, level, h).wait_send()
                if s > 0:
                    z_copy(s, m, h).wait_send()
            for level in range(2):
                a_copy(m, level, h).wait_send()
        for s in range(SLOTS):
            if s > 0:
                w_copy(s, m, 3).wait_send()
            g_copy(s, m, 0).wait_send()
        p_copy(m).wait_send()
        a_copy(m, 2).wait_send()
    for j in range(1, 8):
        sr_copy(j).wait_send()
        sa_copy(j).wait_send()
    for o in range(1, n_tensor):
        sz_copy(o).wait_send()
    pltpu.make_async_copy(NM, out_hbm, out_sem.at[0]).wait()
    for g in range(G):
        out_copy(g).wait()
    for copy in tail:
        copy.wait()
    for m in range(2):
        own_half(m).wait()


def hand_over(
    out_in, grad_in, gr, ge, small,
    block_out, input_grad, kernel_grad, bias_grad, gain_grad, shift_grad,
    expand_grad, expand_bias_grad, reduce_grad, reduce_bias_grad, scale_grad,
    narrow, wide, grad_rows, out_rows, sums, taps, *rest,
):
    vectors, (there_sem, back_sem, in_sem, out_sem, small_sem) = rest[:6], rest[6:]
    D = gr.shape[0]
    third = D // 3
    half = out_in.shape[0] // 2
    halves = [
        (held.at[pl.ds(i * half, half)], src.at[pl.ds(i * half, half)], dst.at[pl.ds(i * half, half)])
        for i in range(2)
        for held, src, dst in ((grad_rows, grad_in, input_grad), (out_rows, out_in, block_out))
    ]
    there = [pltpu.make_async_copy(v[1], v[0], there_sem.at[i]) for i, v in enumerate(halves)]
    back = [pltpu.make_async_copy(v[0], v[2], back_sem.at[i]) for i, v in enumerate(halves)]
    parts = [(i, m) for i in range(3) for m in range(2)]

    def rows(i):
        return pl.ds(i * third, third)

    reads = {
        (i, m): pltpu.make_async_copy((gr, ge)[m].at[rows(i)], narrow.at[m, rows(i)], in_sem.at[m, i])
        for i, m in parts
    }
    writes = {
        (i, m): pltpu.make_async_copy(
            wide.at[m, rows(i)], (reduce_grad, expand_grad)[m].at[rows(i)], out_sem.at[m, i]
        )
        for i, m in parts
    }
    load = pltpu.make_async_copy(small, sums, small_sem.at[0])
    load.start()
    for part in parts[:2]:
        reads[part].start()
    for copy in there[:2]:
        copy.start()
    for part in parts[2:]:
        reads[part].start()
    for copy in there[2:]:
        copy.start()
    for i, m in parts:
        reads[i, m].wait()
        def widen(k, c):
            at = pl.ds(pl.multiple_of(i * third + k * 32, 32), 32)
            wide[m, at, :] = narrow[m, at, :].astype(f32)
            return c

        lax.fori_loop(0, third // 32, widen, 0)
        writes[i, m].start()
        if m == 1:
            for k in range(len(there)):
                if k * 3 // len(there) == i:
                    there[k].wait()
                    back[k].start()
    load.wait()
    taps[...] = sums[:TAPS, :]
    own = ROW_EXPAND + lax.axis_index("tensor")
    given = [pltpu.make_async_copy(taps, kernel_grad, small_sem.at[0])]
    for i, (row, ref) in enumerate((
        (ROW_BIAS, bias_grad), (ROW_GAIN, gain_grad), (ROW_SHIFT, shift_grad),
        (ROW_REDUCE, reduce_bias_grad), (ROW_SCALE, scale_grad), (own, expand_bias_grad),
    )):
        vectors[i][...] = sums[pl.ds(row, 1), :].reshape(D)
        given.append(pltpu.make_async_copy(vectors[i], ref, small_sem.at[1 + i]))
    for copy in given:
        copy.start()
    for part in parts:
        writes[part].wait()
    for copy in back + given:
        copy.wait()


def per_device(
    n_dp,
    n_tensor,
    pixels,
    crop_sides,
    out_cotangent,
    depth_kernel,
    depth_bias,
    norm_gain,
    norm_shift,
    expand_weight,
    expand_bias,
    reduce_weight,
    reduce_bias,
    layer_scale,
):
    rows, D = pixels.shape
    G = D // LANES
    img = rows // PLACES
    slots = n_tensor
    extra = max(n_dp.bit_length() - 4, 1)
    hbm = pl.BlockSpec(memory_space=pltpu.HBM)
    V = pltpu.VMEM
    DMA = pltpu.SemaphoreType.DMA
    scratch = [pltpu.SMEM((img,), jnp.int32), V((TAPS, D), bf16)] + [V((D,), bf16) for _ in range(6)] + [
        V((8, rows, LANES), f32),
        V((G, rows, LANES), f32),
        V((G, rows, LANES), f32),
        V((rows, LANES), f32),
        V((rows, D), bf16),
        V((rows, D), bf16),
        V((rows, D), bf16),
        V((G, TAPS * img, LANES), f32),
        V((slots, D, D), bf16),
        V((slots, D, D), bf16),
        V((slots, 8, D), f32),
        V((slots, rows, D), bf16),
        V((slots, rows, D), bf16),
        V((slots, 8, D), f32),
        V((G, rows, LANES), f32),
        V((G, 56, LANES), f32),
        V((5, G, 8, LANES), f32),
        V((slots, 2, D, D), bf16),
        V((slots, 2, D // 2, D), bf16),
        V((slots - 1, 2, 2, D // 8, D), bf16),
        V((slots - 1, 2, 2, D // 16, D), bf16),
        V((2, D // 2, D), bf16),
        V((slots - 2, 2, 2, D // 16, D), bf16),
        V((extra, 2, 2, D // 16 if n_dp > 8 else 16, D), bf16),
        V((2, D // 2, D), bf16),
        V((SMALL, D), f32),
        V((7, 8, D), f32),
        V((slots, 8, D), f32),
        V((extra, 8, D), f32),
        V((SMALL, D), f32),
        DMA((12,)),
        DMA((1 + G,)),
        DMA((slots, 2, 8)),
        DMA((slots, 2, 8)),
        DMA((slots,)),
        DMA((slots,)),
        DMA((slots, 2, 12)),
        DMA((slots, 2, 12)),
        DMA((extra, 2, 2)),
        DMA((extra, 2, 2)),
        DMA((4, 8)),
        DMA((4, 8)),
    ]
    block_out, input_grad, gr, ge, small = pl.pallas_call(
        functools.partial(kernel, n_dp, n_tensor),
        out_shape=[
            jax.ShapeDtypeStruct((rows, D), bf16),
            jax.ShapeDtypeStruct((rows, D), f32),
            jax.ShapeDtypeStruct((D, D), bf16),
            jax.ShapeDtypeStruct((D, D), bf16),
            jax.ShapeDtypeStruct((SMALL, D), f32),
        ],
        in_specs=[hbm] * 12,
        out_specs=[hbm] * 5,
        scratch_shapes=scratch,
        compiler_params=pltpu.CompilerParams(
            collective_id=0, has_side_effects=True, vmem_limit_bytes=63 << 20
        ),
        cost_estimate=pl.CostEstimate(
            flops=12 * rows * D * D * slots, bytes_accessed=20 * rows * D, transcendentals=0
        ),
    )(
        pixels,
        crop_sides,
        out_cotangent,
        depth_kernel,
        depth_bias,
        norm_gain,
        norm_shift,
        expand_weight,
        expand_bias,
        reduce_weight,
        reduce_bias,
        layer_scale,
    )
    vec = jax.ShapeDtypeStruct((D,), f32)
    square = jax.ShapeDtypeStruct((D, D), f32)
    return pl.pallas_call(
        hand_over,
        out_shape=[
            jax.ShapeDtypeStruct((rows, D), bf16),
            jax.ShapeDtypeStruct((rows, D), f32),
            jax.ShapeDtypeStruct((TAPS, D), f32),
            vec, vec, vec, square, vec, square, vec, vec,
        ],
        in_specs=[hbm] * 5,
        out_specs=[hbm] * 11,
        scratch_shapes=[
            V((2, D, D), bf16),
            V((2, D, D), f32),
            V((rows, D), f32),
            V((rows, D), bf16),
            V((SMALL, D), f32),
            V((TAPS, D), f32),
            *[V((D,), f32) for _ in range(6)],
            DMA((4,)),
            DMA((4,)),
            DMA((2, 3)),
            DMA((2, 3)),
            DMA((7,)),
        ],
        compiler_params=pltpu.CompilerParams(vmem_limit_bytes=60 << 20),
    )(block_out, input_grad, gr, ge, small)


def solution(mesh):
    in_specs = (
        P(("dp", "tensor"), None),
        P(("dp", "tensor")),
        P(("dp", "tensor"), None),
        P(),
        P(),
        P(),
        P(),
        P(None, "tensor"),
        P("tensor"),
        P("tensor", None),
        P(),
        P(),
    )
    out_specs = (
        P(("dp", "tensor"), None),
        P(("dp", "tensor"), None),
        P(),
        P(),
        P(),
        P(),
        P(None, "tensor"),
        P("tensor"),
        P("tensor", None),
        P(),
        P(),
    )
    return jax.shard_map(
        functools.partial(per_device, mesh.shape["dp"], mesh.shape["tensor"]),
        mesh=mesh,
        in_specs=in_specs,
        out_specs=out_specs,
        check_vma=False,
    )
```
